32 devices in a mesh: seq: 32 (over z, y, x, core), mp: 1.
Axes of the slice: x: 2, y: 2, z: 4, core: 2. Of those that a mesh axis runs over, the one named last changes fastest.
Arguments:
- state: bfloat16 [15360, 1024], P('seq'), may hold values from -60 to 60
- condition: bfloat16 [15360, 1024], P('seq'), may hold values from -6 to 6
- time_vector: bfloat16 [1024], replicated, may hold values from -4 to 4
- norm_gain: bfloat16 [1024], replicated, may hold values from 0.59765625 to 1.3984375
- w_qkv: bfloat16 [3, 1024, 1024], P(None, None, 'mp'), may hold values from -2 to 2
- w_out: bfloat16 [1024, 1024], P('mp'), may hold values from -0.75 to 0.75
- utterance_ids: int32 [15360], P('seq'), may hold values from 0 to 59, never falling along the last dimension, each value on 1 to 1024 neighbouring positions
Outputs:
- final_state: bfloat16 [15360, 1024], P('seq', 'mp')
The draws below stay inside these ranges and needn't reach their ends.
Inputs may be any that keep to these rules, and one draw needn't show every extreme that they name: `utterance_ids`: never falling along the frames; each utterance has 1 to 1024 frames and one has exactly 1024.
All inputs are finite; a program needn't handle non-finite values.
Results may differ from the reference program's by a relative error of at most 0.03.
Values may be sent and summed in bfloat16 or wider, within the bound.
No kernel may reach another device: no remote copies, remote signals or barrier semaphores. Data moves between devices by JAX's collectives and lax.ppermute only.
A program may use at most 64 MiB of HBM per device.

```python
import math
import jax
import jax.numpy as jnp
import numpy as np
from jax import lax

D = 1024
HEAD_DIM = 64
BLOCK = 24
MAX_LEN = 1024
FRAMES = 15360
UTTS = 60


def draw_state(key, part):
    key = jax.random.fold_in(key, 11)
    values = jnp.clip(jax.random.normal(key, (FRAMES, D), jnp.float32), -6.0, 6.0)
    return values.astype(jnp.bfloat16)


def draw_w_qkv(key, part):
    key = jax.random.fold_in(key, 12)
    factors = jnp.array([4.0, 1.0, 1.0], jnp.float32)[:, None, None] * D ** (-0.5)
    weights = jnp.clip(jax.random.normal(key, (3, D, D), jnp.float32), -5.0, 5.0) * factors
    return weights.astype(jnp.bfloat16)


def block_scale(key, dims, shards, low, high):
    def one(dim, blocks):
        draws = jax.random.uniform(jax.random.fold_in(jax.random.fold_in(key, 6), dim), (blocks,), jnp.float32, low / len(shards), high / len(shards))
        return jnp.repeat(jnp.exp(draws), dims[dim] // blocks).reshape((-1,) + (1,) * (len(dims) - dim - 1))

    loudness = one(*shards[0])
    for cut in shards[1:]:
        loudness = loudness * one(*cut)
    return loudness


def split_up(count, total, most, lean):
    portions = [(1 << 20) // math.isqrt(grade ** lean) + 1 for grade in range(2, count + 1)]
    rest, holding = total - most - (count - 1), [1] * (count - 1)
    while rest > 0:
        candidates = [i for i in range(count - 1) if holding[i] < most]
        pool, left = sum([portions[i] for i in candidates]), rest
        for i in candidates:
            addition = min(most - holding[i], max(1, left * portions[i] // pool), rest)
            holding[i] = holding[i] + addition
            rest = rest - addition
    return np.array([most] + holding)


def ragged_sizes(key, count, total, limit, slope):
    if count == 2:
        one = jax.random.randint(key, (), max(1, total - limit), min(limit, total - 1) + 1)
        return jnp.stack([one, total - one])
    sizes = jnp.asarray(split_up(count, total, limit, slope), jnp.int32)
    pairs = (count - 1) // 2
    giver, taker = sizes[1:1 + 2 * pairs:2], sizes[2:2 + 2 * pairs:2]
    room = jnp.minimum(giver - 1, limit - taker)
    moved = jax.random.randint(jax.random.fold_in(key, 1), (pairs,), 0, 1 << 20) % (room + 1)
    sizes = sizes.at[1:1 + 2 * pairs:2].set(giver - moved).at[2:2 + 2 * pairs:2].set(taker + moved)
    return sizes[jax.random.permutation(jax.random.fold_in(key, 2), count)]


def bell_draw(rng, dims, deviation, reach, pieces=(), kind=jnp.bfloat16):
    values = deviation * jax.random.normal(rng, dims, jnp.float32)
    if pieces:
        values = values * block_scale(rng, dims, pieces, -0.22, 0.18)
    return jnp.clip(values, -reach, reach).astype(kind)


def setup_inputs(seed: int = 0) -> dict:
    key_list = jax.random.split(jax.random.key(seed), 8)
    return {
        "state": draw_state(jax.random.fold_in(key_list[7], 71), 0),
        "condition": bell_draw(key_list[1], (FRAMES, D), 1.0, 6.0, ((0, 32),)),
        "time_vector": bell_draw(key_list[2], (D,), 1.0, 4.0),
        "norm_gain": jnp.clip(1.0 + 0.08 * jax.random.normal(key_list[3], (D,), jnp.float32), 0.59765625, 1.3984375).astype(jnp.bfloat16),
        "w_qkv": draw_w_qkv(jax.random.fold_in(key_list[7], 71), 0),
        "w_out": bell_draw(key_list[5], (D, D), (D // 16) ** -0.5, 0.75),
        "utterance_ids": jnp.searchsorted(jnp.cumsum(ragged_sizes(key_list[6], UTTS, FRAMES, MAX_LEN, 2)), jnp.arange(FRAMES), side="right").astype(jnp.int32),
    }


def attend_all(q, k, v, seg_plus):
    padded_k = jnp.pad(k, ((2 * BLOCK, BLOCK), (0, 0)))
    padded_v = jnp.pad(v, ((2 * BLOCK, BLOCK), (0, 0)))
    padded_s = jnp.pad(seg_plus, (2 * BLOCK, BLOCK))
    heads = D // HEAD_DIM

    def one_block(index):
        start = (index * BLOCK).astype(jnp.int32)
        q_rows = lax.dynamic_slice_in_dim(q, start, BLOCK, 0).reshape(BLOCK, heads, HEAD_DIM)
        k_rows = lax.dynamic_slice_in_dim(padded_k, start, 4 * BLOCK, 0).reshape(4 * BLOCK, heads, HEAD_DIM)
        v_rows = lax.dynamic_slice_in_dim(padded_v, start, 4 * BLOCK, 0).reshape(4 * BLOCK, heads, HEAD_DIM)
        q_seg = lax.dynamic_slice_in_dim(seg_plus, start, BLOCK, 0)
        k_seg = lax.dynamic_slice_in_dim(padded_s, start, 4 * BLOCK, 0)
        scores = jnp.einsum('qhe,khe->hqk', q_rows.astype(jnp.float32), k_rows.astype(jnp.float32)) * 0.125
        allowed = (q_seg[:, None] == k_seg[None, :])[None]
        scores = jnp.where(allowed, scores, -1e+30)
        top = lax.optimization_barrier(jnp.max(scores, axis=-1, keepdims=True))
        expo = jnp.exp(scores - top)
        probs = (expo / lax.optimization_barrier(jnp.sum(expo, axis=-1, keepdims=True))).astype(jnp.bfloat16)
        out = jnp.einsum('hqk,khe->qhe', probs.astype(jnp.float32), v_rows.astype(jnp.float32))
        return out.astype(jnp.bfloat16).reshape(BLOCK, D)
    blocks = lax.map(one_block, jnp.arange(FRAMES // BLOCK, dtype=jnp.int32))
    return blocks.reshape(FRAMES, D)

def reference(state, condition, time_vector, norm_gain, w_qkv, w_out, utterance_ids):
    x = state.astype(jnp.float32)
    seg_plus = utterance_ids + 1
    for step in range(2):
        t = 0.5 * step
        h = x + condition.astype(jnp.float32) + t * time_vector.astype(jnp.float32)
        scale = lax.rsqrt(lax.optimization_barrier(jnp.mean(h * h, axis=-1, keepdims=True)) + 1e-06)
        normed = (h * scale * norm_gain.astype(jnp.float32)).astype(jnp.bfloat16)
        q = jnp.dot(normed, w_qkv[0], preferred_element_type=jnp.float32).astype(jnp.bfloat16)
        k = jnp.dot(normed, w_qkv[1], preferred_element_type=jnp.float32).astype(jnp.bfloat16)
        v = jnp.dot(normed, w_qkv[2], preferred_element_type=jnp.float32).astype(jnp.bfloat16)
        attended = attend_all(q, k, v, seg_plus)
        velocity = jnp.dot(attended, w_out, preferred_element_type=jnp.float32)
        x = x + 0.5 * velocity
    return x.astype(jnp.bfloat16)
```

```python
import functools
import math

import jax
import jax.numpy as jnp
from jax import lax
from jax.experimental import pallas as pl
from jax.experimental.pallas import tpu as pltpu
from jax.sharding import PartitionSpec as P

HEAD_DIM = 64
BLOCK = 24
UNIT = 2 * BLOCK
BEHIND = 4 * BLOCK
AHEAD = 2 * BLOCK
WINDOW = 128
SPARE = WINDOW - 2 * UNIT
PAIR = 2 * HEAD_DIM
TILE = 256
F32 = jnp.float32
BF16 = jnp.bfloat16
NEG = -1e30


def shifted(shard, axis, by):
    count = lax.axis_size(axis)
    pairs = [(i, i + by) for i in range(count) if 0 <= i + by < count]
    return lax.ppermute(shard, axis, pairs)


def column_of(row):
    n = row.shape[1]
    same = lax.broadcasted_iota(jnp.int32, (n, n), 0) == lax.broadcasted_iota(jnp.int32, (n, n), 1)
    column = jnp.sum(jnp.where(same, row, 0.0), axis=1, keepdims=True)
    return jnp.broadcast_to(column, (n, 128))


def build_masks(behind_ref, ahead_ref, ids_ref, seg_ref, bias_ref):
    own = ids_ref.shape[1]
    seg_ref[0:BEHIND, :] = column_of(behind_ref[BEHIND : BEHIND + 1, 0:BEHIND].astype(F32))
    for at in range(0, own, 128):
        n = min(128, own - at)
        row = (ids_ref[:, at : at + n] + 1).astype(F32)
        seg_ref[BEHIND + at : BEHIND + at + n, :] = column_of(row)
    end = BEHIND + own
    seg_ref[end : end + AHEAD, :] = column_of(ahead_ref[AHEAD : AHEAD + 1, 0:AHEAD].astype(F32))
    end = end + AHEAD
    seg_ref[end : end + SPARE, :] = jnp.full((SPARE, 128), -1.0, F32)

    def one(unit, carry):
        start = pl.multiple_of(unit * UNIT, 16)
        window = seg_ref[pl.ds(pl.multiple_of(start - UNIT, 16), WINDOW), :]
        r = lax.broadcasted_iota(jnp.int32, (WINDOW, WINDOW), 0)
        c = lax.broadcasted_iota(jnp.int32, (WINDOW, WINDOW), 1)
        keys = jnp.sum(jnp.where(r == c, window, 0.0), axis=0, keepdims=True)
        queries = seg_ref[pl.ds(start, UNIT), :]
        row = lax.broadcasted_iota(jnp.int32, (UNIT, WINDOW), 0)
        col = lax.broadcasted_iota(jnp.int32, (UNIT, WINDOW), 1)
        first = jnp.where(row < BLOCK, 0, BLOCK)
        band = (col >= first) & (col < first + 4 * BLOCK)
        bias_ref[unit] = jnp.where(band & (queries == keys), 0.0, NEG)
        return carry

    lax.fori_loop(1, bias_ref.shape[0], one, 0)


def normalize(h_ref, normed_ref, gain, first, last):
    rows = UNIT

    def one(i, carry):
        at = pl.ds(pl.multiple_of(first + i * rows, 16), rows)
        h = h_ref[at, :]
        scale = lax.rsqrt(jnp.mean(h * h, axis=-1, keepdims=True) + 1e-06)
        normed_ref[at, :] = (h * scale * gain).astype(BF16)
        return carry

    lax.fori_loop(0, (last - first) // rows, one, 0)


def project(normed_ref, w_ref, which, first, last, outs):
    width = w_ref.shape[2]
    tile = min(TILE, width)
    for at in range(0, width, tile):
        out = jnp.dot(
            normed_ref[first:last, :], w_ref[which, :, at : at + tile], preferred_element_type=F32
        ).astype(BF16)
        if len(outs) == 1:
            outs[0][first:last, at : at + tile] = out
        else:
            lane = lax.broadcasted_iota(jnp.int32, out.shape, 1) % PAIR
            zero = jnp.zeros_like(out)
            outs[0][first:last, at : at + tile] = jnp.where(lane < HEAD_DIM, out, zero)
            outs[1][first:last, at : at + tile] = jnp.where(lane < HEAD_DIM, zero, out)


def attend(q_ref, k_refs, v_refs, att_ref, bias_ref, first, last):
    pairs = q_ref.shape[1] // PAIR
    lane = lax.broadcasted_iota(jnp.int32, (WINDOW, PAIR), 1)
    ones = [(lane < HEAD_DIM).astype(BF16), (lane >= HEAD_DIM).astype(BF16)]
    factor = HEAD_DIM**-0.5 * math.log2(math.e)

    def one(unit, carry):
        start = pl.multiple_of(unit * UNIT, 16)
        rows = pl.ds(start, UNIT)
        window = pl.ds(pl.multiple_of(start - UNIT, 16), WINDOW)
        bias = bias_ref[unit]
        bias = jnp.concatenate([bias, bias], axis=1)
        scores = []
        for p in range(pairs):
            lanes = slice(p * PAIR, (p + 1) * PAIR)
            keys = jnp.concatenate([k_refs[0][window, lanes], k_refs[1][window, lanes]], axis=0)
            scores.append(
                lax.dot_general(
                    q_ref[rows, lanes], keys, (((1,), (1,)), ((), ())), preferred_element_type=F32
                )
            )
        probs = []
        for p in range(pairs):
            s = scores[p] * factor + bias
            halves = []
            for half in (s[:, :WINDOW], s[:, WINDOW:]):
                top = jnp.max(half, axis=-1, keepdims=True)
                halves.append(jnp.exp2(half - top).astype(BF16))
            probs.append(jnp.concatenate(halves, axis=1))
        for p in range(pairs):
            lanes = slice(p * PAIR, (p + 1) * PAIR)
            values = jnp.concatenate(
                [
                    jnp.concatenate([v_refs[0][window, lanes], ones[0]], axis=1),
                    jnp.concatenate([v_refs[1][window, lanes], ones[1]], axis=1),
                ],
                axis=0,
            )
            out = jnp.dot(probs[p], values, preferred_element_type=F32)
            att_ref[rows, lanes] = (out[:, :PAIR] / out[:, PAIR:]).astype(BF16)
        return carry

    lax.fori_loop(first, last, one, 0)


def clear_spare(refs):
    for ref in refs:
        ref[ref.shape[0] - SPARE :, :] = jnp.zeros((SPARE, ref.shape[1]), ref.dtype)


def both_steps(
    state_ref, cond_ref, time_ref, gain_ref, behind_ref, ahead_ref, ids_ref, wqkv_hbm, wout_hbm,
    out_ref,
    wqkv, wout, h_ref, normed_ref, q_ref, ka_ref, kb_ref, va_ref, vb_ref, att_ref, seg_ref, bias_ref,
    sems,
):
    own = state_ref.shape[0]
    total = BEHIND + own + AHEAD
    k_refs, v_refs = (ka_ref, kb_ref), (va_ref, vb_ref)
    copies = [pltpu.make_async_copy(wqkv_hbm.at[i], wqkv.at[i], sems.at[i]) for i in (0, 1, 2)]
    copies.append(pltpu.make_async_copy(wout_hbm, wout, sems.at[3]))
    for which in (1, 2, 0, 3):
        copies[which].start()
    gain = gain_ref[...].astype(F32)
    half_time = 0.5 * time_ref[...].astype(F32)

    h_ref[0:BEHIND, :] = behind_ref[0:BEHIND, :].astype(F32)
    h_ref[BEHIND : BEHIND + own, :] = state_ref[...].astype(F32) + cond_ref[...].astype(F32)
    h_ref[BEHIND + own : total, :] = ahead_ref[0:AHEAD, :].astype(F32)
    build_masks(behind_ref, ahead_ref, ids_ref, seg_ref, bias_ref)
    clear_spare(k_refs + v_refs)

    normalize(h_ref, normed_ref, gain, 0, total)
    copies[1].wait()
    project(normed_ref, wqkv, 1, 0, total, k_refs)
    copies[2].wait()
    project(normed_ref, wqkv, 2, 0, total, v_refs)
    copies[0].wait()
    project(normed_ref, wqkv, 0, UNIT, total, [q_ref])
    attend(q_ref, k_refs, v_refs, att_ref, bias_ref, 1, total // UNIT)
    copies[3].wait()
    depth = wout.shape[1]
    for at in range(0, depth, TILE):
        cols = slice(at, at + TILE)
        moved = jnp.dot(att_ref[UNIT:total, :], wout[:, cols], preferred_element_type=F32)
        h_ref[UNIT:total, cols] = h_ref[UNIT:total, cols] + 0.5 * moved + half_time[:, cols]

    normalize(h_ref, normed_ref, gain, UNIT, total)
    project(normed_ref, wqkv, 1, UNIT, total, k_refs)
    project(normed_ref, wqkv, 2, UNIT, total, v_refs)
    project(normed_ref, wqkv, 0, BEHIND, BEHIND + own, [q_ref])
    attend(q_ref, k_refs, v_refs, att_ref, bias_ref, BEHIND // UNIT, (BEHIND + own) // UNIT)
    for at in range(0, depth, TILE):
        cols = slice(at, at + TILE)
        moved = jnp.dot(att_ref[BEHIND : BEHIND + own, :], wout[:, cols], preferred_element_type=F32)
        x = h_ref[BEHIND : BEHIND + own, cols] - cond_ref[:, cols].astype(F32) - half_time[:, cols]
        out_ref[:, cols] = (x + 0.5 * moved).astype(BF16)


def one_step(
    final, h_ref, gain_ref, behind_ref, ahead_ref, ids_ref, wqkv, wout,
    out_ref,
    normed_ref, q_ref, ka_ref, kb_ref, va_ref, vb_ref, att_ref, seg_ref, bias_ref,
):
    own = ids_ref.shape[1]
    total = BEHIND + own + AHEAD
    k_refs, v_refs = (ka_ref, kb_ref), (va_ref, vb_ref)
    kv_first = UNIT if final else 0
    first, last = (BEHIND, BEHIND + own) if final else (UNIT, total)
    build_masks(behind_ref, ahead_ref, ids_ref, seg_ref, bias_ref)
    clear_spare(k_refs + v_refs)
    normalize(h_ref, normed_ref, gain_ref[...].astype(F32), kv_first, total)
    project(normed_ref, wqkv, 1, kv_first, total, k_refs)
    project(normed_ref, wqkv, 2, kv_first, total, v_refs)
    project(normed_ref, wqkv, 0, first, last, [q_ref])
    attend(q_ref, k_refs, v_refs, att_ref, bias_ref, first // UNIT, last // UNIT)
    for at in range(0, wout.shape[1], TILE):
        cols = slice(at, at + TILE)
        out_ref[:, cols] = jnp.dot(
            att_ref[first:last, :], wout[:, cols], preferred_element_type=F32
        ).astype(BF16)


def work_shapes(own, depth, width):
    total = BEHIND + own + AHEAD
    return (
        [pltpu.VMEM((total, depth), BF16), pltpu.VMEM((total, width), BF16)]
        + [pltpu.VMEM((total + SPARE, width), BF16)] * 4
        + [
            pltpu.VMEM((total, width), BF16),
            pltpu.VMEM((total + SPARE, 128), F32),
            pltpu.VMEM((total // UNIT, UNIT, WINDOW), F32),
        ]
    )


def shards(state, condition, time_vector, norm_gain, w_qkv, w_out, utterance_ids):
    own, depth = state.shape
    width = w_qkv.shape[2]
    total = BEHIND + own + AHEAD
    parts = lax.axis_size("mp")
    gain = norm_gain.reshape(1, depth)
    ids = utterance_ids.reshape(1, own)

    def edge(rows, by):
        hidden = state[rows].astype(F32) + condition[rows].astype(F32)
        numbers = (utterance_ids[rows] + 1).astype(BF16)[None, :]
        numbers = jnp.pad(numbers, ((0, 15), (0, depth - numbers.shape[1])))
        return shifted(jnp.concatenate([hidden.astype(BF16), numbers], axis=0), "seq", by)

    behind = edge(slice(own - BEHIND, own), 1)
    ahead = edge(slice(0, AHEAD), -1)
    vmem = pl.BlockSpec(memory_space=pltpu.VMEM)
    if parts == 1:
        hbm = pl.BlockSpec(memory_space=pl.ANY)
        return pl.pallas_call(
            both_steps,
            out_shape=jax.ShapeDtypeStruct((own, depth), BF16),
            in_specs=[vmem] * 7 + [hbm] * 2,
            out_specs=vmem,
            scratch_shapes=[
                pltpu.VMEM(w_qkv.shape, BF16),
                pltpu.VMEM(w_out.shape, BF16),
                pltpu.VMEM((total, depth), F32),
            ]
            + work_shapes(own, depth, width)
            + [pltpu.SemaphoreType.DMA((4,))],
            compiler_params=pltpu.CompilerParams(vmem_limit_bytes=40 * 2**20),
        )(state, condition, time_vector.reshape(1, depth), gain, behind, ahead, ids, w_qkv, w_out)

    def terms(h, final):
        rows = own if final else total - UNIT
        mine = pl.pallas_call(
            functools.partial(one_step, final),
            out_shape=jax.ShapeDtypeStruct((rows, depth), BF16),
            in_specs=[vmem] * 7,
            out_specs=vmem,
            scratch_shapes=work_shapes(own, depth, width),
            compiler_params=pltpu.CompilerParams(vmem_limit_bytes=40 * 2**20),
        )(h, gain, behind, ahead, ids, w_qkv, w_out)
        return lax.psum(mine, "mp").astype(F32)

    start = state.astype(F32)
    h = jnp.concatenate(
        [behind[:BEHIND].astype(F32), start + condition.astype(F32), ahead[:AHEAD].astype(F32)]
    )
    velocity = terms(h, False)
    later = jnp.pad(velocity, ((UNIT, 0), (0, 0))) * 0.5 + 0.5 * time_vector.astype(F32)
    x = start + 0.5 * velocity[UNIT : UNIT + own] + 0.5 * terms(h + later, True)
    share = depth // parts
    mine = lax.dynamic_slice_in_dim(x, lax.axis_index("mp") * share, share, 1)
    return mine.astype(BF16)


def solution(mesh):
    in_specs = (
        P("seq", None),
        P("seq", None),
        P(),
        P(),
        P(None, None, "mp"),
        P("mp", None),
        P("seq"),
    )
    out_specs = P("seq", "mp")
    return jax.shard_map(shards, mesh=mesh, in_specs=in_specs, out_specs=out_specs, check_vma=False)
```

```python
import functools
import math

import jax
import jax.numpy as jnp
from jax import lax
from jax.experimental import pallas as pl
from jax.experimental.pallas import tpu as pltpu
from jax.sharding import PartitionSpec as P

HEAD_DIM = 64
BLOCK = 24
UNIT = 2 * BLOCK
BEHIND = 4 * BLOCK
AHEAD = 2 * BLOCK
WINDOW = 128
SPARE = WINDOW - 2 * UNIT
EDGE = UNIT + WINDOW
PAIR = 2 * HEAD_DIM
PAYLOAD = BEHIND + 16
TILE = 256
LIMIT = 44
F32 = jnp.float32
BF16 = jnp.bfloat16
NEG = -1e30


def column_of(row):
    n = row.shape[1]
    same = lax.broadcasted_iota(jnp.int32, (n, n), 0) == lax.broadcasted_iota(jnp.int32, (n, n), 1)
    column = jnp.sum(jnp.where(same, row, 0.0), axis=1, keepdims=True)
    return jnp.broadcast_to(column, (n, 128))


def own_segments(ids_ref, seg_ref):
    own = ids_ref.shape[1]
    for at in range(0, own, 128):
        n = min(128, own - at)
        row = (ids_ref[:, at : at + n] + 1).astype(F32)
        seg_ref[BEHIND + at : BEHIND + at + n, :] = column_of(row)


def edge_segments(behind_ref, ahead_ref, seg_ref):
    end = seg_ref.shape[0] - SPARE
    seg_ref[0:BEHIND, :] = column_of(behind_ref[BEHIND : BEHIND + 1, 0:BEHIND].astype(F32))
    seg_ref[end - AHEAD : end, :] = column_of(ahead_ref[BEHIND : BEHIND + 1, 0:AHEAD].astype(F32))
    seg_ref[end : end + SPARE, :] = jnp.full((SPARE, 128), -1.0, F32)


def build_mask(unit, seg_ref, bias_ref):
    start = unit * UNIT
    if not isinstance(unit, int):
        start = pl.multiple_of(start, 16)
    window = seg_ref[pl.ds(start - UNIT, WINDOW), :]
    r = lax.broadcasted_iota(jnp.int32, (WINDOW, WINDOW), 0)
    c = lax.broadcasted_iota(jnp.int32, (WINDOW, WINDOW), 1)
    keys = jnp.sum(jnp.where(r == c, window, 0.0), axis=0, keepdims=True)
    queries = seg_ref[pl.ds(start, UNIT), :]
    row = lax.broadcasted_iota(jnp.int32, (UNIT, WINDOW), 0)
    col = lax.broadcasted_iota(jnp.int32, (UNIT, WINDOW), 1)
    first = jnp.where(row < BLOCK, 0, BLOCK)
    band = (col >= first) & (col < first + 4 * BLOCK)
    bias_ref[unit] = jnp.where(band & (queries == keys), 0.0, NEG)


def build_masks(units, seg_ref, bias_ref):
    def one(unit, carry):
        build_mask(unit, seg_ref, bias_ref)
        return carry

    lax.fori_loop(units[0], units[1], one, 0)


def normalize(h_ref, normed_ref, gain, first, last):
    def one(i, carry):
        at = pl.ds(pl.multiple_of(first + i * UNIT, 16), UNIT)
        h = h_ref[at, :]
        scale = lax.rsqrt(jnp.mean(h * h, axis=-1, keepdims=True) + 1e-06)
        normed_ref[at, :] = (h * scale * gain).astype(BF16)
        return carry

    lax.fori_loop(0, (last - first) // UNIT, one, 0)


def project(normed_ref, w_ref, which, first, last, outs, places):
    width = w_ref.shape[2]
    tile = min(TILE, width)
    for at in range(0, width, tile):
        cols = slice(at, at + tile)
        out = jnp.dot(
            normed_ref[first:last, :], w_ref[which, :, cols], preferred_element_type=F32
        ).astype(BF16)
        if len(outs) == 1:
            parts = [out]
        else:
            lane = lax.broadcasted_iota(jnp.int32, out.shape, 1) % PAIR
            zero = jnp.zeros_like(out)
            parts = [jnp.where(lane < HEAD_DIM, out, zero), jnp.where(lane < HEAD_DIM, zero, out)]
        for ref, part in zip(outs, parts):
            done = 0
            for rows, place in places:
                ref[place : place + rows, cols] = part[done : done + rows]
                done += rows


def attend(count, place, q_ref, k_refs, v_refs, att_ref, bias_ref):
    pairs = q_ref.shape[1] // PAIR
    lane = lax.broadcasted_iota(jnp.int32, (WINDOW, PAIR), 1)
    ones = [(lane < HEAD_DIM).astype(BF16), (lane >= HEAD_DIM).astype(BF16)]
    factor = HEAD_DIM**-0.5 * math.log2(math.e)

    def one(i, carry):
        unit, *starts = place(i)
        starts = [pl.multiple_of(start, 16) for start in starts]
        rows, out_rows = pl.ds(starts[0], UNIT), pl.ds(starts[2], UNIT)
        window = pl.ds(starts[1], WINDOW)
        bias = bias_ref[unit]
        bias = jnp.concatenate([bias, bias], axis=1)
        scores = []
        for p in range(pairs):
            lanes = slice(p * PAIR, (p + 1) * PAIR)
            keys = jnp.concatenate([k_refs[0][window, lanes], k_refs[1][window, lanes]], axis=0)
            scores.append(
                lax.dot_general(
                    q_ref[rows, lanes], keys, (((1,), (1,)), ((), ())), preferred_element_type=F32
                )
            )
        probs = []
        for p in range(pairs):
            s = scores[p] * factor + bias
            halves = []
            for half in (s[:, :WINDOW], s[:, WINDOW:]):
                top = jnp.max(half, axis=-1, keepdims=True)
                halves.append(jnp.exp2(half - top).astype(BF16))
            probs.append(jnp.concatenate(halves, axis=1))
        for p in range(pairs):
            lanes = slice(p * PAIR, (p + 1) * PAIR)
            values = jnp.concatenate(
                [
                    jnp.concatenate([v_refs[0][window, lanes], ones[0]], axis=1),
                    jnp.concatenate([v_refs[1][window, lanes], ones[1]], axis=1),
                ],
                axis=0,
            )
            out = jnp.dot(probs[p], values, preferred_element_type=F32)
            att_ref[out_rows, lanes] = (out[:, :PAIR] / out[:, PAIR:]).astype(BF16)
        return carry

    lax.fori_loop(0, count, one, 0)


def in_line(first):
    return lambda i: (first + i, (first + i) * UNIT, (first + i - 1) * UNIT, (first + i) * UNIT)


def edge_kernel(state_last, cond_last, state_first, cond_first, ids_ref, low_ref, high_ref):
    me, count = lax.axis_index("seq"), lax.axis_size("seq")
    own = ids_ref.shape[1]
    even = lax.rem(me, 2) == 0

    def fill(to_next, to_previous):
        for ref, state, cond, rows, numbers, live in (
            (to_next, state_last, cond_last, BEHIND, ids_ref[:, own - BEHIND :], me < count - 1),
            (to_previous, state_first, cond_first, AHEAD, ids_ref[:, :BEHIND], me > 0),
        ):
            ref[0:rows, :] = (state[...].astype(F32) + cond[...].astype(F32)).astype(BF16)
            if rows < BEHIND:
                ref[rows:BEHIND, :] = jnp.zeros((BEHIND - rows, ref.shape[1]), BF16)
            row = jnp.where(live, numbers + 1, 0).astype(F32)
            row = jnp.concatenate([row, jnp.zeros((1, ref.shape[1] - BEHIND), F32)], axis=1)
            ref[BEHIND:, :] = jnp.broadcast_to(row, (PAYLOAD - BEHIND, ref.shape[1])).astype(BF16)

    @pl.when(even)
    def _():
        fill(low_ref, high_ref)

    @pl.when(jnp.logical_not(even))
    def _():
        fill(high_ref, low_ref)


def own_kernel(
    state_hbm, cond_hbm, gain_ref, wqkv_hbm,
    q_ref, ka_ref, kb_ref, va_ref, vb_ref,
    wqkv, state_ref, cond_ref, normed_ref, sems,
):
    own = state_ref.shape[0]
    copies = [
        pltpu.make_async_copy(state_hbm, state_ref, sems.at[0]),
        pltpu.make_async_copy(cond_hbm, cond_ref, sems.at[1]),
        pltpu.make_async_copy(wqkv_hbm.at[1], wqkv.at[1], sems.at[2]),
        pltpu.make_async_copy(wqkv_hbm.at[2], wqkv.at[2], sems.at[3]),
        pltpu.make_async_copy(wqkv_hbm.at[0], wqkv.at[0], sems.at[4]),
    ]
    for copy in copies:
        copy.start()
    gain = gain_ref[...].astype(F32)
    copies[0].wait()
    copies[1].wait()

    def one(i, carry):
        at = pl.ds(pl.multiple_of(i * UNIT, 16), UNIT)
        h = state_ref[at, :].astype(F32) + cond_ref[at, :].astype(F32)
        scale = lax.rsqrt(jnp.mean(h * h, axis=-1, keepdims=True) + 1e-06)
        normed_ref[at, :] = (h * scale * gain).astype(BF16)
        return carry

    lax.fori_loop(0, own // UNIT, one, 0)
    for which, copy, outs in (
        (1, copies[2], [ka_ref, kb_ref]),
        (2, copies[3], [va_ref, vb_ref]),
        (0, copies[4], [q_ref]),
    ):
        copy.wait()
        project(normed_ref, wqkv, which, 0, own, outs, [(own, 0)])


def rest_kernel(
    low_hbm, high_hbm, state_hbm, cond_hbm, wqkv_hbm, wout_hbm, time_ref, gain_ref, ids_ref,
    q_own, ka_own, kb_own, va_own, vb_own,
    out_ref,
    wqkv, wout, state_ref, cond_ref, behind_ref, ahead_ref, halo_ref, h_ref, normed_ref, att_ref,
    q_edge, ka_edge, kb_edge, va_edge, vb_edge, q_ref, ka_ref, kb_ref, va_ref, vb_ref,
    seg_ref, bias_ref, sems,
):
    own = state_ref.shape[0]
    units = own // UNIT
    total = BEHIND + own + AHEAD
    end = BEHIND + own
    even = lax.rem(lax.axis_index("seq"), 2) == 0

    def fetch(before, after):
        one = pltpu.make_async_copy(before.at[pl.ds(0, PAYLOAD)], behind_ref, sems.at[0])
        two = pltpu.make_async_copy(after.at[pl.ds(PAYLOAD, PAYLOAD)], ahead_ref, sems.at[1])
        return one, two

    @pl.when(even)
    def _():
        for copy in fetch(high_hbm, low_hbm):
            copy.start()

    @pl.when(jnp.logical_not(even))
    def _():
        for copy in fetch(low_hbm, high_hbm):
            copy.start()

    others = [
        pltpu.make_async_copy(wqkv_hbm.at[1], wqkv.at[1], sems.at[2]),
        pltpu.make_async_copy(wqkv_hbm.at[2], wqkv.at[2], sems.at[3]),
        pltpu.make_async_copy(wqkv_hbm.at[0], wqkv.at[0], sems.at[4]),
        pltpu.make_async_copy(wout_hbm, wout, sems.at[5]),
        pltpu.make_async_copy(state_hbm, state_ref, sems.at[6]),
        pltpu.make_async_copy(cond_hbm, cond_ref, sems.at[7]),
    ]
    for copy in others:
        copy.start()
    gain = gain_ref[...].astype(F32)
    half_time = 0.5 * time_ref[...].astype(F32)

    own_segments(ids_ref, seg_ref)
    build_masks((3, units + 1), seg_ref, bias_ref)
    attend(
        units - 2,
        lambda i: (i + 3, (i + 1) * UNIT, i * UNIT, (i + 3) * UNIT),
        q_own, (ka_own, kb_own), (va_own, vb_own), att_ref, bias_ref,
    )

    for copy in fetch(low_hbm, high_hbm):
        copy.wait()
    edge_segments(behind_ref, ahead_ref, seg_ref)
    for unit in (1, 2, units + 1, units + 2):
        build_mask(unit, seg_ref, bias_ref)
    for ref, rows, place in ((behind_ref, BEHIND, 0), (ahead_ref, AHEAD, BEHIND)):
        h = ref[0:rows, :].astype(F32)
        scale = lax.rsqrt(jnp.mean(h * h, axis=-1, keepdims=True) + 1e-06)
        halo_ref[place : place + rows, :] = (h * scale * gain).astype(BF16)
    for ref, whole in ((ka_edge, ka_own), (kb_edge, kb_own), (va_edge, va_own), (vb_edge, vb_own)):
        ref[BEHIND:EDGE, :] = whole[0 : EDGE - BEHIND, :]
        ref[EDGE : EDGE + BEHIND, :] = whole[own - BEHIND : own, :]
        ref[2 * EDGE - SPARE :, :] = jnp.zeros((SPARE, ref.shape[1]), BF16)
    q_edge[UNIT : 2 * UNIT, :] = q_own[0:UNIT, :]
    q_edge[2 * UNIT : 3 * UNIT, :] = q_own[own - UNIT : own, :]
    for copy in others:
        copy.wait()
    both = [(BEHIND, 0), (AHEAD, EDGE + BEHIND)]
    project(halo_ref, wqkv, 1, 0, BEHIND + AHEAD, (ka_edge, kb_edge), both)
    project(halo_ref, wqkv, 2, 0, BEHIND + AHEAD, (va_edge, vb_edge), both)
    project(halo_ref, wqkv, 0, UNIT, BEHIND + AHEAD, [q_edge], [(UNIT, 0), (UNIT, 3 * UNIT)])

    def edge_unit(i):
        side = i // 2
        unit = i + 1 + side * (units - 2)
        return unit, i * UNIT, side * EDGE + (i - 2 * side) * UNIT, unit * UNIT

    attend(4, edge_unit, q_edge, (ka_edge, kb_edge), (va_edge, vb_edge), att_ref, bias_ref)

    depth = wout.shape[1]
    for at in range(0, depth, TILE):
        cols = slice(at, at + TILE)
        moved = 0.5 * jnp.dot(att_ref[UNIT:total, :], wout[:, cols], preferred_element_type=F32)
        moved = moved + half_time[:, cols]
        h_ref[UNIT:BEHIND, cols] = behind_ref[UNIT:BEHIND, cols].astype(F32) + moved[:UNIT]
        h_ref[BEHIND:end, cols] = (
            state_ref[:, cols].astype(F32) + cond_ref[:, cols].astype(F32)
        ) + moved[UNIT : UNIT + own]
        h_ref[end:total, cols] = ahead_ref[0:AHEAD, cols].astype(F32) + moved[UNIT + own :]

    normalize(h_ref, normed_ref, gain, UNIT, total)
    k_refs, v_refs = (ka_ref, kb_ref), (va_ref, vb_ref)
    project(normed_ref, wqkv, 1, UNIT, total, k_refs, [(total - UNIT, UNIT)])
    project(normed_ref, wqkv, 2, UNIT, total, v_refs, [(total - UNIT, UNIT)])
    project(normed_ref, wqkv, 0, BEHIND, end, [q_ref], [(own, BEHIND)])
    attend(units, in_line(2), q_ref, k_refs, v_refs, att_ref, bias_ref)
    for at in range(0, depth, TILE):
        cols = slice(at, at + TILE)
        moved = jnp.dot(att_ref[BEHIND:end, :], wout[:, cols], preferred_element_type=F32)
        x = h_ref[BEHIND:end, cols] - cond_ref[:, cols].astype(F32) - half_time[:, cols]
        out_ref[:, cols] = (x + 0.5 * moved).astype(BF16)


def clear_spare(refs):
    for ref in refs:
        ref[ref.shape[0] - SPARE :, :] = jnp.zeros((SPARE, ref.shape[1]), ref.dtype)


def one_step(
    final, h_ref, gain_ref, behind_ref, ahead_ref, ids_ref, wqkv, wout,
    out_ref,
    normed_ref, q_ref, ka_ref, kb_ref, va_ref, vb_ref, att_ref, seg_ref, bias_ref,
):
    own = ids_ref.shape[1]
    total = BEHIND + own + AHEAD
    k_refs, v_refs = (ka_ref, kb_ref), (va_ref, vb_ref)
    kv_first = UNIT if final else 0
    first, last = (BEHIND, BEHIND + own) if final else (UNIT, total)
    own_segments(ids_ref, seg_ref)
    edge_segments(behind_ref, ahead_ref, seg_ref)
    build_masks((1, total // UNIT), seg_ref, bias_ref)
    clear_spare(k_refs + v_refs)
    normalize(h_ref, normed_ref, gain_ref[...].astype(F32), kv_first, total)
    project(normed_ref, wqkv, 1, kv_first, total, k_refs, [(total - kv_first, kv_first)])
    project(normed_ref, wqkv, 2, kv_first, total, v_refs, [(total - kv_first, kv_first)])
    project(normed_ref, wqkv, 0, first, last, [q_ref], [(last - first, first)])
    attend((last - first) // UNIT, in_line(first // UNIT), q_ref, k_refs, v_refs, att_ref, bias_ref)
    for at in range(0, wout.shape[1], TILE):
        cols = slice(at, at + TILE)
        out_ref[:, cols] = jnp.dot(
            att_ref[first:last, :], wout[:, cols], preferred_element_type=F32
        ).astype(BF16)


def shards(state, condition, time_vector, norm_gain, w_qkv, w_out, utterance_ids):
    own, depth = state.shape
    width = w_qkv.shape[2]
    total = BEHIND + own + AHEAD
    parts = lax.axis_size("mp")
    count = lax.axis_size("seq")
    gain = norm_gain.reshape(1, depth)
    time = time_vector.reshape(1, depth)
    ids = utterance_ids.reshape(1, own)
    vmem = pl.BlockSpec(memory_space=pltpu.VMEM)
    hbm = pl.BlockSpec(memory_space=pltpu.HBM)

    def limit(mib):
        return pltpu.CompilerParams(vmem_limit_bytes=mib * 2**20)

    def like(*shapes):
        return [jax.ShapeDtypeStruct(shape, dtype) for shape, dtype in shapes]

    last = pl.BlockSpec((BEHIND, depth), lambda i: (own // BEHIND - 1, 0))
    first = pl.BlockSpec((AHEAD, depth), lambda i: (0, 0))
    whole = pl.BlockSpec((PAYLOAD, depth), lambda i: (0, 0))
    low, high = pl.pallas_call(
        edge_kernel,
        grid=(1,),
        out_shape=like(*[((PAYLOAD, depth), BF16)] * 2),
        in_specs=[last, last, first, first, pl.BlockSpec((1, own), lambda i: (0, 0))],
        out_specs=[whole, whole],
        compiler_params=limit(63),
    )(state, condition, state, condition, ids)
    pairs = [[i, i + 1] for i in range(0, count, 2)]
    low = lax.all_gather(low, "seq", axis_index_groups=pairs, tiled=True)
    pairs = [[i + 1, (i + 2) % count] for i in range(0, count, 2)]
    high = lax.all_gather(high, "seq", axis_index_groups=pairs, tiled=True)

    masks = [((total + SPARE, 128), F32), ((total // UNIT, UNIT, WINDOW), F32)]
    qkv = [((total, width), BF16)] + [((total + SPARE, width), BF16)] * 4
    if parts == 1:
        projected = [((own, width), BF16)] * 5
        mine = pl.pallas_call(
            own_kernel,
            out_shape=like(*projected),
            in_specs=[hbm, hbm, vmem, hbm],
            out_specs=[vmem] * 5,
            scratch_shapes=[pltpu.VMEM(w_qkv.shape, BF16)]
            + [pltpu.VMEM((own, depth), BF16)] * 3
            + [pltpu.SemaphoreType.DMA((5,))],
            compiler_params=limit(LIMIT),
        )(state, condition, gain, w_qkv)
        work = [
            (w_qkv.shape, BF16),
            (w_out.shape, BF16),
            (state.shape, BF16),
            (state.shape, BF16),
            ((PAYLOAD, depth), BF16),
            ((PAYLOAD, depth), BF16),
            ((BEHIND + AHEAD, depth), BF16),
            ((total, depth), F32),
            ((total, depth), BF16),
            ((total, width), BF16),
            ((4 * UNIT, width), BF16),
            *[((2 * EDGE, width), BF16)] * 4,
            *[((total, width), BF16)] * 5,
            *masks,
        ]
        return pl.pallas_call(
            rest_kernel,
            out_shape=jax.ShapeDtypeStruct((own, depth), BF16),
            in_specs=[hbm] * 6 + [vmem] * 8,
            out_specs=vmem,
            scratch_shapes=[pltpu.VMEM(*one) for one in work] + [pltpu.SemaphoreType.DMA((8,))],
            compiler_params=limit(LIMIT),
        )(low, high, state, condition, w_qkv, w_out, time, gain, ids, *mine)

    even = lax.axis_index("seq") % 2 == 0
    behind = jnp.where(even, high[:PAYLOAD], low[:PAYLOAD])
    ahead = jnp.where(even, low[PAYLOAD:], high[PAYLOAD:])

    def terms(h, final):
        rows = own if final else total - UNIT
        work = [((total, depth), BF16)] + qkv + [((total, width), BF16)] + masks
        mine = pl.pallas_call(
            functools.partial(one_step, final),
            out_shape=jax.ShapeDtypeStruct((rows, depth), BF16),
            in_specs=[vmem] * 7,
            out_specs=vmem,
            scratch_shapes=[pltpu.VMEM(*one) for one in work],
            compiler_params=limit(LIMIT),
        )(h, gain, behind, ahead, ids, w_qkv, w_out)
        return lax.psum(mine, "mp").astype(F32)

    start = state.astype(F32)
    h = jnp.concatenate(
        [behind[:BEHIND].astype(F32), start + condition.astype(F32), ahead[:AHEAD].astype(F32)]
    )
    velocity = terms(h, False)
    later = jnp.pad(velocity, ((UNIT, 0), (0, 0))) * 0.5 + 0.5 * time_vector.astype(F32)
    x = start + 0.5 * velocity[UNIT : UNIT + own] + 0.5 * terms(h + later, True)
    share = depth // parts
    mine = lax.dynamic_slice_in_dim(x, lax.axis_index("mp") * share, share, 1)
    return mine.astype(BF16)


def solution(mesh):
    in_specs = (
        P("seq", None),
        P("seq", None),
        P(),
        P(),
        P(None, None, "mp"),
        P("mp", None),
        P("seq"),
    )
    out_specs = P("seq", "mp")
    return jax.shard_map(shards, mesh=mesh, in_specs=in_specs, out_specs=out_specs, check_vma=False)
```

```python
import functools
import math

import jax
import jax.numpy as jnp
from jax import lax
from jax.experimental import pallas as pl
from jax.experimental.pallas import tpu as pltpu
from jax.sharding import PartitionSpec as P

HEAD_DIM = 64
BLOCK = 24
UNIT = 2 * BLOCK
BEHIND = 4 * BLOCK
AHEAD = 2 * BLOCK
WINDOW = 128
SPARE = WINDOW - 2 * UNIT
PAIR = 2 * HEAD_DIM
PAYLOAD = BEHIND + 16
TILE = 256
LIMIT = 53
EDGE_LIMIT = 56
F32 = jnp.float32
BF16 = jnp.bfloat16
NEG = -1e30


def column_of(row):
    n = row.shape[1]
    same = lax.broadcasted_iota(jnp.int32, (n, n), 0) == lax.broadcasted_iota(jnp.int32, (n, n), 1)
    column = jnp.sum(jnp.where(same, row, 0.0), axis=1, keepdims=True)
    return jnp.broadcast_to(column, (n, 128))


def own_segments(ids_ref, seg_ref):
    own = ids_ref.shape[1]
    for at in range(0, own, 128):
        n = min(128, own - at)
        row = (ids_ref[:, at : at + n] + 1).astype(F32)
        seg_ref[BEHIND + at : BEHIND + at + n, :] = column_of(row)


def edge_segments(behind_ref, ahead_ref, seg_ref):
    end = seg_ref.shape[0] - SPARE
    seg_ref[0:BEHIND, :] = column_of(behind_ref[BEHIND : BEHIND + 1, 0:BEHIND].astype(F32))
    seg_ref[end - AHEAD : end, :] = column_of(ahead_ref[BEHIND : BEHIND + 1, 0:AHEAD].astype(F32))
    seg_ref[end : end + SPARE, :] = jnp.full((SPARE, 128), -1.0, F32)


def build_mask(unit, seg_ref, bias_ref):
    start = unit * UNIT
    if not isinstance(unit, int):
        start = pl.multiple_of(start, 16)
    window = seg_ref[pl.ds(start - UNIT, WINDOW), :]
    r = lax.broadcasted_iota(jnp.int32, (WINDOW, WINDOW), 0)
    c = lax.broadcasted_iota(jnp.int32, (WINDOW, WINDOW), 1)
    keys = jnp.sum(jnp.where(r == c, window, 0.0), axis=0, keepdims=True)
    queries = seg_ref[pl.ds(start, UNIT), :]
    row = lax.broadcasted_iota(jnp.int32, (UNIT, WINDOW), 0)
    col = lax.broadcasted_iota(jnp.int32, (UNIT, WINDOW), 1)
    first = jnp.where(row < BLOCK, 0, BLOCK)
    band = (col >= first) & (col < first + 4 * BLOCK)
    bias_ref[unit] = jnp.where(band & (queries == keys), 0.0, NEG)


def build_masks(units, seg_ref, bias_ref):
    def one(unit, carry):
        build_mask(unit, seg_ref, bias_ref)
        return carry

    lax.fori_loop(units[0], units[1], one, 0)


def normalize(h_ref, normed_ref, gain, first, last):
    def one(i, carry):
        at = pl.ds(pl.multiple_of(first + i * UNIT, 16), UNIT)
        h = h_ref[at, :]
        scale = lax.rsqrt(jnp.mean(h * h, axis=-1, keepdims=True) + 1e-06)
        normed_ref[at, :] = (h * scale * gain).astype(BF16)
        return carry

    lax.fori_loop(0, (last - first) // UNIT, one, 0)


def project(normed_ref, w_ref, first, last, outs):
    width = w_ref.shape[1]
    tile = min(TILE, width)
    for at in range(0, width, tile):
        cols = slice(at, at + tile)
        out = jnp.dot(
            normed_ref[first:last, :], w_ref[:, cols], preferred_element_type=F32
        ).astype(BF16)
        if len(outs) == 1:
            outs[0][first:last, cols] = out
        else:
            lane = lax.broadcasted_iota(jnp.int32, out.shape, 1) % PAIR
            zero = jnp.zeros_like(out)
            outs[0][first:last, cols] = jnp.where(lane < HEAD_DIM, out, zero)
            outs[1][first:last, cols] = jnp.where(lane < HEAD_DIM, zero, out)


def attend(first, last, q_ref, k_refs, v_refs, att_ref, bias_ref, score_ref, prob_ref):
    pairs = q_ref.shape[1] // PAIR
    lane = lax.broadcasted_iota(jnp.int32, (WINDOW, PAIR), 1)
    ones = [(lane < HEAD_DIM).astype(BF16), (lane >= HEAD_DIM).astype(BF16)]
    factor = HEAD_DIM**-0.5 * math.log2(math.e)

    def at(unit):
        start = pl.multiple_of(unit * UNIT, 16)
        return pl.ds(start, UNIT), pl.ds(pl.multiple_of(start - UNIT, 16), WINDOW)

    def score(unit):
        rows, window = at(unit)
        for p in range(pairs):
            lanes = slice(p * PAIR, (p + 1) * PAIR)
            keys = jnp.concatenate([k_refs[0][window, lanes], k_refs[1][window, lanes]], axis=0)
            score_ref[:, 2 * p * WINDOW : 2 * (p + 1) * WINDOW] = lax.dot_general(
                q_ref[rows, lanes], keys, (((1,), (1,)), ((), ())), preferred_element_type=F32
            )

    def soften(unit):
        bias = bias_ref[unit]
        for head in range(2 * pairs):
            lanes = slice(head * WINDOW, (head + 1) * WINDOW)
            s = score_ref[:, lanes] * factor + bias
            prob_ref[:, lanes] = jnp.exp2(s - jnp.max(s, axis=-1, keepdims=True)).astype(BF16)

    def mix(unit):
        rows, window = at(unit)
        for p in range(pairs):
            lanes = slice(p * PAIR, (p + 1) * PAIR)
            values = jnp.concatenate(
                [
                    jnp.concatenate([v_refs[0][window, lanes], ones[0]], axis=1),
                    jnp.concatenate([v_refs[1][window, lanes], ones[1]], axis=1),
                ],
                axis=0,
            )
            out = jnp.dot(
                prob_ref[:, 2 * p * WINDOW : 2 * (p + 1) * WINDOW],
                values,
                preferred_element_type=F32,
            )
            att_ref[rows, lanes] = (out[:, :PAIR] / out[:, PAIR:]).astype(BF16)

    score(first)
    soften(first)
    score(first + 1)

    def one(unit, carry):
        mix(unit)
        soften(unit + 1)
        score(unit + 2)
        return carry

    lax.fori_loop(first, last - 2, one, 0)
    mix(last - 2)
    soften(last - 1)
    mix(last - 1)


def edge_kernel(
    state_hbm, cond_hbm, ids_ref, time_ref, gain_ref,
    cross_ref, core_ref,
    state_last, cond_last, state_first, cond_first, sems,
):
    own = state_hbm.shape[0]
    copies = [
        pltpu.make_async_copy(source.at[pl.ds(first, rows)], target, sems.at[i])
        for i, (source, first, rows, target) in enumerate(
            (
                (state_hbm, own - BEHIND, BEHIND, state_last),
                (cond_hbm, own - BEHIND, BEHIND, cond_last),
                (state_hbm, 0, AHEAD, state_first),
                (cond_hbm, 0, AHEAD, cond_first),
            )
        )
    ]
    for copy in copies:
        copy.start()
    even = lax.rem(lax.axis_index("seq"), 2) == 0
    time = time_ref[...].astype(F32).reshape(1, -1)
    gain = gain_ref[...].astype(F32).reshape(1, -1)
    for copy in copies:
        copy.wait()

    def fill(ref, state, cond, ids):
        rows = state.shape[0]
        ref[0:rows, :] = (state[...].astype(F32) + cond[...].astype(F32)).astype(BF16)
        if rows < BEHIND:
            ref[rows:BEHIND, :] = jnp.zeros((BEHIND - rows, ref.shape[1]), BF16)
        depth = ref.shape[1]
        number_row = jnp.concatenate([(ids + 1).astype(F32), jnp.zeros((1, depth - BEHIND), F32)], axis=1)
        spare = jnp.zeros((PAYLOAD - BEHIND - 3, depth), F32)
        ref[BEHIND:, :] = jnp.concatenate([number_row, time, gain, spare], axis=0).astype(BF16)

    def fill_both(to_next, to_previous):
        fill(to_next, state_last, cond_last, ids_ref[:, own - BEHIND :])
        fill(to_previous, state_first, cond_first, ids_ref[:, :BEHIND])

    @pl.when(even)
    def _():
        fill_both(core_ref, cross_ref)

    @pl.when(jnp.logical_not(even))
    def _():
        fill_both(cross_ref, core_ref)


def both_steps(
    cross_ref, core_ref, state_hbm, cond_hbm, ids_ref, wqkv_hbm, wout_hbm,
    out_ref,
    state_ref, cond_ref, wqkv, wout, behind_ref, ahead_ref, h_ref,
    normed_ref, q_ref, ka_ref, kb_ref, va_ref, vb_ref, att_ref, seg_ref, bias_ref, score_ref, prob_ref,
    sems,
):
    own = state_ref.shape[0]
    end = BEHIND + own
    total = end + AHEAD
    k_refs, v_refs = (ka_ref, kb_ref), (va_ref, vb_ref)
    copies = [
        pltpu.make_async_copy(source, target, sems.at[i])
        for i, (source, target) in enumerate(
            (
                (state_hbm, state_ref),
                (cond_hbm, cond_ref),
                (wqkv_hbm.at[1], wqkv.at[1]),
                (wqkv_hbm.at[2], wqkv.at[2]),
                (wqkv_hbm.at[0], wqkv.at[0]),
                (wout_hbm, wout),
            )
        )
    ]
    for copy in copies:
        copy.start()
    half_time = 0.5 * core_ref[BEHIND + 1 : BEHIND + 2, :].astype(F32)
    gain = core_ref[BEHIND + 2 : BEHIND + 3, :].astype(F32)
    even = lax.rem(lax.axis_index("seq"), 2) == 0

    def take(before, after):
        behind_ref[...] = before[...]
        ahead_ref[...] = after[...]

    @pl.when(even)
    def _():
        take(cross_ref, core_ref)

    @pl.when(jnp.logical_not(even))
    def _():
        take(core_ref, cross_ref)

    own_segments(ids_ref, seg_ref)
    edge_segments(behind_ref, ahead_ref, seg_ref)
    build_masks((1, total // UNIT), seg_ref, bias_ref)
    clear_spare(k_refs + v_refs)
    h_ref[0:BEHIND, :] = behind_ref[0:BEHIND, :].astype(F32)
    h_ref[end:total, :] = ahead_ref[0:AHEAD, :].astype(F32)
    copies[0].wait()
    copies[1].wait()
    h_ref[BEHIND:end, :] = state_ref[...].astype(F32) + cond_ref[...].astype(F32)
    normalize(h_ref, normed_ref, gain, 0, total)
    copies[2].wait()
    project(normed_ref, wqkv.at[1], 0, total, k_refs)
    copies[3].wait()
    project(normed_ref, wqkv.at[2], 0, total, v_refs)
    copies[4].wait()
    project(normed_ref, wqkv.at[0], UNIT, total, [q_ref])
    attend(1, total // UNIT, q_ref, k_refs, v_refs, att_ref, bias_ref, score_ref, prob_ref)
    copies[5].wait()
    depth = wout.shape[1]
    for at in range(0, depth, TILE):
        cols = slice(at, at + TILE)
        moved = jnp.dot(att_ref[UNIT:total, :], wout[:, cols], preferred_element_type=F32)
        h_ref[UNIT:total, cols] = h_ref[UNIT:total, cols] + 0.5 * moved + half_time[:, cols]

    normalize(h_ref, normed_ref, gain, UNIT, total)
    project(normed_ref, wqkv.at[1], UNIT, total, k_refs)
    project(normed_ref, wqkv.at[2], UNIT, total, v_refs)
    project(normed_ref, wqkv.at[0], BEHIND, end, [q_ref])
    attend(
        BEHIND // UNIT, end // UNIT, q_ref, k_refs, v_refs, att_ref, bias_ref, score_ref, prob_ref
    )
    for at in range(0, depth, TILE):
        cols = slice(at, at + TILE)
        moved = jnp.dot(att_ref[BEHIND:end, :], wout[:, cols], preferred_element_type=F32)
        x = h_ref[BEHIND:end, cols] - cond_ref[:, cols].astype(F32) - half_time[:, cols]
        out_ref[:, cols] = (x + 0.5 * moved).astype(BF16)


def clear_spare(refs):
    for ref in refs:
        ref[ref.shape[0] - SPARE :, :] = jnp.zeros((SPARE, ref.shape[1]), ref.dtype)


def one_step(
    final, h_ref, gain_ref, behind_ref, ahead_ref, ids_ref, wqkv, wout,
    out_ref,
    normed_ref, q_ref, ka_ref, kb_ref, va_ref, vb_ref, att_ref, seg_ref, bias_ref, score_ref, prob_ref,
):
    own = ids_ref.shape[1]
    total = BEHIND + own + AHEAD
    k_refs, v_refs = (ka_ref, kb_ref), (va_ref, vb_ref)
    kv_first = UNIT if final else 0
    first, last = (BEHIND, BEHIND + own) if final else (UNIT, total)
    own_segments(ids_ref, seg_ref)
    edge_segments(behind_ref, ahead_ref, seg_ref)
    build_masks((1, total // UNIT), seg_ref, bias_ref)
    clear_spare(k_refs + v_refs)
    normalize(h_ref, normed_ref, gain_ref[...].astype(F32), kv_first, total)
    project(normed_ref, wqkv.at[1], kv_first, total, k_refs)
    project(normed_ref, wqkv.at[2], kv_first, total, v_refs)
    project(normed_ref, wqkv.at[0], first, last, [q_ref])
    attend(
        first // UNIT, last // UNIT,
        q_ref, k_refs, v_refs, att_ref, bias_ref, score_ref, prob_ref,
    )
    for at in range(0, wout.shape[1], TILE):
        cols = slice(at, at + TILE)
        out_ref[:, cols] = jnp.dot(
            att_ref[first:last, :], wout[:, cols], preferred_element_type=F32
        ).astype(BF16)


def shards(state, condition, time_vector, norm_gain, w_qkv, w_out, utterance_ids):
    own, depth = state.shape
    width = w_qkv.shape[2]
    total = BEHIND + own + AHEAD
    parts = lax.axis_size("mp")
    count = lax.axis_size("seq")
    ids = utterance_ids.reshape(1, own)
    vmem = pl.BlockSpec(memory_space=pltpu.VMEM)
    hbm = pl.BlockSpec(memory_space=pltpu.HBM)

    def limit(mib):
        return pltpu.CompilerParams(vmem_limit_bytes=mib * 2**20)

    cross, core = pl.pallas_call(
        edge_kernel,
        out_shape=[jax.ShapeDtypeStruct((PAYLOAD, depth), BF16)] * 2,
        in_specs=[hbm, hbm, vmem, vmem, vmem],
        out_specs=[vmem, vmem],
        scratch_shapes=[pltpu.VMEM((BEHIND, depth), BF16)] * 2
        + [pltpu.VMEM((AHEAD, depth), BF16)] * 2
        + [pltpu.SemaphoreType.DMA((4,))],
        compiler_params=limit(EDGE_LIMIT),
    )(state, condition, ids, time_vector, norm_gain)
    ends = [(i, i + 1) for i in range(1, count - 1, 2)]
    cross = lax.ppermute(cross, "seq", ends + [(j, i) for i, j in ends])
    ends = [(i, i + 1) for i in range(0, count - 1, 2)]
    core = lax.ppermute(core, "seq", ends + [(j, i) for i, j in ends])

    work = [((total, depth), BF16), ((total, width), BF16)]
    work += [((total + SPARE, width), BF16)] * 4
    work += [
        ((total, width), BF16),
        ((total + SPARE, 128), F32),
        ((total // UNIT, UNIT, WINDOW), F32),
        ((UNIT, width // HEAD_DIM * WINDOW), F32),
        ((UNIT, width // HEAD_DIM * WINDOW), BF16),
    ]
    if parts == 1:
        first = [((own, depth), BF16)] * 2 + [(w_qkv.shape, BF16), (w_out.shape, BF16)]
        first += [((PAYLOAD, depth), BF16)] * 2 + [((total, depth), F32)]
        return pl.pallas_call(
            both_steps,
            out_shape=jax.ShapeDtypeStruct((own, depth), BF16),
            in_specs=[vmem, vmem, hbm, hbm, vmem, hbm, hbm],
            out_specs=vmem,
            scratch_shapes=[pltpu.VMEM(*one) for one in first + work]
            + [pltpu.SemaphoreType.DMA((6,))],
            compiler_params=limit(LIMIT),
        )(cross, core, state, condition, ids, w_qkv, w_out)

    even = lax.axis_index("seq") % 2 == 0
    behind = jnp.where(even, cross, core)
    ahead = jnp.where(even, core, cross)
    gain = norm_gain.reshape(1, depth)

    def terms(h, final):
        rows = own if final else total - UNIT
        mine = pl.pallas_call(
            functools.partial(one_step, final),
            out_shape=jax.ShapeDtypeStruct((rows, depth), BF16),
            in_specs=[vmem] * 7,
            out_specs=vmem,
            scratch_shapes=[pltpu.VMEM(*one) for one in work],
            compiler_params=limit(LIMIT),
        )(h, gain, behind, ahead, ids, w_qkv, w_out)
        return lax.psum(mine, "mp").astype(F32)

    start = state.astype(F32)
    h = jnp.concatenate(
        [behind[:BEHIND].astype(F32), start + condition.astype(F32), ahead[:AHEAD].astype(F32)]
    )
    velocity = terms(h, False)
    later = jnp.pad(velocity, ((UNIT, 0), (0, 0))) * 0.5 + 0.5 * time_vector.astype(F32)
    x = start + 0.5 * velocity[UNIT : UNIT + own] + 0.5 * terms(h + later, True)
    share = depth // parts
    mine = lax.dynamic_slice_in_dim(x, lax.axis_index("mp") * share, share, 1)
    return mine.astype(BF16)


def solution(mesh):
    in_specs = (
        P("seq", None),
        P("seq", None),
        P(),
        P(),
        P(None, None, "mp"),
        P("mp", None),
        P("seq"),
    )
    out_specs = P("seq", "mp")
    return jax.shard_map(shards, mesh=mesh, in_specs=in_specs, out_specs=out_specs, check_vma=False)
```

```python
import functools
import math

import jax
import jax.numpy as jnp
from jax import lax
from jax.experimental import pallas as pl
from jax.experimental.pallas import tpu as pltpu
from jax.sharding import PartitionSpec as P

HEAD_DIM = 64
BLOCK = 24
UNIT = 2 * BLOCK
BEHIND = 4 * BLOCK
AHEAD = 2 * BLOCK
WINDOW = 128
SPARE = WINDOW - 2 * UNIT
PAIR = 2 * HEAD_DIM
SMALL = 16
PAYLOAD = BEHIND + 16
TILE = 256
EDGE_LIMIT, OWN_LIMIT, LIMIT = 56, 49, 48
F32 = jnp.float32
BF16 = jnp.bfloat16
NEG = -1e30


def column_of(row):
    n = row.shape[1]
    same = lax.broadcasted_iota(jnp.int32, (n, n), 0) == lax.broadcasted_iota(jnp.int32, (n, n), 1)
    column = jnp.sum(jnp.where(same, row, 0.0), axis=1, keepdims=True)
    return jnp.broadcast_to(column, (n, 128))


def own_segments(small_ref, seg_ref, own):
    for at in range(0, own, 128):
        n = min(128, own - at)
        row = small_ref[0:1, at : at + n].astype(F32)
        seg_ref[BEHIND + at : BEHIND + at + n, :] = column_of(row)


def edge_segments(behind_ref, ahead_ref, seg_ref):
    end = seg_ref.shape[0] - SPARE
    seg_ref[0:BEHIND, :] = column_of(behind_ref[BEHIND : BEHIND + 1, 0:BEHIND].astype(F32))
    seg_ref[end - AHEAD : end, :] = column_of(ahead_ref[BEHIND : BEHIND + 1, 0:AHEAD].astype(F32))
    seg_ref[end : end + SPARE, :] = jnp.full((SPARE, 128), -1.0, F32)


def build_mask(unit, seg_ref, bias_ref):
    start = unit * UNIT
    if not isinstance(unit, int):
        start = pl.multiple_of(start, 16)
    window = seg_ref[pl.ds(start - UNIT, WINDOW), :]
    r = lax.broadcasted_iota(jnp.int32, (WINDOW, WINDOW), 0)
    c = lax.broadcasted_iota(jnp.int32, (WINDOW, WINDOW), 1)
    keys = jnp.sum(jnp.where(r == c, window, 0.0), axis=0, keepdims=True)
    queries = seg_ref[pl.ds(start, UNIT), :]
    row = lax.broadcasted_iota(jnp.int32, (UNIT, WINDOW), 0)
    col = lax.broadcasted_iota(jnp.int32, (UNIT, WINDOW), 1)
    first = jnp.where(row < BLOCK, 0, BLOCK)
    band = (col >= first) & (col < first + 4 * BLOCK)
    bias_ref[unit] = jnp.where(band & (queries == keys), 0.0, NEG)


def build_masks(units, seg_ref, bias_ref):
    def one(unit, carry):
        build_mask(unit, seg_ref, bias_ref)
        return carry

    lax.fori_loop(units[0], units[1], one, 0)


def normalize(h_ref, normed_ref, gain, first, last):
    def one(i, carry):
        at = pl.ds(pl.multiple_of(first + i * UNIT, 16), UNIT)
        h = h_ref[at, :]
        scale = lax.rsqrt(jnp.mean(h * h, axis=-1, keepdims=True) + 1e-06)
        normed_ref[at, :] = (h * scale * gain).astype(BF16)
        return carry

    lax.fori_loop(0, (last - first) // UNIT, one, 0)


def project(normed_ref, w_ref, first, last, out_ref, places):
    width = w_ref.shape[1]
    tile = min(TILE, width)
    for at in range(0, width, tile):
        cols = slice(at, at + tile)
        out = jnp.dot(
            normed_ref[first:last, :], w_ref[:, cols], preferred_element_type=F32
        ).astype(BF16)
        done = 0
        for rows, place in places:
            out_ref[place : place + rows, cols] = out[done : done + rows]
            done += rows


def attend(first, last, q_ref, k_ref, v_ref, att_ref, bias_ref, score_ref, prob_ref):
    pairs = q_ref.shape[1] // PAIR
    ones = jnp.ones((WINDOW, PAIR), BF16)
    factor = HEAD_DIM**-0.5 * math.log2(math.e)

    def at(unit):
        start = pl.multiple_of(unit * UNIT, 16)
        return pl.ds(start, UNIT), pl.ds(pl.multiple_of(start - UNIT, 16), WINDOW)

    def score(unit):
        rows, window = at(unit)
        one = lax.broadcasted_iota(jnp.int32, (UNIT, PAIR), 1) < HEAD_DIM
        for p in range(pairs):
            lanes = slice(p * PAIR, (p + 1) * PAIR)
            q = q_ref[rows, lanes]
            zero = jnp.zeros_like(q)
            both = jnp.concatenate([jnp.where(one, q, zero), jnp.where(one, zero, q)], axis=0)
            score_ref[2 * p * UNIT : 2 * (p + 1) * UNIT, :] = lax.dot_general(
                both, k_ref[window, lanes], (((1,), (1,)), ((), ())), preferred_element_type=F32
            )

    def soften(unit):
        bias = bias_ref[unit]
        for head in range(2 * pairs):
            rows = slice(head * UNIT, (head + 1) * UNIT)
            s = score_ref[rows, :] * factor + bias
            prob_ref[rows, :] = jnp.exp2(s - jnp.max(s, axis=-1, keepdims=True)).astype(BF16)

    def mix(unit):
        rows, window = at(unit)
        one = lax.broadcasted_iota(jnp.int32, (UNIT, PAIR), 1) < HEAD_DIM
        for p in range(pairs):
            lanes = slice(p * PAIR, (p + 1) * PAIR)
            values = jnp.concatenate([v_ref[window, lanes], ones], axis=1)
            out = jnp.dot(
                prob_ref[2 * p * UNIT : 2 * (p + 1) * UNIT, :], values, preferred_element_type=F32
            )
            mixed = jnp.where(one, out[:UNIT, :PAIR], out[UNIT:, :PAIR])
            sums = jnp.where(one, out[:UNIT, PAIR:], out[UNIT:, PAIR:])
            att_ref[rows, lanes] = (mixed / sums).astype(BF16)

    score(first)
    soften(first)
    score(first + 1)

    def one(unit, carry):
        mix(unit)
        soften(unit + 1)
        score(unit + 2)
        return carry

    lax.fori_loop(first, last - 2, one, 0)
    mix(last - 2)
    soften(last - 1)
    mix(last - 1)


def edge_kernel(
    state_hbm, cond_hbm, ids_hbm, time_hbm, gain_hbm,
    cross_ref, core_ref, small_ref,
    state_last, cond_last, state_first, cond_first, ids_ref, time_ref, gain_ref, sems,
):
    own = state_hbm.shape[0]
    copies = [
        pltpu.make_async_copy(source, target, sems.at[i])
        for i, (source, target) in enumerate(
            (
                (state_hbm.at[pl.ds(own - BEHIND, BEHIND)], state_last),
                (cond_hbm.at[pl.ds(own - BEHIND, BEHIND)], cond_last),
                (state_hbm.at[pl.ds(0, AHEAD)], state_first),
                (cond_hbm.at[pl.ds(0, AHEAD)], cond_first),
                (ids_hbm, ids_ref),
                (time_hbm, time_ref),
                (gain_hbm, gain_ref),
            )
        )
    ]
    for copy in copies:
        copy.start()
    even = lax.rem(lax.axis_index("seq"), 2) == 0
    for copy in copies:
        copy.wait()

    depth = core_ref.shape[1]

    def number_row(ids):
        blank = jnp.zeros((1, depth - ids.shape[1]), F32)
        return jnp.concatenate([(ids + 1).astype(F32), blank], axis=1)

    vectors = [ref[...].astype(F32).reshape(1, -1) for ref in (time_ref, gain_ref)]
    blank = jnp.zeros((SMALL - 3, depth), F32)
    small_ref[...] = jnp.concatenate([number_row(ids_ref[...]), *vectors, blank], axis=0).astype(BF16)

    def fill(ref, state, cond, ids):
        rows = state.shape[0]
        ref[0:rows, :] = (state[...].astype(F32) + cond[...].astype(F32)).astype(BF16)
        if rows < BEHIND:
            ref[rows:BEHIND, :] = jnp.zeros((BEHIND - rows, depth), BF16)
        ref[BEHIND:, :] = jnp.broadcast_to(number_row(ids), (PAYLOAD - BEHIND, depth)).astype(BF16)

    def fill_both(to_next, to_previous):
        fill(to_next, state_last, cond_last, ids_ref[:, own - BEHIND :])
        fill(to_previous, state_first, cond_first, ids_ref[:, :BEHIND])

    @pl.when(even)
    def _():
        fill_both(core_ref, cross_ref)

    @pl.when(jnp.logical_not(even))
    def _():
        fill_both(cross_ref, core_ref)


def own_kernel(
    small_ref, state_hbm, cond_hbm, wqkv_hbm,
    state_ref, cond_ref, q_ref, k_ref, v_ref,
    wqkv, normed_ref, sems,
):
    own = state_ref.shape[0]
    copies = [
        pltpu.make_async_copy(source, target, sems.at[i])
        for i, (source, target) in enumerate(
            (
                (state_hbm, state_ref),
                (cond_hbm, cond_ref),
                (wqkv_hbm.at[1], wqkv.at[1]),
                (wqkv_hbm.at[2], wqkv.at[2]),
                (wqkv_hbm.at[0], wqkv.at[0]),
            )
        )
    ]
    for copy in copies:
        copy.start()
    gain = small_ref[2:3, :].astype(F32)
    copies[0].wait()
    copies[1].wait()

    def one(i, carry):
        at = pl.ds(pl.multiple_of(i * UNIT, 16), UNIT)
        h = state_ref[at, :].astype(F32) + cond_ref[at, :].astype(F32)
        scale = lax.rsqrt(jnp.mean(h * h, axis=-1, keepdims=True) + 1e-06)
        normed_ref[at, :] = (h * scale * gain).astype(BF16)
        return carry

    lax.fori_loop(0, own // UNIT, one, 0)
    for which, copy, out_ref in ((1, copies[2], k_ref), (2, copies[3], v_ref), (0, copies[4], q_ref)):
        copy.wait()
        project(normed_ref, wqkv.at[which], 0, own, out_ref, [(own, 0)])


def rest_kernel(
    cross_ref, core_ref, small_ref, state_ref, cond_ref, q_own, k_own, v_own,
    wqkv_hbm, wout_hbm,
    out_ref,
    wqkv, wout, behind_ref, ahead_ref, halo_ref, h_ref,
    normed_ref, q_ref, k_ref, v_ref, att_ref, seg_ref, bias_ref, score_ref, prob_ref,
    sems,
):
    own = state_ref.shape[0]
    end = BEHIND + own
    total = end + AHEAD
    copies = [
        pltpu.make_async_copy(source, target, sems.at[i])
        for i, (source, target) in enumerate(
            (
                (wqkv_hbm.at[1], wqkv.at[1]),
                (wqkv_hbm.at[2], wqkv.at[2]),
                (wqkv_hbm.at[0], wqkv.at[0]),
                (wout_hbm, wout),
            )
        )
    ]
    for copy in copies:
        copy.start()
    half_time = 0.5 * small_ref[1:2, :].astype(F32)
    gain = small_ref[2:3, :].astype(F32)
    even = lax.rem(lax.axis_index("seq"), 2) == 0

    def take(before, after):
        behind_ref[...] = before[...]
        ahead_ref[...] = after[...]

    @pl.when(even)
    def _():
        take(cross_ref, core_ref)

    @pl.when(jnp.logical_not(even))
    def _():
        take(core_ref, cross_ref)

    own_segments(small_ref, seg_ref, own)
    edge_segments(behind_ref, ahead_ref, seg_ref)
    build_masks((1, total // UNIT), seg_ref, bias_ref)
    for ref, rows, place in ((behind_ref, BEHIND, 0), (ahead_ref, AHEAD, BEHIND)):
        h = ref[0:rows, :].astype(F32)
        scale = lax.rsqrt(jnp.mean(h * h, axis=-1, keepdims=True) + 1e-06)
        halo_ref[place : place + rows, :] = (h * scale * gain).astype(BF16)
    for ref, whole in ((q_ref, q_own), (k_ref, k_own), (v_ref, v_own)):
        ref[BEHIND:end, :] = whole[...]
    clear_spare((k_ref, v_ref))
    both = [(BEHIND, 0), (AHEAD, end)]
    copies[0].wait()
    project(halo_ref, wqkv.at[1], 0, BEHIND + AHEAD, k_ref, both)
    copies[1].wait()
    project(halo_ref, wqkv.at[2], 0, BEHIND + AHEAD, v_ref, both)
    copies[2].wait()
    project(halo_ref, wqkv.at[0], UNIT, BEHIND + AHEAD, q_ref, [(UNIT, UNIT), (AHEAD, end)])
    attend(1, total // UNIT, q_ref, k_ref, v_ref, att_ref, bias_ref, score_ref, prob_ref)
    copies[3].wait()
    depth = wout.shape[1]
    for at in range(0, depth, TILE):
        cols = slice(at, at + TILE)
        moved = 0.5 * jnp.dot(att_ref[UNIT:total, :], wout[:, cols], preferred_element_type=F32)
        moved = moved + half_time[:, cols]
        h_ref[UNIT:BEHIND, cols] = behind_ref[UNIT:BEHIND, cols].astype(F32) + moved[:UNIT]
        h_ref[BEHIND:end, cols] = (
            state_ref[:, cols].astype(F32) + cond_ref[:, cols].astype(F32)
        ) + moved[UNIT : UNIT + own]
        h_ref[end:total, cols] = ahead_ref[0:AHEAD, cols].astype(F32) + moved[UNIT + own :]

    normalize(h_ref, normed_ref, gain, UNIT, total)
    project(normed_ref, wqkv.at[1], UNIT, total, k_ref, [(total - UNIT, UNIT)])
    project(normed_ref, wqkv.at[2], UNIT, total, v_ref, [(total - UNIT, UNIT)])
    project(normed_ref, wqkv.at[0], BEHIND, end, q_ref, [(own, BEHIND)])
    attend(
        BEHIND // UNIT, end // UNIT, q_ref, k_ref, v_ref, att_ref, bias_ref, score_ref, prob_ref
    )
    for at in range(0, depth, TILE):
        cols = slice(at, at + TILE)
        moved = jnp.dot(att_ref[BEHIND:end, :], wout[:, cols], preferred_element_type=F32)
        x = h_ref[BEHIND:end, cols] - cond_ref[:, cols].astype(F32) - half_time[:, cols]
        out_ref[:, cols] = (x + 0.5 * moved).astype(BF16)


def clear_spare(refs):
    for ref in refs:
        ref[ref.shape[0] - SPARE :, :] = jnp.zeros((SPARE, ref.shape[1]), ref.dtype)


def one_step(
    final, h_ref, small_ref, behind_ref, ahead_ref, wqkv, wout,
    out_ref,
    normed_ref, q_ref, k_ref, v_ref, att_ref, seg_ref, bias_ref, score_ref, prob_ref,
):
    total = h_ref.shape[0]
    own = total - BEHIND - AHEAD
    kv_first = UNIT if final else 0
    first, last = (BEHIND, BEHIND + own) if final else (UNIT, total)
    own_segments(small_ref, seg_ref, own)
    edge_segments(behind_ref, ahead_ref, seg_ref)
    build_masks((1, total // UNIT), seg_ref, bias_ref)
    clear_spare((k_ref, v_ref))
    normalize(h_ref, normed_ref, small_ref[2:3, :].astype(F32), kv_first, total)
    project(normed_ref, wqkv.at[1], kv_first, total, k_ref, [(total - kv_first, kv_first)])
    project(normed_ref, wqkv.at[2], kv_first, total, v_ref, [(total - kv_first, kv_first)])
    project(normed_ref, wqkv.at[0], first, last, q_ref, [(last - first, first)])
    attend(
        first // UNIT, last // UNIT,
        q_ref, k_ref, v_ref, att_ref, bias_ref, score_ref, prob_ref,
    )
    for at in range(0, wout.shape[1], TILE):
        cols = slice(at, at + TILE)
        out_ref[:, cols] = jnp.dot(
            att_ref[first:last, :], wout[:, cols], preferred_element_type=F32
        ).astype(BF16)


def shards(state, condition, time_vector, norm_gain, w_qkv, w_out, utterance_ids):
    own, depth = state.shape
    width = w_qkv.shape[2]
    total = BEHIND + own + AHEAD
    parts = lax.axis_size("mp")
    count = lax.axis_size("seq")
    ids = utterance_ids.reshape(1, own)
    vmem = pl.BlockSpec(memory_space=pltpu.VMEM)
    hbm = pl.BlockSpec(memory_space=pltpu.HBM)

    def limit(mib):
        return pltpu.CompilerParams(vmem_limit_bytes=mib * 2**20)

    cross, core, small = pl.pallas_call(
        edge_kernel,
        out_shape=[jax.ShapeDtypeStruct((rows, depth), BF16) for rows in (PAYLOAD, PAYLOAD, SMALL)],
        in_specs=[hbm] * 5,
        out_specs=[vmem] * 3,
        scratch_shapes=[pltpu.VMEM((BEHIND, depth), BF16)] * 2
        + [pltpu.VMEM((AHEAD, depth), BF16)] * 2
        + [pltpu.VMEM((1, own), jnp.int32)]
        + [pltpu.VMEM((depth,), BF16)] * 2
        + [pltpu.SemaphoreType.DMA((7,))],
        compiler_params=limit(EDGE_LIMIT),
    )(state, condition, ids, time_vector, norm_gain)
    ends = [(i, i + 1) for i in range(1, count - 1, 2)]
    cross = lax.ppermute(cross, "seq", ends + [(j, i) for i, j in ends])
    ends = [(i, i + 1) for i in range(0, count - 1, 2)]
    core = lax.ppermute(core, "seq", ends + [(j, i) for i, j in ends])

    work = [((total, depth), BF16), ((total, width), BF16)]
    work += [((total + SPARE, width), BF16)] * 2
    work += [
        ((total, width), BF16),
        ((total + SPARE, 128), F32),
        ((total // UNIT, UNIT, WINDOW), F32),
        ((width // HEAD_DIM * UNIT, WINDOW), F32),
        ((width // HEAD_DIM * UNIT, WINDOW), BF16),
    ]
    if parts == 1:
        kept = [jax.ShapeDtypeStruct((own, depth), BF16)] * 2
        kept = pl.pallas_call(
            own_kernel,
            out_shape=kept + [jax.ShapeDtypeStruct((own, width), BF16)] * 3,
            in_specs=[vmem] + [hbm] * 3,
            out_specs=[vmem] * 5,
            scratch_shapes=[pltpu.VMEM(w_qkv.shape, BF16), pltpu.VMEM((own, depth), BF16)]
            + [pltpu.SemaphoreType.DMA((5,))],
            compiler_params=limit(OWN_LIMIT),
            cost_estimate=pl.CostEstimate(
                flops=6 * own * depth * width, bytes_accessed=2 * 4 * depth * width, transcendentals=0
            ),
        )(small, state, condition, w_qkv)
        first = [(w_qkv.shape, BF16), (w_out.shape, BF16)] + [((PAYLOAD, depth), BF16)] * 2
        first += [((BEHIND + AHEAD, depth), BF16), ((total, depth), F32)]
        return pl.pallas_call(
            rest_kernel,
            out_shape=jax.ShapeDtypeStruct((own, depth), BF16),
            in_specs=[vmem] * 8 + [hbm] * 2,
            out_specs=vmem,
            scratch_shapes=[pltpu.VMEM(*one) for one in first + work]
            + [pltpu.SemaphoreType.DMA((4,))],
            compiler_params=limit(LIMIT),
        )(cross, core, small, *kept, w_qkv, w_out)

    even = lax.axis_index("seq") % 2 == 0
    behind = jnp.where(even, cross, core)
    ahead = jnp.where(even, core, cross)

    def terms(h, final):
        rows = own if final else total - UNIT
        mine = pl.pallas_call(
            functools.partial(one_step, final),
            out_shape=jax.ShapeDtypeStruct((rows, depth), BF16),
            in_specs=[vmem] * 6,
            out_specs=vmem,
            scratch_shapes=[pltpu.VMEM(*one) for one in work],
            compiler_params=limit(LIMIT),
        )(h, small, behind, ahead, w_qkv, w_out)
        return lax.psum(mine, "mp").astype(F32)

    start = state.astype(F32)
    h = jnp.concatenate(
        [behind[:BEHIND].astype(F32), start + condition.astype(F32), ahead[:AHEAD].astype(F32)]
    )
    velocity = terms(h, False)
    later = jnp.pad(velocity, ((UNIT, 0), (0, 0))) * 0.5 + 0.5 * time_vector.astype(F32)
    x = start + 0.5 * velocity[UNIT : UNIT + own] + 0.5 * terms(h + later, True)
    share = depth // parts
    mine = lax.dynamic_slice_in_dim(x, lax.axis_index("mp") * share, share, 1)
    return mine.astype(BF16)


def solution(mesh):
    in_specs = (
        P("seq", None),
        P("seq", None),
        P(),
        P(),
        P(None, None, "mp"),
        P("mp", None),
        P("seq"),
    )
    out_specs = P("seq", "mp")
    return jax.shard_map(shards, mesh=mesh, in_specs=in_specs, out_specs=out_specs, check_vma=False)
```

```python
import functools
import math

import jax
import jax.numpy as jnp
from jax import lax
from jax.experimental import pallas as pl
from jax.experimental.pallas import tpu as pltpu
from jax.sharding import PartitionSpec as P

HEAD_DIM = 64
BLOCK = 24
UNIT = 2 * BLOCK
BEHIND = 4 * BLOCK
AHEAD = 2 * BLOCK
WINDOW = 128
SPARE = WINDOW - 2 * UNIT
PAIR = 2 * HEAD_DIM
SMALL = 16
PAYLOAD = BEHIND + 16
TILE = 256
EDGE_LIMIT, OWN_LIMIT, LIMIT = 56, 48, 48
F32 = jnp.float32
BF16 = jnp.bfloat16
NEG = -1e30


def column_of(row):
    n = row.shape[1]
    same = lax.broadcasted_iota(jnp.int32, (n, n), 0) == lax.broadcasted_iota(jnp.int32, (n, n), 1)
    column = jnp.sum(jnp.where(same, row, 0.0), axis=1, keepdims=True)
    return jnp.broadcast_to(column, (n, 128))


def own_segments(small_ref, seg_ref, own):
    for at in range(0, own, 128):
        n = min(128, own - at)
        row = small_ref[0:1, at : at + n].astype(F32)
        seg_ref[BEHIND + at : BEHIND + at + n, :] = column_of(row)


def edge_segments(behind_ref, ahead_ref, seg_ref):
    end = seg_ref.shape[0] - SPARE
    seg_ref[0:BEHIND, :] = column_of(behind_ref[BEHIND : BEHIND + 1, 0:BEHIND].astype(F32))
    seg_ref[end - AHEAD : end, :] = column_of(ahead_ref[BEHIND : BEHIND + 1, 0:AHEAD].astype(F32))
    seg_ref[end : end + SPARE, :] = jnp.full((SPARE, 128), -1.0, F32)


def build_mask(unit, seg_ref, bias_ref):
    start = unit * UNIT
    if not isinstance(unit, int):
        start = pl.multiple_of(start, 16)
    window = seg_ref[pl.ds(start - UNIT, WINDOW), :]
    r = lax.broadcasted_iota(jnp.int32, (WINDOW, WINDOW), 0)
    c = lax.broadcasted_iota(jnp.int32, (WINDOW, WINDOW), 1)
    keys = jnp.sum(jnp.where(r == c, window, 0.0), axis=0, keepdims=True)
    queries = seg_ref[pl.ds(start, UNIT), :]
    row = lax.broadcasted_iota(jnp.int32, (UNIT, WINDOW), 0)
    col = lax.broadcasted_iota(jnp.int32, (UNIT, WINDOW), 1)
    first = jnp.where(row < BLOCK, 0, BLOCK)
    band = (col >= first) & (col < first + 4 * BLOCK)
    bias_ref[unit] = jnp.where(band & (queries == keys), 0.0, NEG)


def build_masks(units, seg_ref, bias_ref):
    def one(unit, carry):
        build_mask(unit, seg_ref, bias_ref)
        return carry

    lax.fori_loop(units[0], units[1], one, 0)


def normalize(h_ref, normed_ref, gain, first, last):
    def one(i, carry):
        at = pl.ds(pl.multiple_of(first + i * UNIT, 16), UNIT)
        h = h_ref[at, :]
        scale = lax.rsqrt(jnp.mean(h * h, axis=-1, keepdims=True) + 1e-06)
        normed_ref[at, :] = (h * scale * gain).astype(BF16)
        return carry

    lax.fori_loop(0, (last - first) // UNIT, one, 0)


def width_tiles(w_ref):
    return w_ref.shape[1] // min(TILE, w_ref.shape[1])


def tile_copies(w_hbm, w_ref, sems, first_sem):
    tile = min(TILE, w_ref.shape[1])
    return [
        pltpu.make_async_copy(
            w_hbm.at[:, pl.ds(i * tile, tile)], w_ref.at[:, pl.ds(i * tile, tile)], sems.at[first_sem + i]
        )
        for i in range(w_ref.shape[1] // tile)
    ]


def project(normed_ref, w_ref, first, last, out_ref, places, arriving=None):
    width = w_ref.shape[1]
    tile = min(TILE, width)
    for at in range(0, width, tile):
        cols = slice(at, at + tile)
        if arriving is not None:
            arriving[at // tile].wait()
        out = jnp.dot(
            normed_ref[first:last, :], w_ref[:, cols], preferred_element_type=F32
        ).astype(BF16)
        done = 0
        for rows, place in places:
            out_ref[place : place + rows, cols] = out[done : done + rows]
            done += rows


def attend(first, last, q_ref, k_ref, v_ref, att_ref, bias_ref, score_ref, prob_ref):
    pairs = q_ref.shape[1] // PAIR
    ones = jnp.ones((WINDOW, PAIR), BF16)
    factor = HEAD_DIM**-0.5 * math.log2(math.e)

    def at(unit):
        start = pl.multiple_of(unit * UNIT, 16)
        return pl.ds(start, UNIT), pl.ds(pl.multiple_of(start - UNIT, 16), WINDOW)

    def score(unit):
        rows, window = at(unit)
        one = lax.broadcasted_iota(jnp.int32, (UNIT, PAIR), 1) < HEAD_DIM
        for p in range(pairs):
            lanes = slice(p * PAIR, (p + 1) * PAIR)
            q = q_ref[rows, lanes]
            zero = jnp.zeros_like(q)
            both = jnp.concatenate([jnp.where(one, q, zero), jnp.where(one, zero, q)], axis=0)
            score_ref[2 * p * UNIT : 2 * (p + 1) * UNIT, :] = lax.dot_general(
                both, k_ref[window, lanes], (((1,), (1,)), ((), ())), preferred_element_type=F32
            )

    def soften(unit):
        bias = bias_ref[unit]
        for head in range(2 * pairs):
            rows = slice(head * UNIT, (head + 1) * UNIT)
            s = score_ref[rows, :] * factor + bias
            prob_ref[rows, :] = jnp.exp2(s - jnp.max(s, axis=-1, keepdims=True)).astype(BF16)

    def mix(unit):
        rows, window = at(unit)
        one = lax.broadcasted_iota(jnp.int32, (UNIT, PAIR), 1) < HEAD_DIM
        for p in range(pairs):
            lanes = slice(p * PAIR, (p + 1) * PAIR)
            values = jnp.concatenate([v_ref[window, lanes], ones], axis=1)
            out = jnp.dot(
                prob_ref[2 * p * UNIT : 2 * (p + 1) * UNIT, :], values, preferred_element_type=F32
            )
            mixed = jnp.where(one, out[:UNIT, :PAIR], out[UNIT:, :PAIR])
            sums = jnp.where(one, out[:UNIT, PAIR:], out[UNIT:, PAIR:])
            att_ref[rows, lanes] = (mixed / sums).astype(BF16)

    score(first)
    soften(first)
    score(first + 1)

    def one(unit, carry):
        mix(unit)
        soften(unit + 1)
        score(unit + 2)
        return carry

    lax.fori_loop(first, last - 2, one, 0)
    mix(last - 2)
    soften(last - 1)
    mix(last - 1)


def edge_kernel(
    state_hbm, cond_hbm, ids_hbm, time_hbm, gain_hbm,
    cross_ref, core_ref, small_ref,
    state_last, cond_last, state_first, cond_first, ids_ref, time_ref, gain_ref, sems,
):
    own = state_hbm.shape[0]
    copies = [
        pltpu.make_async_copy(source, target, sems.at[i])
        for i, (source, target) in enumerate(
            (
                (state_hbm.at[pl.ds(own - BEHIND, BEHIND)], state_last),
                (cond_hbm.at[pl.ds(own - BEHIND, BEHIND)], cond_last),
                (state_hbm.at[pl.ds(0, AHEAD)], state_first),
                (cond_hbm.at[pl.ds(0, AHEAD)], cond_first),
                (ids_hbm, ids_ref),
                (time_hbm, time_ref),
                (gain_hbm, gain_ref),
            )
        )
    ]
    for copy in copies:
        copy.start()
    even = lax.rem(lax.axis_index("seq"), 2) == 0
    for copy in copies:
        copy.wait()

    depth = core_ref.shape[1]

    def number_row(ids):
        blank = jnp.zeros((1, depth - ids.shape[1]), F32)
        return jnp.concatenate([(ids + 1).astype(F32), blank], axis=1)

    vectors = [ref[...].astype(F32).reshape(1, -1) for ref in (time_ref, gain_ref)]
    blank = jnp.zeros((SMALL - 3, depth), F32)
    small_ref[...] = jnp.concatenate([number_row(ids_ref[...]), *vectors, blank], axis=0).astype(BF16)

    def fill(ref, state, cond, ids):
        rows = state.shape[0]
        ref[0:rows, :] = (state[...].astype(F32) + cond[...].astype(F32)).astype(BF16)
        if rows < BEHIND:
            ref[rows:BEHIND, :] = jnp.zeros((BEHIND - rows, depth), BF16)
        ref[BEHIND:, :] = jnp.broadcast_to(number_row(ids), (PAYLOAD - BEHIND, depth)).astype(BF16)

    def fill_both(to_next, to_previous):
        fill(to_next, state_last, cond_last, ids_ref[:, own - BEHIND :])
        fill(to_previous, state_first, cond_first, ids_ref[:, :BEHIND])

    @pl.when(even)
    def _():
        fill_both(core_ref, cross_ref)

    @pl.when(jnp.logical_not(even))
    def _():
        fill_both(cross_ref, core_ref)


def own_kernel(
    small_ref, state_hbm, cond_hbm, wqkv_hbm,
    state_ref, cond_ref, q_ref, k_ref, v_ref, seg_ref, bias_ref,
    wk_ref, wv_ref, wq_ref, normed_ref, sems,
):
    own = state_ref.shape[0]
    copies = [
        pltpu.make_async_copy(state_hbm, state_ref, sems.at[0]),
        pltpu.make_async_copy(cond_hbm, cond_ref, sems.at[1]),
    ]
    tiles = width_tiles(wk_ref)
    weights = [
        tile_copies(wqkv_hbm.at[which], w_ref, sems, 2 + i * tiles)
        for i, (which, w_ref) in enumerate(((1, wk_ref), (2, wv_ref), (0, wq_ref)))
    ]
    for copy in copies + weights[0]:
        copy.start()
    gain = small_ref[2:3, :].astype(F32)
    own_segments(small_ref, seg_ref, own)
    build_masks((3, own // UNIT + 1), seg_ref, bias_ref)
    copies[0].wait()
    copies[1].wait()
    for copy in weights[1] + weights[2]:
        copy.start()

    def one(i, carry):
        at = pl.ds(pl.multiple_of(i * UNIT, 16), UNIT)
        h = state_ref[at, :].astype(F32) + cond_ref[at, :].astype(F32)
        scale = lax.rsqrt(jnp.mean(h * h, axis=-1, keepdims=True) + 1e-06)
        normed_ref[at, :] = (h * scale * gain).astype(BF16)
        return carry

    lax.fori_loop(0, own // UNIT, one, 0)
    for w_ref, arriving, out_ref in zip((wk_ref, wv_ref, wq_ref), weights, (k_ref, v_ref, q_ref)):
        project(normed_ref, w_ref, 0, own, out_ref, [(own, 0)], arriving)


def rest_kernel(
    cross_ref, core_ref, small_ref, state_ref, cond_ref, q_own, k_own, v_own, seg_own, bias_own,
    wqkv_hbm, wout_hbm,
    out_hbm,
    wk_ref, wv_ref, wq_ref, wout, behind_ref, ahead_ref, halo_ref, h_ref, out_ref,
    normed_ref, q_ref, k_ref, v_ref, att_ref, seg_ref, bias_ref, score_ref, prob_ref,
    sems,
):
    own = state_ref.shape[0]
    units = own // UNIT
    end = BEHIND + own
    total = end + AHEAD
    tiles = width_tiles(wk_ref)
    weights = [
        tile_copies(wqkv_hbm.at[which], w_ref, sems, i * tiles)
        for i, (which, w_ref) in enumerate(((1, wk_ref), (2, wv_ref), (0, wq_ref)))
    ]
    wout_copy = pltpu.make_async_copy(wout_hbm, wout, sems.at[3 * tiles])
    for copy in weights[0]:
        copy.start()
    half_time = 0.5 * small_ref[1:2, :].astype(F32)
    gain = small_ref[2:3, :].astype(F32)
    even = lax.rem(lax.axis_index("seq"), 2) == 0

    def take(before, after):
        behind_ref[...] = before[...]
        ahead_ref[...] = after[...]

    @pl.when(even)
    def _():
        take(cross_ref, core_ref)

    @pl.when(jnp.logical_not(even))
    def _():
        take(core_ref, cross_ref)

    seg_ref[BEHIND:end, :] = seg_own[BEHIND:end, :]
    edge_segments(behind_ref, ahead_ref, seg_ref)
    bias_ref[3 : units + 1] = bias_own[3 : units + 1]
    for unit in (1, 2, units + 1, units + 2):
        build_mask(unit, seg_ref, bias_ref)
    for ref, rows, place in ((behind_ref, BEHIND, 0), (ahead_ref, AHEAD, BEHIND)):
        h = ref[0:rows, :].astype(F32)
        scale = lax.rsqrt(jnp.mean(h * h, axis=-1, keepdims=True) + 1e-06)
        halo_ref[place : place + rows, :] = (h * scale * gain).astype(BF16)
    for ref, whole in ((q_ref, q_own), (k_ref, k_own), (v_ref, v_own)):
        ref[BEHIND:end, :] = whole[...]
    for copy in weights[1] + weights[2] + [wout_copy]:
        copy.start()
    clear_spare((k_ref, v_ref))
    both = [(BEHIND, 0), (AHEAD, end)]
    edges = [(UNIT, UNIT), (AHEAD, end)]
    project(halo_ref, wk_ref, 0, BEHIND + AHEAD, k_ref, both, weights[0])
    project(halo_ref, wv_ref, 0, BEHIND + AHEAD, v_ref, both, weights[1])
    project(halo_ref, wq_ref, UNIT, BEHIND + AHEAD, q_ref, edges, weights[2])
    attend(1, total // UNIT, q_ref, k_ref, v_ref, att_ref, bias_ref, score_ref, prob_ref)
    wout_copy.wait()
    depth = wout.shape[1]
    for at in range(0, depth, TILE):
        cols = slice(at, at + TILE)
        moved = 0.5 * jnp.dot(att_ref[UNIT:total, :], wout[:, cols], preferred_element_type=F32)
        moved = moved + half_time[:, cols]
        h_ref[UNIT:BEHIND, cols] = behind_ref[UNIT:BEHIND, cols].astype(F32) + moved[:UNIT]
        h_ref[BEHIND:end, cols] = (
            state_ref[:, cols].astype(F32) + cond_ref[:, cols].astype(F32)
        ) + moved[UNIT : UNIT + own]
        h_ref[end:total, cols] = ahead_ref[0:AHEAD, cols].astype(F32) + moved[UNIT + own :]

    normalize(h_ref, normed_ref, gain, UNIT, total)
    project(normed_ref, wk_ref, UNIT, total, k_ref, [(total - UNIT, UNIT)])
    project(normed_ref, wv_ref, UNIT, total, v_ref, [(total - UNIT, UNIT)])
    project(normed_ref, wq_ref, BEHIND, end, q_ref, [(own, BEHIND)])
    attend(
        BEHIND // UNIT, end // UNIT, q_ref, k_ref, v_ref, att_ref, bias_ref, score_ref, prob_ref
    )
    sent = []
    for i, at in enumerate(range(0, depth, TILE)):
        cols = slice(at, at + TILE)
        moved = jnp.dot(att_ref[BEHIND:end, :], wout[:, cols], preferred_element_type=F32)
        x = h_ref[BEHIND:end, cols] - cond_ref[:, cols].astype(F32) - half_time[:, cols]
        out_ref[:, cols] = (x + 0.5 * moved).astype(BF16)
        tile = pl.ds(at, TILE)
        sem = sems.at[3 * tiles + 1 + i]
        sent.append(pltpu.make_async_copy(out_ref.at[:, tile], out_hbm.at[:, tile], sem))
        sent[-1].start()
    for copy in sent:
        copy.wait()


def clear_spare(refs):
    for ref in refs:
        ref[ref.shape[0] - SPARE :, :] = jnp.zeros((SPARE, ref.shape[1]), ref.dtype)


def one_step(
    final, h_ref, small_ref, behind_ref, ahead_ref, wqkv, wout,
    out_ref,
    normed_ref, q_ref, k_ref, v_ref, att_ref, seg_ref, bias_ref, score_ref, prob_ref,
):
    total = h_ref.shape[0]
    own = total - BEHIND - AHEAD
    kv_first = UNIT if final else 0
    first, last = (BEHIND, BEHIND + own) if final else (UNIT, total)
    own_segments(small_ref, seg_ref, own)
    edge_segments(behind_ref, ahead_ref, seg_ref)
    build_masks((1, total // UNIT), seg_ref, bias_ref)
    clear_spare((k_ref, v_ref))
    normalize(h_ref, normed_ref, small_ref[2:3, :].astype(F32), kv_first, total)
    project(normed_ref, wqkv.at[1], kv_first, total, k_ref, [(total - kv_first, kv_first)])
    project(normed_ref, wqkv.at[2], kv_first, total, v_ref, [(total - kv_first, kv_first)])
    project(normed_ref, wqkv.at[0], first, last, q_ref, [(last - first, first)])
    attend(
        first // UNIT, last // UNIT,
        q_ref, k_ref, v_ref, att_ref, bias_ref, score_ref, prob_ref,
    )
    for at in range(0, wout.shape[1], TILE):
        cols = slice(at, at + TILE)
        out_ref[:, cols] = jnp.dot(
            att_ref[first:last, :], wout[:, cols], preferred_element_type=F32
        ).astype(BF16)


def shards(state, condition, time_vector, norm_gain, w_qkv, w_out, utterance_ids):
    own, depth = state.shape
    width = w_qkv.shape[2]
    total = BEHIND + own + AHEAD
    parts = lax.axis_size("mp")
    count = lax.axis_size("seq")
    ids = utterance_ids.reshape(1, own)
    vmem = pl.BlockSpec(memory_space=pltpu.VMEM)
    hbm = pl.BlockSpec(memory_space=pltpu.HBM)

    def limit(mib):
        return pltpu.CompilerParams(vmem_limit_bytes=int(mib * 2**20))

    cross, core, small = pl.pallas_call(
        edge_kernel,
        out_shape=[jax.ShapeDtypeStruct((rows, depth), BF16) for rows in (PAYLOAD, PAYLOAD, SMALL)],
        in_specs=[hbm] * 5,
        out_specs=[vmem] * 3,
        scratch_shapes=[pltpu.VMEM((BEHIND, depth), BF16)] * 2
        + [pltpu.VMEM((AHEAD, depth), BF16)] * 2
        + [pltpu.VMEM((1, own), jnp.int32)]
        + [pltpu.VMEM((depth,), BF16)] * 2
        + [pltpu.SemaphoreType.DMA((7,))],
        compiler_params=limit(EDGE_LIMIT),
    )(state, condition, ids, time_vector, norm_gain)
    ends = [(i, i + 1) for i in range(1, count - 1, 2)]
    cross = lax.ppermute(cross, "seq", ends + [(j, i) for i, j in ends])
    ends = [(i, i + 1) for i in range(0, count - 1, 2)]
    core = lax.ppermute(core, "seq", ends + [(j, i) for i, j in ends])

    work = [((total, depth), BF16), ((total, width), BF16)]
    work += [((total + SPARE, width), BF16)] * 2
    work += [
        ((total, width), BF16),
        ((total + SPARE, 128), F32),
        ((total // UNIT, UNIT, WINDOW), F32),
        ((width // HEAD_DIM * UNIT, WINDOW), F32),
        ((width // HEAD_DIM * UNIT, WINDOW), BF16),
    ]
    if parts == 1:
        tiles = width // min(TILE, width)
        kept = [(state.shape, BF16)] * 2 + [((own, width), BF16)] * 3
        kept += [((total + SPARE, 128), F32), ((total // UNIT, UNIT, WINDOW), F32)]
        kept = pl.pallas_call(
            own_kernel,
            out_shape=[jax.ShapeDtypeStruct(*one) for one in kept],
            in_specs=[vmem] + [hbm] * 3,
            out_specs=[vmem] * 7,
            scratch_shapes=[pltpu.VMEM((depth, width), BF16)] * 3
            + [pltpu.VMEM((own, depth), BF16), pltpu.SemaphoreType.DMA((2 + 3 * tiles,))],
            compiler_params=limit(OWN_LIMIT),
            cost_estimate=pl.CostEstimate(
                flops=6 * own * depth * width, bytes_accessed=2 * 4 * depth * width, transcendentals=0
            ),
        )(small, state, condition, w_qkv)
        first = [((depth, width), BF16)] * 3 + [(w_out.shape, BF16)] + [((PAYLOAD, depth), BF16)] * 2
        first += [((BEHIND + AHEAD, depth), BF16), ((total, depth), F32), ((own, depth), BF16)]
        return pl.pallas_call(
            rest_kernel,
            out_shape=jax.ShapeDtypeStruct((own, depth), BF16),
            in_specs=[vmem] * 10 + [hbm] * 2,
            out_specs=hbm,
            scratch_shapes=[pltpu.VMEM(*one) for one in first + work]
            + [pltpu.SemaphoreType.DMA((1 + 3 * tiles + depth // TILE,))],
            compiler_params=limit(LIMIT),
        )(cross, core, small, *kept, w_qkv, w_out)

    even = lax.axis_index("seq") % 2 == 0
    behind = jnp.where(even, cross, core)
    ahead = jnp.where(even, core, cross)

    def terms(h, final):
        rows = own if final else total - UNIT
        mine = pl.pallas_call(
            functools.partial(one_step, final),
            out_shape=jax.ShapeDtypeStruct((rows, depth), BF16),
            in_specs=[vmem] * 6,
            out_specs=vmem,
            scratch_shapes=[pltpu.VMEM(*one) for one in work],
            compiler_params=limit(LIMIT),
        )(h, small, behind, ahead, w_qkv, w_out)
        return lax.psum(mine, "mp").astype(F32)

    start = state.astype(F32)
    h = jnp.concatenate(
        [behind[:BEHIND].astype(F32), start + condition.astype(F32), ahead[:AHEAD].astype(F32)]
    )
    velocity = terms(h, False)
    later = jnp.pad(velocity, ((UNIT, 0), (0, 0))) * 0.5 + 0.5 * time_vector.astype(F32)
    x = start + 0.5 * velocity[UNIT : UNIT + own] + 0.5 * terms(h + later, True)
    share = depth // parts
    mine = lax.dynamic_slice_in_dim(x, lax.axis_index("mp") * share, share, 1)
    return mine.astype(BF16)


def solution(mesh):
    in_specs = (
        P("seq", None),
        P("seq", None),
        P(),
        P(),
        P(None, None, "mp"),
        P("mp", None),
        P("seq"),
    )
    out_specs = P("seq", "mp")
    return jax.shard_map(shards, mesh=mesh, in_specs=in_specs, out_specs=out_specs, check_vma=False)
```

```python
import functools
import math

import jax
import jax.numpy as jnp
from jax import lax
from jax.experimental import pallas as pl
from jax.experimental.pallas import tpu as pltpu
from jax.sharding import PartitionSpec as P

HEAD_DIM = 64
BLOCK = 24
UNIT = 2 * BLOCK
BEHIND = 4 * BLOCK
AHEAD = 2 * BLOCK
WINDOW = 128
SPARE = WINDOW - 2 * UNIT
PAIR = 2 * HEAD_DIM
FOUR = 4
SMALL = 16
PAYLOAD = BEHIND + 16
TILE = 256
EDGE_LIMIT, OWN_LIMIT, LIMIT = 56, 48, 48
F32 = jnp.float32
BF16 = jnp.bfloat16
NEG = -1e30


def column_of(row):
    n = row.shape[1]
    same = lax.broadcasted_iota(jnp.int32, (n, n), 0) == lax.broadcasted_iota(jnp.int32, (n, n), 1)
    column = jnp.sum(jnp.where(same, row, 0.0), axis=1, keepdims=True)
    return jnp.broadcast_to(column, (n, 128))


def own_segments(small_ref, seg_ref, own):
    for at in range(0, own, 128):
        n = min(128, own - at)
        row = small_ref[0:1, at : at + n].astype(F32)
        seg_ref[BEHIND + at : BEHIND + at + n, :] = column_of(row)


def edge_segments(behind_ref, ahead_ref, seg_ref):
    end = seg_ref.shape[0] - SPARE
    seg_ref[0:BEHIND, :] = column_of(behind_ref[BEHIND : BEHIND + 1, 0:BEHIND].astype(F32))
    seg_ref[end - AHEAD : end, :] = column_of(ahead_ref[BEHIND : BEHIND + 1, 0:AHEAD].astype(F32))
    seg_ref[end : end + SPARE, :] = jnp.full((SPARE, 128), -1.0, F32)


def build_mask(unit, seg_ref, bias_ref):
    start = unit * UNIT
    if not isinstance(unit, int):
        start = pl.multiple_of(start, 16)
    window = seg_ref[pl.ds(start - UNIT, WINDOW), :]
    r = lax.broadcasted_iota(jnp.int32, (WINDOW, WINDOW), 0)
    c = lax.broadcasted_iota(jnp.int32, (WINDOW, WINDOW), 1)
    keys = jnp.sum(jnp.where(r == c, window, 0.0), axis=0, keepdims=True)
    queries = seg_ref[pl.ds(start, UNIT), :]
    row = lax.broadcasted_iota(jnp.int32, (UNIT, WINDOW), 0)
    col = lax.broadcasted_iota(jnp.int32, (UNIT, WINDOW), 1)
    first = jnp.where(row < BLOCK, 0, BLOCK)
    band = (col >= first) & (col < first + 4 * BLOCK)
    bias_ref[unit] = jnp.where(band & (queries == keys), 0.0, NEG)


def build_masks(units, seg_ref, bias_ref):
    def one(unit, carry):
        build_mask(unit, seg_ref, bias_ref)
        return carry

    lax.fori_loop(units[0], units[1], one, 0)


def normalize(h_ref, normed_ref, gain, first, last):
    def one(i, carry):
        at = pl.ds(pl.multiple_of(first + i * UNIT, 16), UNIT)
        h = h_ref[at, :]
        scale = lax.rsqrt(jnp.mean(h * h, axis=-1, keepdims=True) + 1e-06)
        normed_ref[at, :] = (h * scale * gain).astype(BF16)
        return carry

    lax.fori_loop(0, (last - first) // UNIT, one, 0)


def project(normed_ref, w_ref, first, last, out_ref, places):
    width = w_ref.shape[1]
    tile = min(TILE, width)
    for at in range(0, width, tile):
        cols = slice(at, at + tile)
        out = jnp.dot(
            normed_ref[first:last, :], w_ref[:, cols], preferred_element_type=F32
        ).astype(BF16)
        done = 0
        for rows, place in places:
            out_ref[place : place + rows, cols] = out[done : done + rows]
            done += rows


def attend(first, last, q_ref, k_ref, v_ref, att_ref, bias_ref, score_ref, prob_ref, sum_ref):
    wide = FOUR * HEAD_DIM
    groups = q_ref.shape[1] // wide
    factor = HEAD_DIM**-0.5 * math.log2(math.e)

    def at(unit):
        start = pl.multiple_of(unit * UNIT, 16)
        return pl.ds(start, UNIT), pl.ds(pl.multiple_of(start - UNIT, 16), WINDOW)

    def score(unit):
        rows, window = at(unit)
        head = lax.broadcasted_iota(jnp.int32, (UNIT, wide), 1) // HEAD_DIM
        for g in range(groups):
            lanes = slice(g * wide, (g + 1) * wide)
            q = q_ref[rows, lanes]
            zero = jnp.zeros_like(q)
            stacked = jnp.concatenate([jnp.where(head == j, q, zero) for j in range(FOUR)], axis=0)
            score_ref[FOUR * g * UNIT : FOUR * (g + 1) * UNIT, :] = lax.dot_general(
                stacked, k_ref[window, lanes], (((1,), (1,)), ((), ())), preferred_element_type=F32
            )

    def soften(unit):
        bias = bias_ref[unit]
        for j in range(FOUR * groups):
            rows = slice(j * UNIT, (j + 1) * UNIT)
            s = score_ref[rows, :] * factor + bias
            expo = jnp.exp2(s - jnp.max(s, axis=-1, keepdims=True))
            prob_ref[rows, :] = expo.astype(BF16)
            total = jnp.sum(expo, axis=-1, keepdims=True)
            sum_ref[rows, :] = jnp.broadcast_to(total, (UNIT, PAIR))

    def mix(unit):
        rows, window = at(unit)
        one = lax.broadcasted_iota(jnp.int32, (UNIT, PAIR), 1) < HEAD_DIM
        for g in range(groups):
            lanes = slice(g * wide, (g + 1) * wide)
            top = FOUR * g * UNIT
            out = jnp.dot(
                prob_ref[top : top + FOUR * UNIT, :], v_ref[window, lanes], preferred_element_type=F32
            )
            for p in range(FOUR // 2):
                low, high = 2 * p * UNIT, (2 * p + 1) * UNIT
                cols = slice(p * PAIR, (p + 1) * PAIR)
                mixed = jnp.where(one, out[low : low + UNIT, cols], out[high : high + UNIT, cols])
                sums = jnp.where(
                    one,
                    sum_ref[top + low : top + low + UNIT, :],
                    sum_ref[top + high : top + high + UNIT, :],
                )
                mine = slice(g * wide + p * PAIR, g * wide + (p + 1) * PAIR)
                att_ref[rows, mine] = (mixed / sums).astype(BF16)

    score(first)
    soften(first)
    score(first + 1)

    def one(unit, carry):
        mix(unit)
        soften(unit + 1)
        score(unit + 2)
        return carry

    lax.fori_loop(first, last - 2, one, 0)
    mix(last - 2)
    soften(last - 1)
    mix(last - 1)


def edge_kernel(
    state_hbm, cond_hbm, ids_hbm, time_hbm, gain_hbm,
    cross_ref, core_ref, small_ref,
    state_last, cond_last, state_first, cond_first, ids_ref, time_ref, gain_ref, sems,
):
    own = state_hbm.shape[0]
    copies = [
        pltpu.make_async_copy(source, target, sems.at[i])
        for i, (source, target) in enumerate(
            (
                (state_hbm.at[pl.ds(own - BEHIND, BEHIND)], state_last),
                (cond_hbm.at[pl.ds(own - BEHIND, BEHIND)], cond_last),
                (state_hbm.at[pl.ds(0, AHEAD)], state_first),
                (cond_hbm.at[pl.ds(0, AHEAD)], cond_first),
                (ids_hbm, ids_ref),
                (time_hbm, time_ref),
                (gain_hbm, gain_ref),
            )
        )
    ]
    for copy in copies:
        copy.start()
    even = lax.rem(lax.axis_index("seq"), 2) == 0
    for copy in copies:
        copy.wait()

    depth = core_ref.shape[1]

    def number_row(ids):
        blank = jnp.zeros((1, depth - ids.shape[1]), F32)
        return jnp.concatenate([(ids + 1).astype(F32), blank], axis=1)

    vectors = [ref[...].astype(F32).reshape(1, -1) for ref in (time_ref, gain_ref)]
    blank = jnp.zeros((SMALL - 3, depth), F32)
    small_ref[...] = jnp.concatenate([number_row(ids_ref[...]), *vectors, blank], axis=0).astype(BF16)

    def fill(ref, state, cond, ids):
        rows = state.shape[0]
        ref[0:rows, :] = (state[...].astype(F32) + cond[...].astype(F32)).astype(BF16)
        if rows < BEHIND:
            ref[rows:BEHIND, :] = jnp.zeros((BEHIND - rows, depth), BF16)
        ref[BEHIND:, :] = jnp.broadcast_to(number_row(ids), (PAYLOAD - BEHIND, depth)).astype(BF16)

    def fill_both(to_next, to_previous):
        fill(to_next, state_last, cond_last, ids_ref[:, own - BEHIND :])
        fill(to_previous, state_first, cond_first, ids_ref[:, :BEHIND])

    @pl.when(even)
    def _():
        fill_both(core_ref, cross_ref)

    @pl.when(jnp.logical_not(even))
    def _():
        fill_both(cross_ref, core_ref)


def own_kernel(
    small_ref, state_hbm, cond_hbm, wqkv_hbm,
    state_ref, cond_ref, q_ref, k_ref, v_ref, seg_ref, bias_ref,
    wk_ref, wv_ref, wq_ref, normed_ref, sems,
):
    own = state_ref.shape[0]
    copies = [
        pltpu.make_async_copy(state_hbm, state_ref, sems.at[0]),
        pltpu.make_async_copy(cond_hbm, cond_ref, sems.at[1]),
    ]
    weights = [
        pltpu.make_async_copy(wqkv_hbm.at[which], w_ref, sems.at[2 + which])
        for which, w_ref in ((1, wk_ref), (2, wv_ref), (0, wq_ref))
    ]
    for copy in copies + weights[:1]:
        copy.start()
    gain = small_ref[2:3, :].astype(F32)
    own_segments(small_ref, seg_ref, own)
    build_masks((3, own // UNIT + 1), seg_ref, bias_ref)
    copies[0].wait()
    copies[1].wait()
    for copy in weights[1:]:
        copy.start()

    def one(i, carry):
        at = pl.ds(pl.multiple_of(i * UNIT, 16), UNIT)
        h = state_ref[at, :].astype(F32) + cond_ref[at, :].astype(F32)
        scale = lax.rsqrt(jnp.mean(h * h, axis=-1, keepdims=True) + 1e-06)
        normed_ref[at, :] = (h * scale * gain).astype(BF16)
        return carry

    lax.fori_loop(0, own // UNIT, one, 0)
    for w_ref, copy, out_ref in zip((wk_ref, wv_ref, wq_ref), weights, (k_ref, v_ref, q_ref)):
        copy.wait()
        project(normed_ref, w_ref, 0, own, out_ref, [(own, 0)])


def rest_kernel(
    cross_ref, core_ref, small_ref, state_ref, cond_ref, q_own, k_own, v_own, seg_own, bias_own,
    wqkv_hbm, wout_hbm,
    out_hbm,
    wk_ref, wv_ref, wq_ref, wout, behind_ref, ahead_ref, halo_ref, h_ref, out_ref,
    normed_ref, q_ref, k_ref, v_ref, att_ref, seg_ref, bias_ref, score_ref, prob_ref, sum_ref,
    sems,
):
    own = state_ref.shape[0]
    units = own // UNIT
    end = BEHIND + own
    total = end + AHEAD
    weights = [
        pltpu.make_async_copy(wqkv_hbm.at[which], w_ref, sems.at[which])
        for which, w_ref in ((1, wk_ref), (2, wv_ref), (0, wq_ref))
    ]
    wout_copy = pltpu.make_async_copy(wout_hbm, wout, sems.at[3])
    weights[0].start()
    half_time = 0.5 * small_ref[1:2, :].astype(F32)
    gain = small_ref[2:3, :].astype(F32)
    even = lax.rem(lax.axis_index("seq"), 2) == 0

    def take(before, after):
        behind_ref[...] = before[...]
        ahead_ref[...] = after[...]

    @pl.when(even)
    def _():
        take(cross_ref, core_ref)

    @pl.when(jnp.logical_not(even))
    def _():
        take(core_ref, cross_ref)

    seg_ref[BEHIND:end, :] = seg_own[BEHIND:end, :]
    edge_segments(behind_ref, ahead_ref, seg_ref)
    bias_ref[3 : units + 1] = bias_own[3 : units + 1]
    for unit in (1, 2, units + 1, units + 2):
        build_mask(unit, seg_ref, bias_ref)
    for ref, rows, place in ((behind_ref, BEHIND, 0), (ahead_ref, AHEAD, BEHIND)):
        h = ref[0:rows, :].astype(F32)
        scale = lax.rsqrt(jnp.mean(h * h, axis=-1, keepdims=True) + 1e-06)
        halo_ref[place : place + rows, :] = (h * scale * gain).astype(BF16)
    for ref, whole in ((q_ref, q_own), (k_ref, k_own), (v_ref, v_own)):
        ref[BEHIND:end, :] = whole[...]
    for copy in weights[1:] + [wout_copy]:
        copy.start()
    clear_spare((k_ref, v_ref))
    both = [(BEHIND, 0), (AHEAD, end)]
    edges = [(UNIT, UNIT), (AHEAD, end)]
    weights[0].wait()
    project(halo_ref, wk_ref, 0, BEHIND + AHEAD, k_ref, both)
    weights[1].wait()
    project(halo_ref, wv_ref, 0, BEHIND + AHEAD, v_ref, both)
    weights[2].wait()
    project(halo_ref, wq_ref, UNIT, BEHIND + AHEAD, q_ref, edges)
    attend(1, total // UNIT, q_ref, k_ref, v_ref, att_ref, bias_ref, score_ref, prob_ref, sum_ref)
    wout_copy.wait()
    depth = wout.shape[1]
    for at in range(0, depth, TILE):
        cols = slice(at, at + TILE)
        moved = 0.5 * jnp.dot(att_ref[UNIT:total, :], wout[:, cols], preferred_element_type=F32)
        moved = moved + half_time[:, cols]
        h_ref[UNIT:BEHIND, cols] = behind_ref[UNIT:BEHIND, cols].astype(F32) + moved[:UNIT]
        h_ref[BEHIND:end, cols] = (
            state_ref[:, cols].astype(F32) + cond_ref[:, cols].astype(F32)
        ) + moved[UNIT : UNIT + own]
        h_ref[end:total, cols] = ahead_ref[0:AHEAD, cols].astype(F32) + moved[UNIT + own :]

    normalize(h_ref, normed_ref, gain, UNIT, total)
    project(normed_ref, wk_ref, UNIT, total, k_ref, [(total - UNIT, UNIT)])
    project(normed_ref, wv_ref, UNIT, total, v_ref, [(total - UNIT, UNIT)])
    project(normed_ref, wq_ref, BEHIND, end, q_ref, [(own, BEHIND)])
    attend(
        BEHIND // UNIT, end // UNIT, q_ref, k_ref, v_ref, att_ref, bias_ref, score_ref, prob_ref, sum_ref
    )
    sent = []
    for half in range(2):
        mine = slice(half * own // 2, (half + 1) * own // 2)
        rows = slice(BEHIND + mine.start, BEHIND + mine.stop)
        for at in range(0, depth, TILE):
            cols = slice(at, at + TILE)
            moved = jnp.dot(att_ref[rows, :], wout[:, cols], preferred_element_type=F32)
            x = h_ref[rows, cols] - cond_ref[mine, cols].astype(F32) - half_time[:, cols]
            out_ref[mine, cols] = (x + 0.5 * moved).astype(BF16)
        part = pl.ds(mine.start, own // 2)
        sent.append(pltpu.make_async_copy(out_ref.at[part], out_hbm.at[part], sems.at[4 + half]))
        sent[-1].start()
    for copy in sent:
        copy.wait()


def clear_spare(refs):
    for ref in refs:
        ref[ref.shape[0] - SPARE :, :] = jnp.zeros((SPARE, ref.shape[1]), ref.dtype)


def one_step(
    final, h_ref, small_ref, behind_ref, ahead_ref, wqkv, wout,
    out_ref,
    normed_ref, q_ref, k_ref, v_ref, att_ref, seg_ref, bias_ref, score_ref, prob_ref, sum_ref,
):
    total = h_ref.shape[0]
    own = total - BEHIND - AHEAD
    kv_first = UNIT if final else 0
    first, last = (BEHIND, BEHIND + own) if final else (UNIT, total)
    own_segments(small_ref, seg_ref, own)
    edge_segments(behind_ref, ahead_ref, seg_ref)
    build_masks((1, total // UNIT), seg_ref, bias_ref)
    clear_spare((k_ref, v_ref))
    normalize(h_ref, normed_ref, small_ref[2:3, :].astype(F32), kv_first, total)
    project(normed_ref, wqkv.at[1], kv_first, total, k_ref, [(total - kv_first, kv_first)])
    project(normed_ref, wqkv.at[2], kv_first, total, v_ref, [(total - kv_first, kv_first)])
    project(normed_ref, wqkv.at[0], first, last, q_ref, [(last - first, first)])
    attend(
        first // UNIT, last // UNIT,
        q_ref, k_ref, v_ref, att_ref, bias_ref, score_ref, prob_ref, sum_ref,
    )
    for at in range(0, wout.shape[1], TILE):
        cols = slice(at, at + TILE)
        out_ref[:, cols] = jnp.dot(
            att_ref[first:last, :], wout[:, cols], preferred_element_type=F32
        ).astype(BF16)


def shards(state, condition, time_vector, norm_gain, w_qkv, w_out, utterance_ids):
    own, depth = state.shape
    width = w_qkv.shape[2]
    total = BEHIND + own + AHEAD
    parts = lax.axis_size("mp")
    count = lax.axis_size("seq")
    ids = utterance_ids.reshape(1, own)
    vmem = pl.BlockSpec(memory_space=pltpu.VMEM)
    hbm = pl.BlockSpec(memory_space=pltpu.HBM)

    def limit(mib):
        return pltpu.CompilerParams(vmem_limit_bytes=int(mib * 2**20))

    cross, core, small = pl.pallas_call(
        edge_kernel,
        out_shape=[jax.ShapeDtypeStruct((rows, depth), BF16) for rows in (PAYLOAD, PAYLOAD, SMALL)],
        in_specs=[hbm] * 5,
        out_specs=[vmem] * 3,
        scratch_shapes=[pltpu.VMEM((BEHIND, depth), BF16)] * 2
        + [pltpu.VMEM((AHEAD, depth), BF16)] * 2
        + [pltpu.VMEM((1, own), jnp.int32)]
        + [pltpu.VMEM((depth,), BF16)] * 2
        + [pltpu.SemaphoreType.DMA((7,))],
        compiler_params=limit(EDGE_LIMIT),
    )(state, condition, ids, time_vector, norm_gain)
    ends = [(i, i + 1) for i in range(1, count - 1, 2)]
    cross = lax.ppermute(cross, "seq", ends + [(j, i) for i, j in ends])
    ends = [(i, i + 1) for i in range(0, count - 1, 2)]
    core = lax.ppermute(core, "seq", ends + [(j, i) for i, j in ends])

    work = [((total, depth), BF16), ((total, width), BF16)]
    work += [((total + SPARE, width), BF16)] * 2
    work += [
        ((total, width), BF16),
        ((total + SPARE, 128), F32),
        ((total // UNIT, UNIT, WINDOW), F32),
        ((width // HEAD_DIM * UNIT, WINDOW), F32),
        ((width // HEAD_DIM * UNIT, WINDOW), BF16),
        ((width // HEAD_DIM * UNIT, PAIR), F32),
    ]
    if parts == 1:
        kept = [(state.shape, BF16)] * 2 + [((own, width), BF16)] * 3
        kept += [((total + SPARE, 128), F32), ((total // UNIT, UNIT, WINDOW), F32)]
        kept = pl.pallas_call(
            own_kernel,
            out_shape=[jax.ShapeDtypeStruct(*one) for one in kept],
            in_specs=[vmem] + [hbm] * 3,
            out_specs=[vmem] * 7,
            scratch_shapes=[pltpu.VMEM((depth, width), BF16)] * 3
            + [pltpu.VMEM((own, depth), BF16), pltpu.SemaphoreType.DMA((5,))],
            compiler_params=limit(OWN_LIMIT),
            cost_estimate=pl.CostEstimate(
                flops=6 * own * depth * width, bytes_accessed=2 * 4 * depth * width, transcendentals=0
            ),
        )(small, state, condition, w_qkv)
        first = [((depth, width), BF16)] * 3 + [(w_out.shape, BF16)] + [((PAYLOAD, depth), BF16)] * 2
        first += [((BEHIND + AHEAD, depth), BF16), ((total, depth), F32), ((own, depth), BF16)]
        return pl.pallas_call(
            rest_kernel,
            out_shape=jax.ShapeDtypeStruct((own, depth), BF16),
            in_specs=[vmem] * 10 + [hbm] * 2,
            out_specs=hbm,
            scratch_shapes=[pltpu.VMEM(*one) for one in first + work]
            + [pltpu.SemaphoreType.DMA((6,))],
            compiler_params=limit(LIMIT),
        )(cross, core, small, *kept, w_qkv, w_out)

    even = lax.axis_index("seq") % 2 == 0
    behind = jnp.where(even, cross, core)
    ahead = jnp.where(even, core, cross)

    def terms(h, final):
        rows = own if final else total - UNIT
        mine = pl.pallas_call(
            functools.partial(one_step, final),
            out_shape=jax.ShapeDtypeStruct((rows, depth), BF16),
            in_specs=[vmem] * 6,
            out_specs=vmem,
            scratch_shapes=[pltpu.VMEM(*one) for one in work],
            compiler_params=limit(LIMIT),
        )(h, small, behind, ahead, w_qkv, w_out)
        return lax.psum(mine, "mp").astype(F32)

    start = state.astype(F32)
    h = jnp.concatenate(
        [behind[:BEHIND].astype(F32), start + condition.astype(F32), ahead[:AHEAD].astype(F32)]
    )
    velocity = terms(h, False)
    later = jnp.pad(velocity, ((UNIT, 0), (0, 0))) * 0.5 + 0.5 * time_vector.astype(F32)
    x = start + 0.5 * velocity[UNIT : UNIT + own] + 0.5 * terms(h + later, True)
    share = depth // parts
    mine = lax.dynamic_slice_in_dim(x, lax.axis_index("mp") * share, share, 1)
    return mine.astype(BF16)


def solution(mesh):
    in_specs = (
        P("seq", None),
        P("seq", None),
        P(),
        P(),
        P(None, None, "mp"),
        P("mp", None),
        P("seq"),
    )
    out_specs = P("seq", "mp")
    return jax.shard_map(shards, mesh=mesh, in_specs=in_specs, out_specs=out_specs, check_vma=False)
```

```python
import functools
import math

import jax
import jax.numpy as jnp
from jax import lax
from jax.experimental import pallas as pl
from jax.experimental.pallas import tpu as pltpu
from jax.sharding import PartitionSpec as P

HEAD_DIM = 64
BLOCK = 24
UNIT = 2 * BLOCK
BEHIND = 4 * BLOCK
AHEAD = 2 * BLOCK
WINDOW = 128
SPARE = WINDOW - 2 * UNIT
PAIR = 2 * HEAD_DIM
SUM_LOW, SUM_HIGH = 2.0**-60, 2.0**100
SMALL = 16
PAYLOAD = BEHIND + 16
TILE = 256
EDGE_LIMIT, OWN_LIMIT, LIMIT = 56, 48, 48
F32 = jnp.float32
BF16 = jnp.bfloat16
NEG = -1e30


def column_of(row):
    n = row.shape[1]
    same = lax.broadcasted_iota(jnp.int32, (n, n), 0) == lax.broadcasted_iota(jnp.int32, (n, n), 1)
    column = jnp.sum(jnp.where(same, row, 0.0), axis=1, keepdims=True)
    return jnp.broadcast_to(column, (n, 128))


def own_segments(small_ref, seg_ref, own):
    for at in range(0, own, 128):
        n = min(128, own - at)
        row = small_ref[0:1, at : at + n].astype(F32)
        seg_ref[BEHIND + at : BEHIND + at + n, :] = column_of(row)


def edge_segments(behind_ref, ahead_ref, seg_ref):
    end = seg_ref.shape[0] - SPARE
    seg_ref[0:BEHIND, :] = column_of(behind_ref[BEHIND : BEHIND + 1, 0:BEHIND].astype(F32))
    seg_ref[end - AHEAD : end, :] = column_of(ahead_ref[BEHIND : BEHIND + 1, 0:AHEAD].astype(F32))
    seg_ref[end : end + SPARE, :] = jnp.full((SPARE, 128), -1.0, F32)


def build_mask(unit, seg_ref, bias_ref):
    start = unit * UNIT
    if not isinstance(unit, int):
        start = pl.multiple_of(start, 16)
    window = seg_ref[pl.ds(start - UNIT, WINDOW), :]
    r = lax.broadcasted_iota(jnp.int32, (WINDOW, WINDOW), 0)
    c = lax.broadcasted_iota(jnp.int32, (WINDOW, WINDOW), 1)
    keys = jnp.sum(jnp.where(r == c, window, 0.0), axis=0, keepdims=True)
    queries = seg_ref[pl.ds(start, UNIT), :]
    row = lax.broadcasted_iota(jnp.int32, (UNIT, WINDOW), 0)
    col = lax.broadcasted_iota(jnp.int32, (UNIT, WINDOW), 1)
    first = jnp.where(row < BLOCK, 0, BLOCK)
    band = (col >= first) & (col < first + 4 * BLOCK)
    bias_ref[unit] = jnp.where(band & (queries == keys), 0.0, NEG)


def build_masks(units, seg_ref, bias_ref):
    def one(unit, carry):
        build_mask(unit, seg_ref, bias_ref)
        return carry

    lax.fori_loop(units[0], units[1], one, 0)


def normalize(h_ref, normed_ref, gain, first, last):
    def one(i, carry):
        at = pl.ds(pl.multiple_of(first + i * UNIT, 16), UNIT)
        h = h_ref[at, :]
        scale = lax.rsqrt(jnp.mean(h * h, axis=-1, keepdims=True) + 1e-06)
        normed_ref[at, :] = (h * scale * gain).astype(BF16)
        return carry

    lax.fori_loop(0, (last - first) // UNIT, one, 0)


def project(normed_ref, w_ref, first, last, out_ref, places):
    width = w_ref.shape[1]
    tile = min(TILE, width)
    for at in range(0, width, tile):
        cols = slice(at, at + tile)
        out = jnp.dot(
            normed_ref[first:last, :], w_ref[:, cols], preferred_element_type=F32
        ).astype(BF16)
        done = 0
        for rows, place in places:
            out_ref[place : place + rows, cols] = out[done : done + rows]
            done += rows


def attend(first, last, q_ref, k_ref, v_ref, att_ref, bias_ref, score_ref, prob_ref, range_ref):
    pairs = q_ref.shape[1] // PAIR
    ones = jnp.ones((WINDOW, PAIR), BF16)
    factor = HEAD_DIM**-0.5 * math.log2(math.e)

    def at(unit):
        start = pl.multiple_of(unit * UNIT, 16)
        return pl.ds(start, UNIT), pl.ds(pl.multiple_of(start - UNIT, 16), WINDOW)

    def score(unit):
        rows, window = at(unit)
        one = lax.broadcasted_iota(jnp.int32, (UNIT, PAIR), 1) < HEAD_DIM
        for p in range(pairs):
            lanes = slice(p * PAIR, (p + 1) * PAIR)
            q = q_ref[rows, lanes]
            zero = jnp.zeros_like(q)
            both = jnp.concatenate([jnp.where(one, q, zero), jnp.where(one, zero, q)], axis=0)
            score_ref[2 * p * UNIT : 2 * (p + 1) * UNIT, :] = lax.dot_general(
                both, k_ref[window, lanes], (((1,), (1,)), ((), ())), preferred_element_type=F32
            )

    def soften(unit, shift=False):
        bias = bias_ref[unit]
        for head in range(2 * pairs):
            rows = slice(head * UNIT, (head + 1) * UNIT)
            s = score_ref[rows, :] * factor + bias
            if shift:
                s = s - jnp.max(s, axis=-1, keepdims=True)
            prob_ref[rows, :] = jnp.exp2(s).astype(BF16)

    def mix(unit):
        rows, window = at(unit)
        one = lax.broadcasted_iota(jnp.int32, (UNIT, PAIR), 1) < HEAD_DIM
        low, high = range_ref[0], range_ref[1]
        for p in range(pairs):
            lanes = slice(p * PAIR, (p + 1) * PAIR)
            values = jnp.concatenate([v_ref[window, lanes], ones], axis=1)
            out = jnp.dot(
                prob_ref[2 * p * UNIT : 2 * (p + 1) * UNIT, :], values, preferred_element_type=F32
            )
            mixed = jnp.where(one, out[:UNIT, :PAIR], out[UNIT:, :PAIR])
            sums = jnp.where(one, out[:UNIT, PAIR:], out[UNIT:, PAIR:])
            low, high = jnp.minimum(low, sums), jnp.maximum(high, sums)
            att_ref[rows, lanes] = (mixed * pl.reciprocal(sums, approx=True)).astype(BF16)
        range_ref[0] = low
        range_ref[1] = high

    range_ref[...] = jnp.ones_like(range_ref)
    score(first)
    soften(first)
    score(first + 1)

    def one(unit, carry):
        mix(unit)
        soften(unit + 1)
        score(unit + 2)
        return carry

    lax.fori_loop(first, last - 2, one, 0)
    mix(last - 2)
    soften(last - 1)
    mix(last - 1)
    fine = (jnp.min(range_ref[0]) >= SUM_LOW) & (jnp.max(range_ref[1]) <= SUM_HIGH)

    @pl.when(jnp.logical_not(fine))
    def _():
        def shifted(unit, carry):
            score(unit)
            soften(unit, shift=True)
            mix(unit)
            return carry

        lax.fori_loop(first, last, shifted, 0)


def edge_kernel(
    state_hbm, cond_hbm, ids_hbm, time_hbm, gain_hbm,
    cross_ref, core_ref, small_ref,
    state_last, cond_last, state_first, cond_first, ids_ref, time_ref, gain_ref, sems,
):
    own = state_hbm.shape[0]
    copies = [
        pltpu.make_async_copy(source, target, sems.at[i])
        for i, (source, target) in enumerate(
            (
                (state_hbm.at[pl.ds(own - BEHIND, BEHIND)], state_last),
                (cond_hbm.at[pl.ds(own - BEHIND, BEHIND)], cond_last),
                (state_hbm.at[pl.ds(0, AHEAD)], state_first),
                (cond_hbm.at[pl.ds(0, AHEAD)], cond_first),
                (ids_hbm, ids_ref),
                (time_hbm, time_ref),
                (gain_hbm, gain_ref),
            )
        )
    ]
    for copy in copies:
        copy.start()
    even = lax.rem(lax.axis_index("seq"), 2) == 0
    for copy in copies:
        copy.wait()

    depth = core_ref.shape[1]

    def number_row(ids):
        blank = jnp.zeros((1, depth - ids.shape[1]), F32)
        return jnp.concatenate([(ids + 1).astype(F32), blank], axis=1)

    vectors = [ref[...].astype(F32).reshape(1, -1) for ref in (time_ref, gain_ref)]
    blank = jnp.zeros((SMALL - 3, depth), F32)
    small_ref[...] = jnp.concatenate([number_row(ids_ref[...]), *vectors, blank], axis=0).astype(BF16)

    def fill(ref, state, cond, ids):
        rows = state.shape[0]
        ref[0:rows, :] = (state[...].astype(F32) + cond[...].astype(F32)).astype(BF16)
        if rows < BEHIND:
            ref[rows:BEHIND, :] = jnp.zeros((BEHIND - rows, depth), BF16)
        ref[BEHIND:, :] = jnp.broadcast_to(number_row(ids), (PAYLOAD - BEHIND, depth)).astype(BF16)

    def fill_both(to_next, to_previous):
        fill(to_next, state_last, cond_last, ids_ref[:, own - BEHIND :])
        fill(to_previous, state_first, cond_first, ids_ref[:, :BEHIND])

    @pl.when(even)
    def _():
        fill_both(core_ref, cross_ref)

    @pl.when(jnp.logical_not(even))
    def _():
        fill_both(cross_ref, core_ref)


def own_kernel(
    small_ref, state_hbm, cond_hbm, wqkv_hbm,
    state_ref, cond_ref, q_ref, k_ref, v_ref, seg_ref, bias_ref,
    wk_ref, wv_ref, wq_ref, normed_ref, sems,
):
    own = state_ref.shape[0]
    copies = [
        pltpu.make_async_copy(state_hbm, state_ref, sems.at[0]),
        pltpu.make_async_copy(cond_hbm, cond_ref, sems.at[1]),
    ]
    weights = [
        pltpu.make_async_copy(wqkv_hbm.at[which], w_ref, sems.at[2 + which])
        for which, w_ref in ((1, wk_ref), (2, wv_ref), (0, wq_ref))
    ]
    for copy in copies + weights[:1]:
        copy.start()
    gain = small_ref[2:3, :].astype(F32)
    own_segments(small_ref, seg_ref, own)
    build_masks((3, own // UNIT + 1), seg_ref, bias_ref)
    copies[0].wait()
    copies[1].wait()
    for copy in weights[1:]:
        copy.start()

    def one(i, carry):
        at = pl.ds(pl.multiple_of(i * UNIT, 16), UNIT)
        h = state_ref[at, :].astype(F32) + cond_ref[at, :].astype(F32)
        scale = lax.rsqrt(jnp.mean(h * h, axis=-1, keepdims=True) + 1e-06)
        normed_ref[at, :] = (h * scale * gain).astype(BF16)
        return carry

    lax.fori_loop(0, own // UNIT, one, 0)
    for w_ref, copy, out_ref in zip((wk_ref, wv_ref, wq_ref), weights, (k_ref, v_ref, q_ref)):
        copy.wait()
        project(normed_ref, w_ref, 0, own, out_ref, [(own, 0)])


def rest_kernel(
    cross_ref, core_ref, small_ref, state_ref, cond_ref, q_own, k_own, v_own, seg_own, bias_own,
    wqkv_hbm, wout_hbm,
    out_hbm,
    wk_ref, wv_ref, wq_ref, wout, behind_ref, ahead_ref, halo_ref, h_ref, out_ref,
    normed_ref, q_ref, k_ref, v_ref, att_ref, seg_ref, bias_ref, score_ref, prob_ref, range_ref,
    sems,
):
    own = state_ref.shape[0]
    units = own // UNIT
    end = BEHIND + own
    total = end + AHEAD
    weights = [
        pltpu.make_async_copy(wqkv_hbm.at[which], w_ref, sems.at[which])
        for which, w_ref in ((1, wk_ref), (2, wv_ref), (0, wq_ref))
    ]
    wout_copy = pltpu.make_async_copy(wout_hbm, wout, sems.at[3])
    weights[0].start()
    half_time = 0.5 * small_ref[1:2, :].astype(F32)
    gain = small_ref[2:3, :].astype(F32)
    even = lax.rem(lax.axis_index("seq"), 2) == 0

    def take(before, after):
        behind_ref[...] = before[...]
        ahead_ref[...] = after[...]

    @pl.when(even)
    def _():
        take(cross_ref, core_ref)

    @pl.when(jnp.logical_not(even))
    def _():
        take(core_ref, cross_ref)

    seg_ref[BEHIND:end, :] = seg_own[BEHIND:end, :]
    edge_segments(behind_ref, ahead_ref, seg_ref)
    bias_ref[3 : units + 1] = bias_own[3 : units + 1]
    for unit in (1, 2, units + 1, units + 2):
        build_mask(unit, seg_ref, bias_ref)
    for ref, rows, place in ((behind_ref, BEHIND, 0), (ahead_ref, AHEAD, BEHIND)):
        h = ref[0:rows, :].astype(F32)
        scale = lax.rsqrt(jnp.mean(h * h, axis=-1, keepdims=True) + 1e-06)
        halo_ref[place : place + rows, :] = (h * scale * gain).astype(BF16)
    for ref, whole in ((q_ref, q_own), (k_ref, k_own), (v_ref, v_own)):
        ref[BEHIND:end, :] = whole[...]
    for copy in weights[1:] + [wout_copy]:
        copy.start()
    clear_spare((k_ref, v_ref))
    both = [(BEHIND, 0), (AHEAD, end)]
    edges = [(UNIT, UNIT), (AHEAD, end)]
    weights[0].wait()
    project(halo_ref, wk_ref, 0, BEHIND + AHEAD, k_ref, both)
    weights[1].wait()
    project(halo_ref, wv_ref, 0, BEHIND + AHEAD, v_ref, both)
    weights[2].wait()
    project(halo_ref, wq_ref, UNIT, BEHIND + AHEAD, q_ref, edges)
    attend(1, total // UNIT, q_ref, k_ref, v_ref, att_ref, bias_ref, score_ref, prob_ref, range_ref)
    wout_copy.wait()
    depth = wout.shape[1]
    for at in range(0, depth, TILE):
        cols = slice(at, at + TILE)
        moved = 0.5 * jnp.dot(att_ref[UNIT:total, :], wout[:, cols], preferred_element_type=F32)
        moved = moved + half_time[:, cols]
        h_ref[UNIT:BEHIND, cols] = behind_ref[UNIT:BEHIND, cols].astype(F32) + moved[:UNIT]
        h_ref[BEHIND:end, cols] = (
            state_ref[:, cols].astype(F32) + cond_ref[:, cols].astype(F32)
        ) + moved[UNIT : UNIT + own]
        h_ref[end:total, cols] = ahead_ref[0:AHEAD, cols].astype(F32) + moved[UNIT + own :]

    normalize(h_ref, normed_ref, gain, UNIT, total)
    project(normed_ref, wk_ref, UNIT, total, k_ref, [(total - UNIT, UNIT)])
    project(normed_ref, wv_ref, UNIT, total, v_ref, [(total - UNIT, UNIT)])
    project(normed_ref, wq_ref, BEHIND, end, q_ref, [(own, BEHIND)])
    attend(
        BEHIND // UNIT, end // UNIT, q_ref, k_ref, v_ref, att_ref, bias_ref, score_ref, prob_ref, range_ref
    )
    sent = []
    for half in range(2):
        mine = slice(half * own // 2, (half + 1) * own // 2)
        rows = slice(BEHIND + mine.start, BEHIND + mine.stop)
        for at in range(0, depth, TILE):
            cols = slice(at, at + TILE)
            moved = jnp.dot(att_ref[rows, :], wout[:, cols], preferred_element_type=F32)
            x = h_ref[rows, cols] - cond_ref[mine, cols].astype(F32) - half_time[:, cols]
            out_ref[mine, cols] = (x + 0.5 * moved).astype(BF16)
        part = pl.ds(mine.start, own // 2)
        sent.append(pltpu.make_async_copy(out_ref.at[part], out_hbm.at[part], sems.at[4 + half]))
        sent[-1].start()
    for copy in sent:
        copy.wait()


def clear_spare(refs):
    for ref in refs:
        ref[ref.shape[0] - SPARE :, :] = jnp.zeros((SPARE, ref.shape[1]), ref.dtype)


def one_step(
    final, h_ref, small_ref, behind_ref, ahead_ref, wqkv, wout,
    out_ref,
    normed_ref, q_ref, k_ref, v_ref, att_ref, seg_ref, bias_ref, score_ref, prob_ref, range_ref,
):
    total = h_ref.shape[0]
    own = total - BEHIND - AHEAD
    kv_first = UNIT if final else 0
    first, last = (BEHIND, BEHIND + own) if final else (UNIT, total)
    own_segments(small_ref, seg_ref, own)
    edge_segments(behind_ref, ahead_ref, seg_ref)
    build_masks((1, total // UNIT), seg_ref, bias_ref)
    clear_spare((k_ref, v_ref))
    normalize(h_ref, normed_ref, small_ref[2:3, :].astype(F32), kv_first, total)
    project(normed_ref, wqkv.at[1], kv_first, total, k_ref, [(total - kv_first, kv_first)])
    project(normed_ref, wqkv.at[2], kv_first, total, v_ref, [(total - kv_first, kv_first)])
    project(normed_ref, wqkv.at[0], first, last, q_ref, [(last - first, first)])
    attend(
        first // UNIT, last // UNIT,
        q_ref, k_ref, v_ref, att_ref, bias_ref, score_ref, prob_ref, range_ref,
    )
    for at in range(0, wout.shape[1], TILE):
        cols = slice(at, at + TILE)
        out_ref[:, cols] = jnp.dot(
            att_ref[first:last, :], wout[:, cols], preferred_element_type=F32
        ).astype(BF16)


def shards(state, condition, time_vector, norm_gain, w_qkv, w_out, utterance_ids):
    own, depth = state.shape
    width = w_qkv.shape[2]
    total = BEHIND + own + AHEAD
    parts = lax.axis_size("mp")
    count = lax.axis_size("seq")
    ids = utterance_ids.reshape(1, own)
    vmem = pl.BlockSpec(memory_space=pltpu.VMEM)
    hbm = pl.BlockSpec(memory_space=pltpu.HBM)

    def limit(mib):
        return pltpu.CompilerParams(vmem_limit_bytes=int(mib * 2**20))

    cross, core, small = pl.pallas_call(
        edge_kernel,
        out_shape=[jax.ShapeDtypeStruct((rows, depth), BF16) for rows in (PAYLOAD, PAYLOAD, SMALL)],
        in_specs=[hbm] * 5,
        out_specs=[vmem] * 3,
        scratch_shapes=[pltpu.VMEM((BEHIND, depth), BF16)] * 2
        + [pltpu.VMEM((AHEAD, depth), BF16)] * 2
        + [pltpu.VMEM((1, own), jnp.int32)]
        + [pltpu.VMEM((depth,), BF16)] * 2
        + [pltpu.SemaphoreType.DMA((7,))],
        compiler_params=limit(EDGE_LIMIT),
    )(state, condition, ids, time_vector, norm_gain)
    ends = [(i, i + 1) for i in range(1, count - 1, 2)]
    cross = lax.ppermute(cross, "seq", ends + [(j, i) for i, j in ends])
    ends = [(i, i + 1) for i in range(0, count - 1, 2)]
    core = lax.ppermute(core, "seq", ends + [(j, i) for i, j in ends])

    work = [((total, depth), BF16), ((total, width), BF16)]
    work += [((total + SPARE, width), BF16)] * 2
    work += [
        ((total, width), BF16),
        ((total + SPARE, 128), F32),
        ((total // UNIT, UNIT, WINDOW), F32),
        ((width // HEAD_DIM * UNIT, WINDOW), F32),
        ((width // HEAD_DIM * UNIT, WINDOW), BF16),
        ((2, UNIT, PAIR), F32),
    ]
    if parts == 1:
        kept = [(state.shape, BF16)] * 2 + [((own, width), BF16)] * 3
        kept += [((total + SPARE, 128), F32), ((total // UNIT, UNIT, WINDOW), F32)]
        kept = pl.pallas_call(
            own_kernel,
            out_shape=[jax.ShapeDtypeStruct(*one) for one in kept],
            in_specs=[vmem] + [hbm] * 3,
            out_specs=[vmem] * 7,
            scratch_shapes=[pltpu.VMEM((depth, width), BF16)] * 3
            + [pltpu.VMEM((own, depth), BF16), pltpu.SemaphoreType.DMA((5,))],
            compiler_params=limit(OWN_LIMIT),
            cost_estimate=pl.CostEstimate(
                flops=6 * own * depth * width, bytes_accessed=2 * 4 * depth * width, transcendentals=0
            ),
        )(small, state, condition, w_qkv)
        first = [((depth, width), BF16)] * 3 + [(w_out.shape, BF16)] + [((PAYLOAD, depth), BF16)] * 2
        first += [((BEHIND + AHEAD, depth), BF16), ((total, depth), F32), ((own, depth), BF16)]
        return pl.pallas_call(
            rest_kernel,
            out_shape=jax.ShapeDtypeStruct((own, depth), BF16),
            in_specs=[vmem] * 10 + [hbm] * 2,
            out_specs=hbm,
            scratch_shapes=[pltpu.VMEM(*one) for one in first + work]
            + [pltpu.SemaphoreType.DMA((6,))],
            compiler_params=limit(LIMIT),
        )(cross, core, small, *kept, w_qkv, w_out)

    even = lax.axis_index("seq") % 2 == 0
    behind = jnp.where(even, cross, core)
    ahead = jnp.where(even, core, cross)

    def terms(h, final):
        rows = own if final else total - UNIT
        mine = pl.pallas_call(
            functools.partial(one_step, final),
            out_shape=jax.ShapeDtypeStruct((rows, depth), BF16),
            in_specs=[vmem] * 6,
            out_specs=vmem,
            scratch_shapes=[pltpu.VMEM(*one) for one in work],
            compiler_params=limit(LIMIT),
        )(h, small, behind, ahead, w_qkv, w_out)
        return lax.psum(mine, "mp").astype(F32)

    start = state.astype(F32)
    h = jnp.concatenate(
        [behind[:BEHIND].astype(F32), start + condition.astype(F32), ahead[:AHEAD].astype(F32)]
    )
    velocity = terms(h, False)
    later = jnp.pad(velocity, ((UNIT, 0), (0, 0))) * 0.5 + 0.5 * time_vector.astype(F32)
    x = start + 0.5 * velocity[UNIT : UNIT + own] + 0.5 * terms(h + later, True)
    share = depth // parts
    mine = lax.dynamic_slice_in_dim(x, lax.axis_index("mp") * share, share, 1)
    return mine.astype(BF16)


def solution(mesh):
    in_specs = (
        P("seq", None),
        P("seq", None),
        P(),
        P(),
        P(None, None, "mp"),
        P("mp", None),
        P("seq"),
    )
    out_specs = P("seq", "mp")
    return jax.shard_map(shards, mesh=mesh, in_specs=in_specs, out_specs=out_specs, check_vma=False)
```

```python
import functools
import math

import jax
import jax.numpy as jnp
from jax import lax
from jax.experimental import pallas as pl
from jax.experimental.pallas import tpu as pltpu
from jax.sharding import PartitionSpec as P

HEAD_DIM = 64
BLOCK = 24
UNIT = 2 * BLOCK
BEHIND = 4 * BLOCK
AHEAD = 2 * BLOCK
WINDOW = 128
SPARE = WINDOW - 2 * UNIT
PAIR = 2 * HEAD_DIM
FOUR = 4
SUM_LOW, SUM_HIGH = 2.0**-60, 2.0**100
SMALL = 16
PAYLOAD = BEHIND + 16
TILE = 256
EDGE_LIMIT, OWN_LIMIT, LIMIT = 56, 48, 48
F32 = jnp.float32
BF16 = jnp.bfloat16
NEG = -1e30


def column_of(row):
    n = row.shape[1]
    same = lax.broadcasted_iota(jnp.int32, (n, n), 0) == lax.broadcasted_iota(jnp.int32, (n, n), 1)
    column = jnp.sum(jnp.where(same, row, 0.0), axis=1, keepdims=True)
    return jnp.broadcast_to(column, (n, 128))


def own_segments(small_ref, seg_ref, own):
    for at in range(0, own, 128):
        n = min(128, own - at)
        row = small_ref[0:1, at : at + n].astype(F32)
        seg_ref[BEHIND + at : BEHIND + at + n, :] = column_of(row)


def edge_segments(behind_ref, ahead_ref, seg_ref):
    end = seg_ref.shape[0] - SPARE
    seg_ref[0:BEHIND, :] = column_of(behind_ref[BEHIND : BEHIND + 1, 0:BEHIND].astype(F32))
    seg_ref[end - AHEAD : end, :] = column_of(ahead_ref[BEHIND : BEHIND + 1, 0:AHEAD].astype(F32))
    seg_ref[end : end + SPARE, :] = jnp.full((SPARE, 128), -1.0, F32)


def build_mask(unit, seg_ref, bias_ref):
    start = unit * UNIT
    if not isinstance(unit, int):
        start = pl.multiple_of(start, 16)
    window = seg_ref[pl.ds(start - UNIT, WINDOW), :]
    r = lax.broadcasted_iota(jnp.int32, (WINDOW, WINDOW), 0)
    c = lax.broadcasted_iota(jnp.int32, (WINDOW, WINDOW), 1)
    keys = jnp.sum(jnp.where(r == c, window, 0.0), axis=0, keepdims=True)
    queries = seg_ref[pl.ds(start, UNIT), :]
    row = lax.broadcasted_iota(jnp.int32, (UNIT, WINDOW), 0)
    col = lax.broadcasted_iota(jnp.int32, (UNIT, WINDOW), 1)
    first = jnp.where(row < BLOCK, 0, BLOCK)
    band = (col >= first) & (col < first + 4 * BLOCK)
    bias_ref[unit] = jnp.where(band & (queries == keys), 0.0, NEG)


def build_masks(units, seg_ref, bias_ref):
    def one(unit, carry):
        build_mask(unit, seg_ref, bias_ref)
        return carry

    lax.fori_loop(units[0], units[1], one, 0)


def normalize(h_ref, normed_ref, gain, first, last):
    def one(i, carry):
        at = pl.ds(pl.multiple_of(first + i * UNIT, 16), UNIT)
        h = h_ref[at, :]
        scale = lax.rsqrt(jnp.mean(h * h, axis=-1, keepdims=True) + 1e-06)
        normed_ref[at, :] = (h * scale * gain).astype(BF16)
        return carry

    lax.fori_loop(0, (last - first) // UNIT, one, 0)


def project(normed_ref, w_ref, first, last, out_ref, places):
    width = w_ref.shape[1]
    tile = min(TILE, width)
    for at in range(0, width, tile):
        cols = slice(at, at + tile)
        out = jnp.dot(
            normed_ref[first:last, :], w_ref[:, cols], preferred_element_type=F32
        ).astype(BF16)
        done = 0
        for rows, place in places:
            out_ref[place : place + rows, cols] = out[done : done + rows]
            done += rows


def attend(first, last, q_ref, k_ref, v_ref, att_ref, bias_ref, score_ref, prob_ref, range_ref):
    wide = FOUR * HEAD_DIM
    groups = q_ref.shape[1] // wide
    factor = HEAD_DIM**-0.5 * math.log2(math.e)

    def at(unit):
        start = pl.multiple_of(unit * UNIT, 16)
        return pl.ds(start, UNIT), pl.ds(pl.multiple_of(start - UNIT, 16), WINDOW)

    def score(unit):
        rows, window = at(unit)
        head = lax.broadcasted_iota(jnp.int32, (UNIT, wide), 1) // HEAD_DIM
        for g in range(groups):
            lanes = slice(g * wide, (g + 1) * wide)
            q = q_ref[rows, lanes]
            zero = jnp.zeros_like(q)
            stacked = jnp.concatenate([jnp.where(head == j, q, zero) for j in range(FOUR)], axis=0)
            score_ref[FOUR * g * UNIT : FOUR * (g + 1) * UNIT, :] = lax.dot_general(
                stacked, k_ref[window, lanes], (((1,), (1,)), ((), ())), preferred_element_type=F32
            )

    def soften(unit, shift=False):
        bias = bias_ref[unit]
        low, high = range_ref[0], range_ref[1]
        for j in range(FOUR * groups):
            rows = slice(j * UNIT, (j + 1) * UNIT)
            s = score_ref[rows, :] * factor + bias
            if shift:
                s = s - jnp.max(s, axis=-1, keepdims=True)
            expo = jnp.exp2(s)
            total = jnp.sum(expo, axis=-1, keepdims=True)
            low, high = jnp.minimum(low, total), jnp.maximum(high, total)
            prob_ref[rows, :] = (expo * pl.reciprocal(total, approx=True)).astype(BF16)
        range_ref[0] = low
        range_ref[1] = high

    def mix(unit):
        rows, window = at(unit)
        one = lax.broadcasted_iota(jnp.int32, (UNIT, PAIR), 1) < HEAD_DIM
        for g in range(groups):
            lanes = slice(g * wide, (g + 1) * wide)
            top = FOUR * g * UNIT
            out = jnp.dot(
                prob_ref[top : top + FOUR * UNIT, :], v_ref[window, lanes], preferred_element_type=F32
            )
            for p in range(FOUR // 2):
                low, high = 2 * p * UNIT, (2 * p + 1) * UNIT
                cols = slice(p * PAIR, (p + 1) * PAIR)
                mixed = jnp.where(one, out[low : low + UNIT, cols], out[high : high + UNIT, cols])
                att_ref[rows, g * wide + p * PAIR : g * wide + (p + 1) * PAIR] = mixed.astype(BF16)

    range_ref[...] = jnp.ones_like(range_ref)
    score(first)
    soften(first)
    score(first + 1)

    def one(unit, carry):
        mix(unit)
        soften(unit + 1)
        score(unit + 2)
        return carry

    lax.fori_loop(first, last - 2, one, 0)
    mix(last - 2)
    soften(last - 1)
    mix(last - 1)
    fine = (jnp.min(range_ref[0]) >= SUM_LOW) & (jnp.max(range_ref[1]) <= SUM_HIGH)

    @pl.when(jnp.logical_not(fine))
    def _():
        def shifted(unit, carry):
            score(unit)
            soften(unit, shift=True)
            mix(unit)
            return carry

        lax.fori_loop(first, last, shifted, 0)


def edge_kernel(
    state_hbm, cond_hbm, ids_hbm, time_hbm, gain_hbm,
    cross_ref, core_ref, small_hbm,
    small_ref, state_last, cond_last, state_first, cond_first, ids_ref, time_ref, gain_ref, sems,
):
    own = state_hbm.shape[0]
    copies = [
        pltpu.make_async_copy(source, target, sems.at[i])
        for i, (source, target) in enumerate(
            (
                (state_hbm.at[pl.ds(own - BEHIND, BEHIND)], state_last),
                (cond_hbm.at[pl.ds(own - BEHIND, BEHIND)], cond_last),
                (state_hbm.at[pl.ds(0, AHEAD)], state_first),
                (cond_hbm.at[pl.ds(0, AHEAD)], cond_first),
                (ids_hbm, ids_ref),
                (time_hbm, time_ref),
                (gain_hbm, gain_ref),
            )
        )
    ]
    for copy in copies:
        copy.start()
    even = lax.rem(lax.axis_index("seq"), 2) == 0
    for copy in copies:
        copy.wait()

    depth = core_ref.shape[1]

    def number_row(ids):
        blank = jnp.zeros((1, depth - ids.shape[1]), F32)
        return jnp.concatenate([(ids + 1).astype(F32), blank], axis=1)

    vectors = [ref[...].astype(F32).reshape(1, -1) for ref in (time_ref, gain_ref)]
    blank = jnp.zeros((SMALL - 3, depth), F32)
    small_ref[...] = jnp.concatenate([number_row(ids_ref[...]), *vectors, blank], axis=0).astype(BF16)
    kept = pltpu.make_async_copy(small_ref, small_hbm.at[pl.ds(0, SMALL)], sems.at[7])
    kept.start()

    def fill(ref, state, cond, ids):
        rows = state.shape[0]
        ref[0:rows, :] = (state[...].astype(F32) + cond[...].astype(F32)).astype(BF16)
        if rows < BEHIND:
            ref[rows:BEHIND, :] = jnp.zeros((BEHIND - rows, depth), BF16)
        ref[BEHIND:, :] = jnp.broadcast_to(number_row(ids), (PAYLOAD - BEHIND, depth)).astype(BF16)

    def fill_both(to_next, to_previous):
        fill(to_next, state_last, cond_last, ids_ref[:, own - BEHIND :])
        fill(to_previous, state_first, cond_first, ids_ref[:, :BEHIND])

    @pl.when(even)
    def _():
        fill_both(core_ref, cross_ref)

    @pl.when(jnp.logical_not(even))
    def _():
        fill_both(cross_ref, core_ref)

    kept.wait()


def own_kernel(
    small_hbm, state_hbm, cond_hbm, wqkv_hbm,
    small_ref, state_ref, cond_ref, q_ref, k_ref, v_ref, seg_ref, bias_ref,
    wk_ref, wv_ref, wq_ref, normed_ref, sems,
):
    own = state_ref.shape[0]
    copies = [
        pltpu.make_async_copy(state_hbm, state_ref, sems.at[0]),
        pltpu.make_async_copy(cond_hbm, cond_ref, sems.at[1]),
        pltpu.make_async_copy(small_hbm.at[pl.ds(0, SMALL)], small_ref, sems.at[5]),
    ]
    weights = [
        pltpu.make_async_copy(wqkv_hbm.at[which], w_ref, sems.at[2 + which])
        for which, w_ref in ((1, wk_ref), (2, wv_ref), (0, wq_ref))
    ]
    for copy in copies + weights[:1]:
        copy.start()
    copies[2].wait()
    gain = small_ref[2:3, :].astype(F32)
    own_segments(small_ref, seg_ref, own)
    build_masks((3, own // UNIT + 1), seg_ref, bias_ref)
    copies[0].wait()
    copies[1].wait()
    for copy in weights[1:]:
        copy.start()

    def one(i, carry):
        at = pl.ds(pl.multiple_of(i * UNIT, 16), UNIT)
        h = state_ref[at, :].astype(F32) + cond_ref[at, :].astype(F32)
        scale = lax.rsqrt(jnp.mean(h * h, axis=-1, keepdims=True) + 1e-06)
        normed_ref[at, :] = (h * scale * gain).astype(BF16)
        return carry

    lax.fori_loop(0, own // UNIT, one, 0)
    for w_ref, copy, out_ref in zip((wk_ref, wv_ref, wq_ref), weights, (k_ref, v_ref, q_ref)):
        copy.wait()
        project(normed_ref, w_ref, 0, own, out_ref, [(own, 0)])


def rest_kernel(
    cross_ref, core_ref, small_ref, state_ref, cond_ref, q_own, k_own, v_own, seg_own, bias_own,
    wqkv_hbm, wout_hbm,
    out_ref,
    wk_ref, wv_ref, wq_ref, wout, behind_ref, ahead_ref, halo_ref, h_ref,
    normed_ref, q_ref, k_ref, v_ref, att_ref, seg_ref, bias_ref, score_ref, prob_ref, range_ref,
    sems,
):
    own = state_ref.shape[0]
    units = own // UNIT
    end = BEHIND + own
    total = end + AHEAD
    weights = [
        pltpu.make_async_copy(wqkv_hbm.at[which], w_ref, sems.at[which])
        for which, w_ref in ((1, wk_ref), (2, wv_ref), (0, wq_ref))
    ]
    wout_copy = pltpu.make_async_copy(wout_hbm, wout, sems.at[3])
    weights[0].start()
    half_time = 0.5 * small_ref[1:2, :].astype(F32)
    gain = small_ref[2:3, :].astype(F32)
    even = lax.rem(lax.axis_index("seq"), 2) == 0

    def take(before, after):
        behind_ref[...] = before[...]
        ahead_ref[...] = after[...]

    @pl.when(even)
    def _():
        take(cross_ref, core_ref)

    @pl.when(jnp.logical_not(even))
    def _():
        take(core_ref, cross_ref)

    seg_ref[BEHIND:end, :] = seg_own[BEHIND:end, :]
    edge_segments(behind_ref, ahead_ref, seg_ref)
    bias_ref[3 : units + 1] = bias_own[3 : units + 1]
    for unit in (1, 2, units + 1, units + 2):
        build_mask(unit, seg_ref, bias_ref)
    for ref, rows, place in ((behind_ref, BEHIND, 0), (ahead_ref, AHEAD, BEHIND)):
        h = ref[0:rows, :].astype(F32)
        scale = lax.rsqrt(jnp.mean(h * h, axis=-1, keepdims=True) + 1e-06)
        halo_ref[place : place + rows, :] = (h * scale * gain).astype(BF16)
    for ref, whole in ((q_ref, q_own), (k_ref, k_own), (v_ref, v_own)):
        ref[BEHIND:end, :] = whole[...]
    for copy in weights[1:] + [wout_copy]:
        copy.start()
    clear_spare((k_ref, v_ref))
    both = [(BEHIND, 0), (AHEAD, end)]
    edges = [(UNIT, UNIT), (AHEAD, end)]
    weights[0].wait()
    project(halo_ref, wk_ref, 0, BEHIND + AHEAD, k_ref, both)
    weights[1].wait()
    project(halo_ref, wv_ref, 0, BEHIND + AHEAD, v_ref, both)
    weights[2].wait()
    project(halo_ref, wq_ref, UNIT, BEHIND + AHEAD, q_ref, edges)
    attend(1, total // UNIT, q_ref, k_ref, v_ref, att_ref, bias_ref, score_ref, prob_ref, range_ref)
    wout_copy.wait()
    depth = wout.shape[1]
    for at in range(0, depth, TILE):
        cols = slice(at, at + TILE)
        moved = 0.5 * jnp.dot(att_ref[UNIT:total, :], wout[:, cols], preferred_element_type=F32)
        moved = moved + half_time[:, cols]
        h_ref[UNIT:BEHIND, cols] = behind_ref[UNIT:BEHIND, cols].astype(F32) + moved[:UNIT]
        h_ref[BEHIND:end, cols] = (
            state_ref[:, cols].astype(F32) + cond_ref[:, cols].astype(F32)
        ) + moved[UNIT : UNIT + own]
        h_ref[end:total, cols] = ahead_ref[0:AHEAD, cols].astype(F32) + moved[UNIT + own :]

    normalize(h_ref, normed_ref, gain, UNIT, total)
    project(normed_ref, wk_ref, UNIT, total, k_ref, [(total - UNIT, UNIT)])
    project(normed_ref, wv_ref, UNIT, total, v_ref, [(total - UNIT, UNIT)])
    project(normed_ref, wq_ref, BEHIND, end, q_ref, [(own, BEHIND)])
    attend(
        BEHIND // UNIT, end // UNIT, q_ref, k_ref, v_ref, att_ref, bias_ref, score_ref, prob_ref, range_ref
    )
    for at in range(0, depth, TILE):
        cols = slice(at, at + TILE)
        moved = jnp.dot(att_ref[BEHIND:end, :], wout[:, cols], preferred_element_type=F32)
        x = h_ref[BEHIND:end, cols] - cond_ref[:, cols].astype(F32) - half_time[:, cols]
        out_ref[:, cols] = (x + 0.5 * moved).astype(BF16)


def clear_spare(refs):
    for ref in refs:
        ref[ref.shape[0] - SPARE :, :] = jnp.zeros((SPARE, ref.shape[1]), ref.dtype)


def one_step(
    final, h_ref, small_ref, behind_ref, ahead_ref, wqkv, wout,
    out_ref,
    normed_ref, q_ref, k_ref, v_ref, att_ref, seg_ref, bias_ref, score_ref, prob_ref, range_ref,
):
    total = h_ref.shape[0]
    own = total - BEHIND - AHEAD
    kv_first = UNIT if final else 0
    first, last = (BEHIND, BEHIND + own) if final else (UNIT, total)
    own_segments(small_ref, seg_ref, own)
    edge_segments(behind_ref, ahead_ref, seg_ref)
    build_masks((1, total // UNIT), seg_ref, bias_ref)
    clear_spare((k_ref, v_ref))
    normalize(h_ref, normed_ref, small_ref[2:3, :].astype(F32), kv_first, total)
    project(normed_ref, wqkv.at[1], kv_first, total, k_ref, [(total - kv_first, kv_first)])
    project(normed_ref, wqkv.at[2], kv_first, total, v_ref, [(total - kv_first, kv_first)])
    project(normed_ref, wqkv.at[0], first, last, q_ref, [(last - first, first)])
    attend(
        first // UNIT, last // UNIT,
        q_ref, k_ref, v_ref, att_ref, bias_ref, score_ref, prob_ref, range_ref,
    )
    for at in range(0, wout.shape[1], TILE):
        cols = slice(at, at + TILE)
        out_ref[:, cols] = jnp.dot(
            att_ref[first:last, :], wout[:, cols], preferred_element_type=F32
        ).astype(BF16)


def shards(state, condition, time_vector, norm_gain, w_qkv, w_out, utterance_ids):
    own, depth = state.shape
    width = w_qkv.shape[2]
    total = BEHIND + own + AHEAD
    parts = lax.axis_size("mp")
    count = lax.axis_size("seq")
    ids = utterance_ids.reshape(1, own)
    vmem = pl.BlockSpec(memory_space=pltpu.VMEM)
    hbm = pl.BlockSpec(memory_space=pltpu.HBM)

    def limit(mib):
        return pltpu.CompilerParams(vmem_limit_bytes=int(mib * 2**20))

    cross, core, small = pl.pallas_call(
        edge_kernel,
        out_shape=[jax.ShapeDtypeStruct((rows, depth), BF16) for rows in (PAYLOAD, PAYLOAD, 2 * own)],
        in_specs=[hbm] * 5,
        out_specs=[vmem, vmem, hbm],
        scratch_shapes=[pltpu.VMEM((SMALL, depth), BF16)]
        + [pltpu.VMEM((BEHIND, depth), BF16)] * 2
        + [pltpu.VMEM((AHEAD, depth), BF16)] * 2
        + [pltpu.VMEM((1, own), jnp.int32)]
        + [pltpu.VMEM((depth,), BF16)] * 2
        + [pltpu.SemaphoreType.DMA((8,))],
        compiler_params=limit(EDGE_LIMIT),
    )(state, condition, ids, time_vector, norm_gain)
    ends = [(i, i + 1) for i in range(1, count - 1, 2)]
    cross = lax.ppermute(cross, "seq", ends + [(j, i) for i, j in ends])
    ends = [(i, i + 1) for i in range(0, count - 1, 2)]
    core = lax.ppermute(core, "seq", ends + [(j, i) for i, j in ends])

    work = [((total, depth), BF16), ((total, width), BF16)]
    work += [((total + SPARE, width), BF16)] * 2
    work += [
        ((total, width), BF16),
        ((total + SPARE, 128), F32),
        ((total // UNIT, UNIT, WINDOW), F32),
        ((width // HEAD_DIM * UNIT, WINDOW), F32),
        ((width // HEAD_DIM * UNIT, WINDOW), BF16),
        ((2, UNIT, PAIR), F32),
    ]
    if parts == 1:
        kept = [((SMALL, depth), BF16)] + [(state.shape, BF16)] * 2 + [((own, width), BF16)] * 3
        kept += [((total + SPARE, 128), F32), ((total // UNIT, UNIT, WINDOW), F32)]
        kept = pl.pallas_call(
            own_kernel,
            out_shape=[jax.ShapeDtypeStruct(*one) for one in kept],
            in_specs=[hbm] * 4,
            out_specs=[vmem] * 8,
            scratch_shapes=[pltpu.VMEM((depth, width), BF16)] * 3
            + [pltpu.VMEM((own, depth), BF16), pltpu.SemaphoreType.DMA((6,))],
            compiler_params=limit(OWN_LIMIT),
            cost_estimate=pl.CostEstimate(
                flops=6 * own * depth * width, bytes_accessed=2 * 4 * depth * width, transcendentals=0
            ),
        )(small, state, condition, w_qkv)
        first = [((depth, width), BF16)] * 3 + [(w_out.shape, BF16)] + [((PAYLOAD, depth), BF16)] * 2
        first += [((BEHIND + AHEAD, depth), BF16), ((total, depth), F32)]
        return pl.pallas_call(
            rest_kernel,
            out_shape=jax.ShapeDtypeStruct((own, depth), BF16),
            in_specs=[vmem] * 10 + [hbm] * 2,
            out_specs=vmem,
            scratch_shapes=[pltpu.VMEM(*one) for one in first + work]
            + [pltpu.SemaphoreType.DMA((4,))],
            compiler_params=limit(LIMIT),
        )(cross, core, *kept, w_qkv, w_out)

    even = lax.axis_index("seq") % 2 == 0
    small = small[:SMALL]
    behind = jnp.where(even, cross, core)
    ahead = jnp.where(even, core, cross)

    def terms(h, final):
        rows = own if final else total - UNIT
        mine = pl.pallas_call(
            functools.partial(one_step, final),
            out_shape=jax.ShapeDtypeStruct((rows, depth), BF16),
            in_specs=[vmem] * 6,
            out_specs=vmem,
            scratch_shapes=[pltpu.VMEM(*one) for one in work],
            compiler_params=limit(LIMIT),
        )(h, small, behind, ahead, w_qkv, w_out)
        return lax.psum(mine, "mp").astype(F32)

    start = state.astype(F32)
    h = jnp.concatenate(
        [behind[:BEHIND].astype(F32), start + condition.astype(F32), ahead[:AHEAD].astype(F32)]
    )
    velocity = terms(h, False)
    later = jnp.pad(velocity, ((UNIT, 0), (0, 0))) * 0.5 + 0.5 * time_vector.astype(F32)
    x = start + 0.5 * velocity[UNIT : UNIT + own] + 0.5 * terms(h + later, True)
    share = depth // parts
    mine = lax.dynamic_slice_in_dim(x, lax.axis_index("mp") * share, share, 1)
    return mine.astype(BF16)


def solution(mesh):
    in_specs = (
        P("seq", None),
        P("seq", None),
        P(),
        P(),
        P(None, None, "mp"),
        P("mp", None),
        P("seq"),
    )
    out_specs = P("seq", "mp")
    return jax.shard_map(shards, mesh=mesh, in_specs=in_specs, out_specs=out_specs, check_vma=False)
```

```python
import functools
import math

import jax
import jax.numpy as jnp
from jax import lax
from jax.experimental import pallas as pl
from jax.experimental.pallas import tpu as pltpu
from jax.sharding import PartitionSpec as P

HEAD_DIM = 64
BLOCK = 24
UNIT = 2 * BLOCK
BEHIND = 4 * BLOCK
AHEAD = 2 * BLOCK
WINDOW = 128
SPARE = WINDOW - 2 * UNIT
PAIR = 2 * HEAD_DIM
FOUR = 4
SUM_LOW, SUM_HIGH = 2.0**-60, 2.0**100
SMALL = 16
PAYLOAD = BEHIND + 16
TILE = 256
EDGE_LIMIT, OWN_LIMIT, LIMIT = 56, 48, 48
F32 = jnp.float32
BF16 = jnp.bfloat16
NEG = -1e30


def column_of(row):
    n = row.shape[1]
    same = lax.broadcasted_iota(jnp.int32, (n, n), 0) == lax.broadcasted_iota(jnp.int32, (n, n), 1)
    column = jnp.sum(jnp.where(same, row, 0.0), axis=1, keepdims=True)
    return jnp.broadcast_to(column, (n, 128))


def own_segments(small_ref, seg_ref, own):
    for at in range(0, own, 128):
        n = min(128, own - at)
        row = small_ref[0:1, at : at + n].astype(F32)
        seg_ref[BEHIND + at : BEHIND + at + n, :] = column_of(row)


def edge_segments(behind_ref, ahead_ref, seg_ref):
    end = seg_ref.shape[0] - SPARE
    seg_ref[0:BEHIND, :] = column_of(behind_ref[BEHIND : BEHIND + 1, 0:BEHIND].astype(F32))
    seg_ref[end - AHEAD : end, :] = column_of(ahead_ref[BEHIND : BEHIND + 1, 0:AHEAD].astype(F32))
    seg_ref[end : end + SPARE, :] = jnp.full((SPARE, 128), -1.0, F32)


def build_mask(unit, seg_ref, bias_ref):
    start = unit * UNIT
    if not isinstance(unit, int):
        start = pl.multiple_of(start, 16)
    window = seg_ref[pl.ds(start - UNIT, WINDOW), :]
    r = lax.broadcasted_iota(jnp.int32, (WINDOW, WINDOW), 0)
    c = lax.broadcasted_iota(jnp.int32, (WINDOW, WINDOW), 1)
    keys = jnp.sum(jnp.where(r == c, window, 0.0), axis=0, keepdims=True)
    queries = seg_ref[pl.ds(start, UNIT), :]
    row = lax.broadcasted_iota(jnp.int32, (UNIT, WINDOW), 0)
    col = lax.broadcasted_iota(jnp.int32, (UNIT, WINDOW), 1)
    first = jnp.where(row < BLOCK, 0, BLOCK)
    band = (col >= first) & (col < first + 4 * BLOCK)
    bias_ref[unit] = jnp.where(band & (queries == keys), 0.0, NEG)


def build_masks(units, seg_ref, bias_ref):
    def one(unit, carry):
        build_mask(unit, seg_ref, bias_ref)
        return carry

    lax.fori_loop(units[0], units[1], one, 0)


def normalize(h_ref, normed_ref, gain, first, last):
    def one(i, carry):
        at = pl.ds(pl.multiple_of(first + i * UNIT, 16), UNIT)
        h = h_ref[at, :]
        scale = lax.rsqrt(jnp.mean(h * h, axis=-1, keepdims=True) + 1e-06)
        normed_ref[at, :] = (h * scale * gain).astype(BF16)
        return carry

    lax.fori_loop(0, (last - first) // UNIT, one, 0)


def project(normed_ref, w_ref, first, last, out_ref, places):
    width = w_ref.shape[1]
    tile = min(TILE, width)
    for at in range(0, width, tile):
        cols = slice(at, at + tile)
        out = jnp.dot(
            normed_ref[first:last, :], w_ref[:, cols], preferred_element_type=F32
        ).astype(BF16)
        done = 0
        for rows, place in places:
            out_ref[place : place + rows, cols] = out[done : done + rows]
            done += rows


def attend(first, last, q_ref, k_ref, v_ref, att_ref, bias_ref, range_ref, group_refs):
    wide = FOUR * HEAD_DIM
    groups = q_ref.shape[1] // wide
    factor = HEAD_DIM**-0.5 * math.log2(math.e)

    def at(unit):
        start = pl.multiple_of(unit * UNIT, 16)
        return pl.ds(start, UNIT), pl.ds(pl.multiple_of(start - UNIT, 16), WINDOW)

    score_refs, prob_refs = group_refs[:groups], group_refs[groups:]

    def score(unit, g):
        rows, window = at(unit)
        head = lax.broadcasted_iota(jnp.int32, (UNIT, wide), 1) // HEAD_DIM
        lanes = slice(g * wide, (g + 1) * wide)
        q = q_ref[rows, lanes]
        zero = jnp.zeros_like(q)
        stacked = jnp.concatenate([jnp.where(head == j, q, zero) for j in range(FOUR)], axis=0)
        score_refs[g][...] = lax.dot_general(
            stacked, k_ref[window, lanes], (((1,), (1,)), ((), ())), preferred_element_type=F32
        )

    def soften(unit, g, shift=False):
        bias = bias_ref[unit]
        low, high = range_ref[0], range_ref[1]
        for j in range(FOUR):
            rows = slice(j * UNIT, (j + 1) * UNIT)
            s = score_refs[g][rows, :] * factor + bias
            if shift:
                s = s - jnp.max(s, axis=-1, keepdims=True)
            expo = jnp.exp2(s)
            total = jnp.sum(expo, axis=-1, keepdims=True)
            low, high = jnp.minimum(low, total), jnp.maximum(high, total)
            prob_refs[g][rows, :] = (expo * pl.reciprocal(total, approx=True)).astype(BF16)
        range_ref[0] = low
        range_ref[1] = high

    def mix(unit, g):
        rows, window = at(unit)
        one = lax.broadcasted_iota(jnp.int32, (UNIT, PAIR), 1) < HEAD_DIM
        lanes = slice(g * wide, (g + 1) * wide)
        out = jnp.dot(prob_refs[g][...], v_ref[window, lanes], preferred_element_type=F32)
        for p in range(FOUR // 2):
            low, high = 2 * p * UNIT, (2 * p + 1) * UNIT
            cols = slice(p * PAIR, (p + 1) * PAIR)
            mixed = jnp.where(one, out[low : low + UNIT, cols], out[high : high + UNIT, cols])
            att_ref[rows, g * wide + p * PAIR : g * wide + (p + 1) * PAIR] = mixed.astype(BF16)

    def stages(mixed=None, softened=None, scored=None):
        for g in range(groups):
            if mixed is not None:
                mix(mixed, g)
            if softened is not None:
                soften(softened, g)
            if scored is not None:
                score(scored, g)

    range_ref[...] = jnp.ones_like(range_ref)
    stages(scored=first)
    stages(softened=first, scored=first + 1)

    def one(unit, carry):
        stages(unit, unit + 1, unit + 2)
        return carry

    lax.fori_loop(first, last - 2, one, 0)
    stages(mixed=last - 2, softened=last - 1)
    stages(mixed=last - 1)
    fine = (jnp.min(range_ref[0]) >= SUM_LOW) & (jnp.max(range_ref[1]) <= SUM_HIGH)

    @pl.when(jnp.logical_not(fine))
    def _():
        def shifted(unit, carry):
            for g in range(groups):
                score(unit, g)
                soften(unit, g, shift=True)
                mix(unit, g)
            return carry

        lax.fori_loop(first, last, shifted, 0)


def edge_kernel(
    state_hbm, cond_hbm, ids_hbm, time_hbm, gain_hbm,
    cross_hbm, core_hbm, small_hbm,
    cross_ref, core_ref, small_ref, state_last, cond_last, state_first, cond_first, ids_ref, time_ref, gain_ref, sems,
):
    own = state_hbm.shape[0]
    copies = [
        pltpu.make_async_copy(source, target, sems.at[i])
        for i, (source, target) in enumerate(
            (
                (state_hbm.at[pl.ds(own - BEHIND, BEHIND)], state_last),
                (cond_hbm.at[pl.ds(own - BEHIND, BEHIND)], cond_last),
                (state_hbm.at[pl.ds(0, AHEAD)], state_first),
                (cond_hbm.at[pl.ds(0, AHEAD)], cond_first),
                (ids_hbm, ids_ref),
                (time_hbm, time_ref),
                (gain_hbm, gain_ref),
            )
        )
    ]
    for copy in copies:
        copy.start()
    even = lax.rem(lax.axis_index("seq"), 2) == 0
    for copy in copies:
        copy.wait()

    depth = core_ref.shape[1]

    def number_row(ids):
        blank = jnp.zeros((1, depth - ids.shape[1]), F32)
        return jnp.concatenate([(ids + 1).astype(F32), blank], axis=1)

    vectors = [ref[...].astype(F32).reshape(1, -1) for ref in (time_ref, gain_ref)]
    blank = jnp.zeros((SMALL - 3, depth), F32)
    small_ref[...] = jnp.concatenate([number_row(ids_ref[...]), *vectors, blank], axis=0).astype(BF16)
    leaving = [
        pltpu.make_async_copy(small_ref, small_hbm.at[pl.ds(0, SMALL)], sems.at[7]),
        pltpu.make_async_copy(cross_ref, cross_hbm, sems.at[8]),
        pltpu.make_async_copy(core_ref, core_hbm, sems.at[9]),
    ]
    leaving[0].start()

    def fill(ref, state, cond, ids):
        rows = state.shape[0]
        ref[0:rows, :] = (state[...].astype(F32) + cond[...].astype(F32)).astype(BF16)
        if rows < BEHIND:
            ref[rows:BEHIND, :] = jnp.zeros((BEHIND - rows, depth), BF16)
        ref[BEHIND:, :] = jnp.broadcast_to(number_row(ids), (PAYLOAD - BEHIND, depth)).astype(BF16)

    def fill_both(to_next, to_previous):
        fill(to_next, state_last, cond_last, ids_ref[:, own - BEHIND :])
        fill(to_previous, state_first, cond_first, ids_ref[:, :BEHIND])

    @pl.when(even)
    def _():
        fill_both(core_ref, cross_ref)

    @pl.when(jnp.logical_not(even))
    def _():
        fill_both(cross_ref, core_ref)

    leaving[1].start()
    leaving[2].start()
    for copy in leaving:
        copy.wait()


def own_kernel(
    small_hbm, state_hbm, cond_hbm, wqkv_hbm,
    small_ref, state_ref, cond_ref, q_ref, k_ref, v_ref, seg_ref, bias_ref,
    wk_ref, wv_ref, wq_ref, normed_ref, sems,
):
    own = state_ref.shape[0]
    copies = [
        pltpu.make_async_copy(state_hbm, state_ref, sems.at[0]),
        pltpu.make_async_copy(cond_hbm, cond_ref, sems.at[1]),
        pltpu.make_async_copy(small_hbm.at[pl.ds(0, SMALL)], small_ref, sems.at[5]),
    ]
    weights = [
        pltpu.make_async_copy(wqkv_hbm.at[which], w_ref, sems.at[2 + which])
        for which, w_ref in ((1, wk_ref), (2, wv_ref), (0, wq_ref))
    ]
    for copy in copies + weights[:1]:
        copy.start()
    copies[2].wait()
    gain = small_ref[2:3, :].astype(F32)
    own_segments(small_ref, seg_ref, own)
    build_masks((3, own // UNIT + 1), seg_ref, bias_ref)
    copies[0].wait()
    copies[1].wait()
    for copy in weights[1:]:
        copy.start()

    def one(i, carry):
        at = pl.ds(pl.multiple_of(i * UNIT, 16), UNIT)
        h = state_ref[at, :].astype(F32) + cond_ref[at, :].astype(F32)
        scale = lax.rsqrt(jnp.mean(h * h, axis=-1, keepdims=True) + 1e-06)
        normed_ref[at, :] = (h * scale * gain).astype(BF16)
        return carry

    lax.fori_loop(0, own // UNIT, one, 0)
    for w_ref, copy, out_ref in zip((wk_ref, wv_ref, wq_ref), weights, (k_ref, v_ref, q_ref)):
        copy.wait()
        project(normed_ref, w_ref, 0, own, out_ref, [(own, 0)])


def rest_kernel(
    cross_ref, core_ref, small_ref, state_ref, cond_ref, q_own, k_own, v_own, seg_own, bias_own,
    wqkv_hbm, wout_hbm,
    out_ref,
    wk_ref, wv_ref, wq_ref, wout, behind_ref, ahead_ref, halo_ref, h_ref,
    normed_ref, q_ref, k_ref, v_ref, att_ref, seg_ref, bias_ref, range_ref, sems, *group_refs,
):
    own = state_ref.shape[0]
    units = own // UNIT
    end = BEHIND + own
    total = end + AHEAD
    weights = [
        pltpu.make_async_copy(wqkv_hbm.at[which], w_ref, sems.at[which])
        for which, w_ref in ((1, wk_ref), (2, wv_ref), (0, wq_ref))
    ]
    wout_copy = pltpu.make_async_copy(wout_hbm, wout, sems.at[3])
    weights[0].start()
    half_time = 0.5 * small_ref[1:2, :].astype(F32)
    gain = small_ref[2:3, :].astype(F32)
    even = lax.rem(lax.axis_index("seq"), 2) == 0

    def take(before, after):
        behind_ref[...] = before[...]
        ahead_ref[...] = after[...]

    @pl.when(even)
    def _():
        take(cross_ref, core_ref)

    @pl.when(jnp.logical_not(even))
    def _():
        take(core_ref, cross_ref)

    seg_ref[BEHIND:end, :] = seg_own[BEHIND:end, :]
    edge_segments(behind_ref, ahead_ref, seg_ref)
    bias_ref[3 : units + 1] = bias_own[3 : units + 1]
    for unit in (1, 2, units + 1, units + 2):
        build_mask(unit, seg_ref, bias_ref)
    for ref, rows, place in ((behind_ref, BEHIND, 0), (ahead_ref, AHEAD, BEHIND)):
        h = ref[0:rows, :].astype(F32)
        scale = lax.rsqrt(jnp.mean(h * h, axis=-1, keepdims=True) + 1e-06)
        halo_ref[place : place + rows, :] = (h * scale * gain).astype(BF16)
    for ref, whole in ((q_ref, q_own), (k_ref, k_own), (v_ref, v_own)):
        ref[BEHIND:end, :] = whole[...]
    for copy in weights[1:] + [wout_copy]:
        copy.start()
    clear_spare((k_ref, v_ref))
    both = [(BEHIND, 0), (AHEAD, end)]
    edges = [(UNIT, UNIT), (AHEAD, end)]
    weights[0].wait()
    project(halo_ref, wk_ref, 0, BEHIND + AHEAD, k_ref, both)
    weights[1].wait()
    project(halo_ref, wv_ref, 0, BEHIND + AHEAD, v_ref, both)
    weights[2].wait()
    project(halo_ref, wq_ref, UNIT, BEHIND + AHEAD, q_ref, edges)
    attend(1, total // UNIT, q_ref, k_ref, v_ref, att_ref, bias_ref, range_ref, group_refs)
    wout_copy.wait()
    depth = wout.shape[1]
    for at in range(0, depth, TILE):
        cols = slice(at, at + TILE)
        moved = 0.5 * jnp.dot(att_ref[UNIT:total, :], wout[:, cols], preferred_element_type=F32)
        moved = moved + half_time[:, cols]
        h_ref[UNIT:BEHIND, cols] = behind_ref[UNIT:BEHIND, cols].astype(F32) + moved[:UNIT]
        h_ref[BEHIND:end, cols] = (
            state_ref[:, cols].astype(F32) + cond_ref[:, cols].astype(F32)
        ) + moved[UNIT : UNIT + own]
        h_ref[end:total, cols] = ahead_ref[0:AHEAD, cols].astype(F32) + moved[UNIT + own :]

    normalize(h_ref, normed_ref, gain, UNIT, total)
    project(normed_ref, wk_ref, UNIT, total, k_ref, [(total - UNIT, UNIT)])
    project(normed_ref, wv_ref, UNIT, total, v_ref, [(total - UNIT, UNIT)])
    project(normed_ref, wq_ref, BEHIND, end, q_ref, [(own, BEHIND)])
    attend(
        BEHIND // UNIT, end // UNIT, q_ref, k_ref, v_ref, att_ref, bias_ref, range_ref, group_refs
    )
    for at in range(0, depth, TILE):
        cols = slice(at, at + TILE)
        moved = jnp.dot(att_ref[BEHIND:end, :], wout[:, cols], preferred_element_type=F32)
        x = h_ref[BEHIND:end, cols] - cond_ref[:, cols].astype(F32) - half_time[:, cols]
        out_ref[:, cols] = (x + 0.5 * moved).astype(BF16)


def clear_spare(refs):
    for ref in refs:
        ref[ref.shape[0] - SPARE :, :] = jnp.zeros((SPARE, ref.shape[1]), ref.dtype)


def one_step(
    final, h_ref, small_ref, behind_ref, ahead_ref, wqkv, wout,
    out_ref,
    normed_ref, q_ref, k_ref, v_ref, att_ref, seg_ref, bias_ref, range_ref, *group_refs,
):
    total = h_ref.shape[0]
    own = total - BEHIND - AHEAD
    kv_first = UNIT if final else 0
    first, last = (BEHIND, BEHIND + own) if final else (UNIT, total)
    own_segments(small_ref, seg_ref, own)
    edge_segments(behind_ref, ahead_ref, seg_ref)
    build_masks((1, total // UNIT), seg_ref, bias_ref)
    clear_spare((k_ref, v_ref))
    normalize(h_ref, normed_ref, small_ref[2:3, :].astype(F32), kv_first, total)
    project(normed_ref, wqkv.at[1], kv_first, total, k_ref, [(total - kv_first, kv_first)])
    project(normed_ref, wqkv.at[2], kv_first, total, v_ref, [(total - kv_first, kv_first)])
    project(normed_ref, wqkv.at[0], first, last, q_ref, [(last - first, first)])
    attend(
        first // UNIT, last // UNIT,
        q_ref, k_ref, v_ref, att_ref, bias_ref, range_ref, group_refs,
    )
    for at in range(0, wout.shape[1], TILE):
        cols = slice(at, at + TILE)
        out_ref[:, cols] = jnp.dot(
            att_ref[first:last, :], wout[:, cols], preferred_element_type=F32
        ).astype(BF16)


def shards(state, condition, time_vector, norm_gain, w_qkv, w_out, utterance_ids):
    own, depth = state.shape
    width = w_qkv.shape[2]
    total = BEHIND + own + AHEAD
    parts = lax.axis_size("mp")
    count = lax.axis_size("seq")
    ids = utterance_ids.reshape(1, own)
    vmem = pl.BlockSpec(memory_space=pltpu.VMEM)
    hbm = pl.BlockSpec(memory_space=pltpu.HBM)

    def limit(mib):
        return pltpu.CompilerParams(vmem_limit_bytes=int(mib * 2**20))

    cross, core, small = pl.pallas_call(
        edge_kernel,
        out_shape=[jax.ShapeDtypeStruct((rows, depth), BF16) for rows in (PAYLOAD, PAYLOAD, 2 * own)],
        in_specs=[hbm] * 5,
        out_specs=[hbm] * 3,
        scratch_shapes=[pltpu.VMEM((PAYLOAD, depth), BF16)] * 2
        + [pltpu.VMEM((SMALL, depth), BF16)]
        + [pltpu.VMEM((BEHIND, depth), BF16)] * 2
        + [pltpu.VMEM((AHEAD, depth), BF16)] * 2
        + [pltpu.VMEM((1, own), jnp.int32)]
        + [pltpu.VMEM((depth,), BF16)] * 2
        + [pltpu.SemaphoreType.DMA((10,))],
        compiler_params=limit(EDGE_LIMIT),
    )(state, condition, ids, time_vector, norm_gain)
    ends = [(i, i + 1) for i in range(1, count - 1, 2)]
    cross = lax.ppermute(cross, "seq", ends + [(j, i) for i, j in ends])
    ends = [(i, i + 1) for i in range(0, count - 1, 2)]
    core = lax.ppermute(core, "seq", ends + [(j, i) for i, j in ends])

    work = [((total, depth), BF16), ((total, width), BF16)]
    work += [((total + SPARE, width), BF16)] * 2
    work += [
        ((total, width), BF16),
        ((total + SPARE, 128), F32),
        ((total // UNIT, UNIT, WINDOW), F32),
        ((2, UNIT, PAIR), F32),
    ]
    groups = [((FOUR * UNIT, WINDOW), kind) for kind in (F32, BF16) for _ in range(width // (FOUR * HEAD_DIM))]
    groups = [pltpu.VMEM(*one) for one in groups]
    if parts == 1:
        kept = [((SMALL, depth), BF16)] + [(state.shape, BF16)] * 2 + [((own, width), BF16)] * 3
        kept += [((total + SPARE, 128), F32), ((total // UNIT, UNIT, WINDOW), F32)]
        kept = pl.pallas_call(
            own_kernel,
            out_shape=[jax.ShapeDtypeStruct(*one) for one in kept],
            in_specs=[hbm] * 4,
            out_specs=[vmem] * 8,
            scratch_shapes=[pltpu.VMEM((depth, width), BF16)] * 3
            + [pltpu.VMEM((own, depth), BF16), pltpu.SemaphoreType.DMA((6,))],
            compiler_params=limit(OWN_LIMIT),
            cost_estimate=pl.CostEstimate(
                flops=6 * own * depth * width, bytes_accessed=2 * 4 * depth * width, transcendentals=0
            ),
        )(small, state, condition, w_qkv)
        first = [((depth, width), BF16)] * 3 + [(w_out.shape, BF16)] + [((PAYLOAD, depth), BF16)] * 2
        first += [((BEHIND + AHEAD, depth), BF16), ((total, depth), F32)]
        return pl.pallas_call(
            rest_kernel,
            out_shape=jax.ShapeDtypeStruct((own, depth), BF16),
            in_specs=[vmem] * 10 + [hbm] * 2,
            out_specs=vmem,
            scratch_shapes=[pltpu.VMEM(*one) for one in first + work]
            + [pltpu.SemaphoreType.DMA((4,))]
            + groups,
            compiler_params=limit(LIMIT),
        )(cross, core, *kept, w_qkv, w_out)

    even = lax.axis_index("seq") % 2 == 0
    small = small[:SMALL]
    behind = jnp.where(even, cross, core)
    ahead = jnp.where(even, core, cross)

    def terms(h, final):
        rows = own if final else total - UNIT
        mine = pl.pallas_call(
            functools.partial(one_step, final),
            out_shape=jax.ShapeDtypeStruct((rows, depth), BF16),
            in_specs=[vmem] * 6,
            out_specs=vmem,
            scratch_shapes=[pltpu.VMEM(*one) for one in work] + groups,
            compiler_params=limit(LIMIT),
        )(h, small, behind, ahead, w_qkv, w_out)
        return lax.psum(mine, "mp").astype(F32)

    start = state.astype(F32)
    h = jnp.concatenate(
        [behind[:BEHIND].astype(F32), start + condition.astype(F32), ahead[:AHEAD].astype(F32)]
    )
    velocity = terms(h, False)
    later = jnp.pad(velocity, ((UNIT, 0), (0, 0))) * 0.5 + 0.5 * time_vector.astype(F32)
    x = start + 0.5 * velocity[UNIT : UNIT + own] + 0.5 * terms(h + later, True)
    share = depth // parts
    mine = lax.dynamic_slice_in_dim(x, lax.axis_index("mp") * share, share, 1)
    return mine.astype(BF16)


def solution(mesh):
    in_specs = (
        P("seq", None),
        P("seq", None),
        P(),
        P(),
        P(None, None, "mp"),
        P("mp", None),
        P("seq"),
    )
    out_specs = P("seq", "mp")
    return jax.shard_map(shards, mesh=mesh, in_specs=in_specs, out_specs=out_specs, check_vma=False)
```

```python
import functools
import math

import jax
import jax.numpy as jnp
from jax import lax
from jax.experimental import pallas as pl
from jax.experimental.pallas import tpu as pltpu
from jax.sharding import PartitionSpec as P

HEAD_DIM = 64
BLOCK = 24
UNIT = 2 * BLOCK
BEHIND = 4 * BLOCK
AHEAD = 2 * BLOCK
WINDOW = 128
SPARE = WINDOW - 2 * UNIT
PAIR = 2 * HEAD_DIM
FOUR = 4
SUM_LOW, SUM_HIGH = 2.0**-60, 2.0**100
SMALL = 16
PAYLOAD = BEHIND + 16
TILE = 256
ROWS = 16
EDGE_LIMIT, OWN_LIMIT, LIMIT = 56, 48, 48
F32 = jnp.float32
BF16 = jnp.bfloat16
NEG = -1e30


def column_of(row):
    n = row.shape[1]
    same = lax.broadcasted_iota(jnp.int32, (n, n), 0) == lax.broadcasted_iota(jnp.int32, (n, n), 1)
    column = jnp.sum(jnp.where(same, row, 0.0), axis=1, keepdims=True)
    return jnp.broadcast_to(column, (n, 128))


def own_segments(small_ref, seg_ref, own):
    for at in range(0, own, 128):
        n = min(128, own - at)
        row = small_ref[0:1, at : at + n].astype(F32)
        seg_ref[BEHIND + at : BEHIND + at + n, :] = column_of(row)


def edge_segments(behind_ref, ahead_ref, seg_ref):
    end = seg_ref.shape[0] - SPARE
    seg_ref[0:BEHIND, :] = column_of(behind_ref[BEHIND : BEHIND + 1, 0:BEHIND].astype(F32))
    seg_ref[end - AHEAD : end, :] = column_of(ahead_ref[BEHIND : BEHIND + 1, 0:AHEAD].astype(F32))
    seg_ref[end : end + SPARE, :] = jnp.full((SPARE, 128), -1.0, F32)


def build_mask(unit, seg_ref, bias_ref):
    start = unit * UNIT
    if not isinstance(unit, int):
        start = pl.multiple_of(start, 16)
    window = seg_ref[pl.ds(start - UNIT, WINDOW), :]
    r = lax.broadcasted_iota(jnp.int32, (WINDOW, WINDOW), 0)
    c = lax.broadcasted_iota(jnp.int32, (WINDOW, WINDOW), 1)
    keys = jnp.sum(jnp.where(r == c, window, 0.0), axis=0, keepdims=True)
    queries = seg_ref[pl.ds(start, UNIT), :]
    row = lax.broadcasted_iota(jnp.int32, (UNIT, WINDOW), 0)
    col = lax.broadcasted_iota(jnp.int32, (UNIT, WINDOW), 1)
    first = jnp.where(row < BLOCK, 0, BLOCK)
    band = (col >= first) & (col < first + 4 * BLOCK)
    bias_ref[unit] = jnp.where(band & (queries == keys), 0.0, NEG)


def build_masks(units, seg_ref, bias_ref):
    for unit in range(*units):
        build_mask(unit, seg_ref, bias_ref)


def normalize(load, normed_ref, gain, first, last):
    groups = (last - first) // ROWS
    many = max(n for n in range(1, 13) if groups % n == 0)

    def one(i, carry):
        for j in range(many):
            at = pl.ds(pl.multiple_of(first + (i * many + j) * ROWS, ROWS), ROWS)
            h = load(at)
            scale = lax.rsqrt(jnp.mean(h * h, axis=-1, keepdims=True) + 1e-06)
            normed_ref[at, :] = (h * scale * gain).astype(BF16)
        return carry

    lax.fori_loop(0, groups // many, one, 0)


def project(normed_ref, w_ref, first, last, out_ref, places):
    width = w_ref.shape[1]
    tile = min(TILE, width)
    for at in range(0, width, tile):
        cols = slice(at, at + tile)
        out = jnp.dot(
            normed_ref[first:last, :], w_ref[:, cols], preferred_element_type=F32
        ).astype(BF16)
        done = 0
        for rows, place in places:
            out_ref[place : place + rows, cols] = out[done : done + rows]
            done += rows


def attend(first, last, q_ref, k_ref, v_ref, att_ref, bias_ref, range_ref, group_refs):
    wide = FOUR * HEAD_DIM
    groups = q_ref.shape[1] // wide
    factor = HEAD_DIM**-0.5 * math.log2(math.e)

    def at(unit):
        start = pl.multiple_of(unit * UNIT, 16)
        return pl.ds(start, UNIT), pl.ds(pl.multiple_of(start - UNIT, 16), WINDOW)

    score_refs, prob_refs = group_refs[:groups], group_refs[groups:]

    def score(unit, g):
        rows, window = at(unit)
        head = lax.broadcasted_iota(jnp.int32, (UNIT, wide), 1) // HEAD_DIM
        lanes = slice(g * wide, (g + 1) * wide)
        q = q_ref[rows, lanes]
        zero = jnp.zeros_like(q)
        stacked = jnp.concatenate([jnp.where(head == j, q, zero) for j in range(FOUR)], axis=0)
        score_refs[g][...] = lax.dot_general(
            stacked, k_ref[window, lanes], (((1,), (1,)), ((), ())), preferred_element_type=F32
        )

    def soften(unit, g, shift=False):
        bias = bias_ref[unit]
        low, high = range_ref[0], range_ref[1]
        for j in range(FOUR):
            rows = slice(j * UNIT, (j + 1) * UNIT)
            s = score_refs[g][rows, :] * factor + bias
            if shift:
                s = s - jnp.max(s, axis=-1, keepdims=True)
            expo = jnp.exp2(s)
            total = jnp.sum(expo, axis=-1, keepdims=True)
            low, high = jnp.minimum(low, total), jnp.maximum(high, total)
            prob_refs[g][rows, :] = (expo * pl.reciprocal(total, approx=True)).astype(BF16)
        range_ref[0] = low
        range_ref[1] = high

    def mix(unit, g):
        rows, window = at(unit)
        one = lax.broadcasted_iota(jnp.int32, (UNIT, PAIR), 1) < HEAD_DIM
        lanes = slice(g * wide, (g + 1) * wide)
        out = jnp.dot(prob_refs[g][...], v_ref[window, lanes], preferred_element_type=F32)
        for p in range(FOUR // 2):
            low, high = 2 * p * UNIT, (2 * p + 1) * UNIT
            cols = slice(p * PAIR, (p + 1) * PAIR)
            mixed = jnp.where(one, out[low : low + UNIT, cols], out[high : high + UNIT, cols])
            att_ref[rows, g * wide + p * PAIR : g * wide + (p + 1) * PAIR] = mixed.astype(BF16)

    def stages(mixed=None, softened=None, scored=None):
        for g in range(groups):
            if mixed is not None:
                mix(mixed, g)
            if softened is not None:
                soften(softened, g)
            if scored is not None:
                score(scored, g)

    range_ref[...] = jnp.ones_like(range_ref)
    stages(scored=first)
    stages(softened=first, scored=first + 1)

    def two(i, carry):
        unit = first + 2 * i
        stages(unit, unit + 1, unit + 2)
        stages(unit + 1, unit + 2, unit + 3)
        return carry

    passes = (last - 2 - first) // 2
    lax.fori_loop(0, passes, two, 0)
    if first + 2 * passes < last - 2:
        stages(last - 3, last - 2, last - 1)
    stages(mixed=last - 2, softened=last - 1)
    stages(mixed=last - 1)
    fine = (jnp.min(range_ref[0]) >= SUM_LOW) & (jnp.max(range_ref[1]) <= SUM_HIGH)

    @pl.when(jnp.logical_not(fine))
    def _():
        def shifted(unit, carry):
            for g in range(groups):
                score(unit, g)
                soften(unit, g, shift=True)
                mix(unit, g)
            return carry

        lax.fori_loop(first, last, shifted, 0)


def edge_kernel(
    state_hbm, cond_hbm, ids_hbm, time_hbm, gain_hbm,
    cross_hbm, core_hbm, small_hbm,
    cross_ref, core_ref, small_ref, state_last, cond_last, state_first, cond_first, ids_ref, time_ref, gain_ref, sems,
):
    own = state_hbm.shape[0]
    copies = [
        pltpu.make_async_copy(source, target, sems.at[i])
        for i, (source, target) in enumerate(
            (
                (state_hbm.at[pl.ds(own - BEHIND, BEHIND)], state_last),
                (cond_hbm.at[pl.ds(own - BEHIND, BEHIND)], cond_last),
                (state_hbm.at[pl.ds(0, AHEAD)], state_first),
                (cond_hbm.at[pl.ds(0, AHEAD)], cond_first),
                (ids_hbm, ids_ref),
                (time_hbm, time_ref),
                (gain_hbm, gain_ref),
            )
        )
    ]
    for copy in copies:
        copy.start()
    even = lax.rem(lax.axis_index("seq"), 2) == 0
    for copy in copies:
        copy.wait()

    depth = core_ref.shape[1]

    def number_row(ids):
        blank = jnp.zeros((1, depth - ids.shape[1]), F32)
        return jnp.concatenate([(ids + 1).astype(F32), blank], axis=1)

    vectors = [ref[...].astype(F32).reshape(1, -1) for ref in (time_ref, gain_ref)]
    blank = jnp.zeros((SMALL - 3, depth), F32)
    small_ref[...] = jnp.concatenate([number_row(ids_ref[...]), *vectors, blank], axis=0).astype(BF16)
    leaving = [
        pltpu.make_async_copy(small_ref, small_hbm.at[pl.ds(0, SMALL)], sems.at[7]),
        pltpu.make_async_copy(cross_ref, cross_hbm, sems.at[8]),
        pltpu.make_async_copy(core_ref, core_hbm, sems.at[9]),
    ]
    leaving[0].start()

    def fill(ref, state, cond, ids):
        rows = state.shape[0]
        ref[0:rows, :] = (state[...].astype(F32) + cond[...].astype(F32)).astype(BF16)
        if rows < BEHIND:
            ref[rows:BEHIND, :] = jnp.zeros((BEHIND - rows, depth), BF16)
        ref[BEHIND:, :] = jnp.broadcast_to(number_row(ids), (PAYLOAD - BEHIND, depth)).astype(BF16)

    def fill_both(to_next, to_previous):
        fill(to_next, state_last, cond_last, ids_ref[:, own - BEHIND :])
        fill(to_previous, state_first, cond_first, ids_ref[:, :BEHIND])

    @pl.when(even)
    def _():
        fill_both(core_ref, cross_ref)

    @pl.when(jnp.logical_not(even))
    def _():
        fill_both(cross_ref, core_ref)

    leaving[1].start()
    leaving[2].start()
    for copy in leaving:
        copy.wait()


def own_kernel(
    small_hbm, state_hbm, cond_hbm, wqkv_hbm,
    small_ref, state_ref, cond_ref, q_ref, k_ref, v_ref, seg_ref, bias_ref,
    wk_ref, wv_ref, wq_ref, normed_ref, sems,
):
    own = state_ref.shape[0]
    copies = [
        pltpu.make_async_copy(state_hbm, state_ref, sems.at[0]),
        pltpu.make_async_copy(cond_hbm, cond_ref, sems.at[1]),
        pltpu.make_async_copy(small_hbm.at[pl.ds(0, SMALL)], small_ref, sems.at[5]),
    ]
    weights = [
        pltpu.make_async_copy(wqkv_hbm.at[which], w_ref, sems.at[2 + which])
        for which, w_ref in ((1, wk_ref), (2, wv_ref), (0, wq_ref))
    ]
    for copy in copies + weights[:1]:
        copy.start()
    copies[2].wait()
    gain = small_ref[2:3, :].astype(F32)
    own_segments(small_ref, seg_ref, own)
    build_masks((3, own // UNIT + 1), seg_ref, bias_ref)
    copies[0].wait()
    copies[1].wait()
    for copy in weights[1:]:
        copy.start()

    def hidden(at):
        return state_ref[at, :].astype(F32) + cond_ref[at, :].astype(F32)

    normalize(hidden, normed_ref, gain, 0, own)
    for w_ref, copy, out_ref in zip((wk_ref, wv_ref, wq_ref), weights, (k_ref, v_ref, q_ref)):
        copy.wait()
        project(normed_ref, w_ref, 0, own, out_ref, [(own, 0)])


def rest_kernel(
    cross_ref, core_ref, small_ref, state_ref, cond_ref, q_own, k_own, v_own, seg_own, bias_own,
    wqkv_hbm, wout_hbm,
    out_ref,
    wk_ref, wv_ref, wq_ref, wout, behind_ref, ahead_ref, halo_ref, h_ref,
    normed_ref, q_ref, k_ref, v_ref, att_ref, seg_ref, bias_ref, range_ref, sems, *group_refs,
):
    own = state_ref.shape[0]
    units = own // UNIT
    end = BEHIND + own
    total = end + AHEAD
    weights = [
        pltpu.make_async_copy(wqkv_hbm.at[which], w_ref, sems.at[which])
        for which, w_ref in ((1, wk_ref), (2, wv_ref), (0, wq_ref))
    ]
    wout_copy = pltpu.make_async_copy(wout_hbm, wout, sems.at[3])
    weights[0].start()
    half_time = 0.5 * small_ref[1:2, :].astype(F32)
    gain = small_ref[2:3, :].astype(F32)
    even = lax.rem(lax.axis_index("seq"), 2) == 0

    def take(before, after):
        behind_ref[...] = before[...]
        ahead_ref[...] = after[...]

    @pl.when(even)
    def _():
        take(cross_ref, core_ref)

    @pl.when(jnp.logical_not(even))
    def _():
        take(core_ref, cross_ref)

    seg_ref[BEHIND:end, :] = seg_own[BEHIND:end, :]
    edge_segments(behind_ref, ahead_ref, seg_ref)
    bias_ref[3 : units + 1] = bias_own[3 : units + 1]
    for unit in (1, 2, units + 1, units + 2):
        build_mask(unit, seg_ref, bias_ref)
    for ref, rows, place in ((behind_ref, BEHIND, 0), (ahead_ref, AHEAD, BEHIND)):
        h = ref[0:rows, :].astype(F32)
        scale = lax.rsqrt(jnp.mean(h * h, axis=-1, keepdims=True) + 1e-06)
        halo_ref[place : place + rows, :] = (h * scale * gain).astype(BF16)
    for ref, whole in ((q_ref, q_own), (k_ref, k_own), (v_ref, v_own)):
        ref[BEHIND:end, :] = whole[...]
    for copy in weights[1:] + [wout_copy]:
        copy.start()
    clear_spare((k_ref, v_ref))
    both = [(BEHIND, 0), (AHEAD, end)]
    edges = [(UNIT, UNIT), (AHEAD, end)]
    weights[0].wait()
    project(halo_ref, wk_ref, 0, BEHIND + AHEAD, k_ref, both)
    weights[1].wait()
    project(halo_ref, wv_ref, 0, BEHIND + AHEAD, v_ref, both)
    weights[2].wait()
    project(halo_ref, wq_ref, UNIT, BEHIND + AHEAD, q_ref, edges)
    attend(1, total // UNIT, q_ref, k_ref, v_ref, att_ref, bias_ref, range_ref, group_refs)
    wout_copy.wait()
    depth = wout.shape[1]
    for at in range(0, depth, TILE):
        cols = slice(at, at + TILE)
        moved = 0.5 * jnp.dot(att_ref[UNIT:total, :], wout[:, cols], preferred_element_type=F32)
        moved = moved + half_time[:, cols]
        h_ref[UNIT:BEHIND, cols] = behind_ref[UNIT:BEHIND, cols].astype(F32) + moved[:UNIT]
        h_ref[BEHIND:end, cols] = (
            state_ref[:, cols].astype(F32) + cond_ref[:, cols].astype(F32)
        ) + moved[UNIT : UNIT + own]
        h_ref[end:total, cols] = ahead_ref[0:AHEAD, cols].astype(F32) + moved[UNIT + own :]

    normalize(lambda at: h_ref[at, :], normed_ref, gain, UNIT, total)
    project(normed_ref, wk_ref, UNIT, total, k_ref, [(total - UNIT, UNIT)])
    project(normed_ref, wv_ref, UNIT, total, v_ref, [(total - UNIT, UNIT)])
    project(normed_ref, wq_ref, BEHIND, end, q_ref, [(own, BEHIND)])
    attend(
        BEHIND // UNIT, end // UNIT, q_ref, k_ref, v_ref, att_ref, bias_ref, range_ref, group_refs
    )
    for at in range(0, depth, TILE):
        cols = slice(at, at + TILE)
        moved = jnp.dot(att_ref[BEHIND:end, :], wout[:, cols], preferred_element_type=F32)
        x = h_ref[BEHIND:end, cols] - cond_ref[:, cols].astype(F32) - half_time[:, cols]
        out_ref[:, cols] = (x + 0.5 * moved).astype(BF16)


def clear_spare(refs):
    for ref in refs:
        ref[ref.shape[0] - SPARE :, :] = jnp.zeros((SPARE, ref.shape[1]), ref.dtype)


def one_step(
    final, h_ref, small_ref, behind_ref, ahead_ref, wqkv, wout,
    out_ref,
    normed_ref, q_ref, k_ref, v_ref, att_ref, seg_ref, bias_ref, range_ref, *group_refs,
):
    total = h_ref.shape[0]
    own = total - BEHIND - AHEAD
    kv_first = UNIT if final else 0
    first, last = (BEHIND, BEHIND + own) if final else (UNIT, total)
    own_segments(small_ref, seg_ref, own)
    edge_segments(behind_ref, ahead_ref, seg_ref)
    build_masks((1, total // UNIT), seg_ref, bias_ref)
    clear_spare((k_ref, v_ref))
    gain = small_ref[2:3, :].astype(F32)
    normalize(lambda at: h_ref[at, :], normed_ref, gain, kv_first, total)
    project(normed_ref, wqkv.at[1], kv_first, total, k_ref, [(total - kv_first, kv_first)])
    project(normed_ref, wqkv.at[2], kv_first, total, v_ref, [(total - kv_first, kv_first)])
    project(normed_ref, wqkv.at[0], first, last, q_ref, [(last - first, first)])
    attend(
        first // UNIT, last // UNIT,
        q_ref, k_ref, v_ref, att_ref, bias_ref, range_ref, group_refs,
    )
    for at in range(0, wout.shape[1], TILE):
        cols = slice(at, at + TILE)
        out_ref[:, cols] = jnp.dot(
            att_ref[first:last, :], wout[:, cols], preferred_element_type=F32
        ).astype(BF16)


def shards(state, condition, time_vector, norm_gain, w_qkv, w_out, utterance_ids):
    own, depth = state.shape
    width = w_qkv.shape[2]
    total = BEHIND + own + AHEAD
    parts = lax.axis_size("mp")
    count = lax.axis_size("seq")
    ids = utterance_ids.reshape(1, own)
    vmem = pl.BlockSpec(memory_space=pltpu.VMEM)
    hbm = pl.BlockSpec(memory_space=pltpu.HBM)

    def limit(mib):
        return pltpu.CompilerParams(vmem_limit_bytes=int(mib * 2**20))

    cross, core, small = pl.pallas_call(
        edge_kernel,
        out_shape=[jax.ShapeDtypeStruct((rows, depth), BF16) for rows in (PAYLOAD, PAYLOAD, 2 * own)],
        in_specs=[hbm] * 5,
        out_specs=[hbm] * 3,
        scratch_shapes=[pltpu.VMEM((PAYLOAD, depth), BF16)] * 2
        + [pltpu.VMEM((SMALL, depth), BF16)]
        + [pltpu.VMEM((BEHIND, depth), BF16)] * 2
        + [pltpu.VMEM((AHEAD, depth), BF16)] * 2
        + [pltpu.VMEM((1, own), jnp.int32)]
        + [pltpu.VMEM((depth,), BF16)] * 2
        + [pltpu.SemaphoreType.DMA((10,))],
        compiler_params=limit(EDGE_LIMIT),
    )(state, condition, ids, time_vector, norm_gain)
    ends = [(i, i + 1) for i in range(1, count - 1, 2)]
    cross = lax.ppermute(cross, "seq", ends + [(j, i) for i, j in ends])
    ends = [(i, i + 1) for i in range(0, count - 1, 2)]
    core = lax.ppermute(core, "seq", ends + [(j, i) for i, j in ends])

    work = [((total, depth), BF16), ((total, width), BF16)]
    work += [((total + SPARE, width), BF16)] * 2
    work += [
        ((total, width), BF16),
        ((total + SPARE, 128), F32),
        ((total // UNIT, UNIT, WINDOW), F32),
        ((2, UNIT, PAIR), F32),
    ]
    groups = [((FOUR * UNIT, WINDOW), kind) for kind in (F32, BF16) for _ in range(width // (FOUR * HEAD_DIM))]
    groups = [pltpu.VMEM(*one) for one in groups]
    if parts == 1:
        kept = [((SMALL, depth), BF16)] + [(state.shape, BF16)] * 2 + [((own, width), BF16)] * 3
        kept += [((total + SPARE, 128), F32), ((total // UNIT, UNIT, WINDOW), F32)]
        kept = pl.pallas_call(
            own_kernel,
            out_shape=[jax.ShapeDtypeStruct(*one) for one in kept],
            in_specs=[hbm] * 4,
            out_specs=[vmem] * 8,
            scratch_shapes=[pltpu.VMEM((depth, width), BF16)] * 3
            + [pltpu.VMEM((own, depth), BF16), pltpu.SemaphoreType.DMA((6,))],
            compiler_params=limit(OWN_LIMIT),
            cost_estimate=pl.CostEstimate(
                flops=6 * own * depth * width, bytes_accessed=2 * 4 * depth * width, transcendentals=0
            ),
        )(small, state, condition, w_qkv)
        first = [((depth, width), BF16)] * 3 + [(w_out.shape, BF16)] + [((PAYLOAD, depth), BF16)] * 2
        first += [((BEHIND + AHEAD, depth), BF16), ((total, depth), F32)]
        return pl.pallas_call(
            rest_kernel,
            out_shape=jax.ShapeDtypeStruct((own, depth), BF16),
            in_specs=[vmem] * 10 + [hbm] * 2,
            out_specs=vmem,
            scratch_shapes=[pltpu.VMEM(*one) for one in first + work]
            + [pltpu.SemaphoreType.DMA((4,))]
            + groups,
            compiler_params=limit(LIMIT),
        )(cross, core, *kept, w_qkv, w_out)

    even = lax.axis_index("seq") % 2 == 0
    small = small[:SMALL]
    behind = jnp.where(even, cross, core)
    ahead = jnp.where(even, core, cross)

    def terms(h, final):
        rows = own if final else total - UNIT
        mine = pl.pallas_call(
            functools.partial(one_step, final),
            out_shape=jax.ShapeDtypeStruct((rows, depth), BF16),
            in_specs=[vmem] * 6,
            out_specs=vmem,
            scratch_shapes=[pltpu.VMEM(*one) for one in work] + groups,
            compiler_params=limit(LIMIT),
        )(h, small, behind, ahead, w_qkv, w_out)
        return lax.psum(mine, "mp").astype(F32)

    start = state.astype(F32)
    h = jnp.concatenate(
        [behind[:BEHIND].astype(F32), start + condition.astype(F32), ahead[:AHEAD].astype(F32)]
    )
    velocity = terms(h, False)
    later = jnp.pad(velocity, ((UNIT, 0), (0, 0))) * 0.5 + 0.5 * time_vector.astype(F32)
    x = start + 0.5 * velocity[UNIT : UNIT + own] + 0.5 * terms(h + later, True)
    share = depth // parts
    mine = lax.dynamic_slice_in_dim(x, lax.axis_index("mp") * share, share, 1)
    return mine.astype(BF16)


def solution(mesh):
    in_specs = (
        P("seq", None),
        P("seq", None),
        P(),
        P(),
        P(None, None, "mp"),
        P("mp", None),
        P("seq"),
    )
    out_specs = P("seq", "mp")
    return jax.shard_map(shards, mesh=mesh, in_specs=in_specs, out_specs=out_specs, check_vma=False)
```

```python
import functools
import math

import jax
import jax.numpy as jnp
from jax import lax
from jax.experimental import pallas as pl
from jax.experimental.pallas import tpu as pltpu
from jax.sharding import PartitionSpec as P

HEAD_DIM = 64
BLOCK = 24
UNIT = 2 * BLOCK
BEHIND = 4 * BLOCK
AHEAD = 2 * BLOCK
WINDOW = 128
SPARE = WINDOW - 2 * UNIT
EDGE = UNIT + WINDOW
PAIR = 2 * HEAD_DIM
MANY = 6
FOUR = 4
SUM_LOW, SUM_HIGH = 2.0**-60, 2.0**100
SMALL = 16
PAYLOAD = BEHIND + 16
TILE = 256
ROWS = 16
EDGE_LIMIT, OWN_LIMIT, LIMIT = 56, 48, 48
F32 = jnp.float32
BF16 = jnp.bfloat16
NEG = -1e30


def column_of(row):
    n = row.shape[1]
    same = lax.broadcasted_iota(jnp.int32, (n, n), 0) == lax.broadcasted_iota(jnp.int32, (n, n), 1)
    column = jnp.sum(jnp.where(same, row, 0.0), axis=1, keepdims=True)
    return jnp.broadcast_to(column, (n, 128))


def own_segments(small_ref, seg_ref, own):
    for at in range(0, own, 128):
        n = min(128, own - at)
        row = small_ref[0:1, at : at + n].astype(F32)
        seg_ref[BEHIND + at : BEHIND + at + n, :] = column_of(row)


def edge_segments(behind_ref, ahead_ref, seg_ref):
    end = seg_ref.shape[0] - SPARE
    seg_ref[0:BEHIND, :] = column_of(behind_ref[BEHIND : BEHIND + 1, 0:BEHIND].astype(F32))
    seg_ref[end - AHEAD : end, :] = column_of(ahead_ref[BEHIND : BEHIND + 1, 0:AHEAD].astype(F32))
    seg_ref[end : end + SPARE, :] = jnp.full((SPARE, 128), -1.0, F32)


def build_mask(unit, seg_ref, bias_ref):
    start = unit * UNIT
    if not isinstance(unit, int):
        start = pl.multiple_of(start, 16)
    window = seg_ref[pl.ds(start - UNIT, WINDOW), :]
    r = lax.broadcasted_iota(jnp.int32, (WINDOW, WINDOW), 0)
    c = lax.broadcasted_iota(jnp.int32, (WINDOW, WINDOW), 1)
    keys = jnp.sum(jnp.where(r == c, window, 0.0), axis=0, keepdims=True)
    queries = seg_ref[pl.ds(start, UNIT), :]
    row = lax.broadcasted_iota(jnp.int32, (UNIT, WINDOW), 0)
    col = lax.broadcasted_iota(jnp.int32, (UNIT, WINDOW), 1)
    first = jnp.where(row < BLOCK, 0, BLOCK)
    band = (col >= first) & (col < first + 4 * BLOCK)
    bias_ref[unit] = jnp.where(band & (queries == keys), 0.0, NEG)


def build_masks(units, seg_ref, bias_ref):
    for unit in range(*units):
        build_mask(unit, seg_ref, bias_ref)


def normalize(load, normed_ref, gain, first, last):
    groups = (last - first) // ROWS
    many = max(n for n in range(1, 13) if groups % n == 0)

    def one(i, carry):
        for j in range(many):
            at = pl.ds(pl.multiple_of(first + (i * many + j) * ROWS, ROWS), ROWS)
            h = load(at)
            scale = lax.rsqrt(jnp.mean(h * h, axis=-1, keepdims=True) + 1e-06)
            normed_ref[at, :] = (h * scale * gain).astype(BF16)
        return carry

    lax.fori_loop(0, groups // many, one, 0)


def project(normed_ref, w_ref, first, last, out_ref, places):
    width = w_ref.shape[1]
    tile = min(TILE, width)
    for at in range(0, width, tile):
        cols = slice(at, at + tile)
        out = jnp.dot(
            normed_ref[first:last, :], w_ref[:, cols], preferred_element_type=F32
        ).astype(BF16)
        done = 0
        for rows, place in places:
            out_ref[place : place + rows, cols] = out[done : done + rows]
            done += rows


def attend(count, place, q_ref, k_ref, v_ref, att_ref, bias_ref, range_ref, group_refs):
    wide = FOUR * HEAD_DIM
    groups = q_ref.shape[1] // wide
    factor = HEAD_DIM**-0.5 * math.log2(math.e)

    def row(start):
        return start if isinstance(start, int) else pl.multiple_of(start, 16)

    score_refs, prob_refs = group_refs[:groups], group_refs[groups:]

    def score(i, g):
        _, q_row, kv_row, _ = place(i)
        rows, window = pl.ds(row(q_row), UNIT), pl.ds(row(kv_row), WINDOW)
        head = lax.broadcasted_iota(jnp.int32, (UNIT, wide), 1) // HEAD_DIM
        lanes = slice(g * wide, (g + 1) * wide)
        q = q_ref[rows, lanes]
        zero = jnp.zeros_like(q)
        stacked = jnp.concatenate([jnp.where(head == j, q, zero) for j in range(FOUR)], axis=0)
        score_refs[g][...] = lax.dot_general(
            stacked, k_ref[window, lanes], (((1,), (1,)), ((), ())), preferred_element_type=F32
        )

    def soften(i, g, shift=False):
        bias = bias_ref[place(i)[0]]
        low, high = range_ref[0], range_ref[1]
        for j in range(FOUR):
            rows = slice(j * UNIT, (j + 1) * UNIT)
            s = score_refs[g][rows, :] * factor + bias
            if shift:
                s = s - jnp.max(s, axis=-1, keepdims=True)
            expo = jnp.exp2(s)
            total = jnp.sum(expo, axis=-1, keepdims=True)
            low, high = jnp.minimum(low, total), jnp.maximum(high, total)
            prob_refs[g][rows, :] = (expo * pl.reciprocal(total, approx=True)).astype(BF16)
        range_ref[0] = low
        range_ref[1] = high

    def mix(i, g):
        _, _, kv_row, att_row = place(i)
        rows, window = pl.ds(row(att_row), UNIT), pl.ds(row(kv_row), WINDOW)
        one = lax.broadcasted_iota(jnp.int32, (UNIT, PAIR), 1) < HEAD_DIM
        lanes = slice(g * wide, (g + 1) * wide)
        out = jnp.dot(prob_refs[g][...], v_ref[window, lanes], preferred_element_type=F32)
        for p in range(FOUR // 2):
            low, high = 2 * p * UNIT, (2 * p + 1) * UNIT
            cols = slice(p * PAIR, (p + 1) * PAIR)
            mixed = jnp.where(one, out[low : low + UNIT, cols], out[high : high + UNIT, cols])
            att_ref[rows, g * wide + p * PAIR : g * wide + (p + 1) * PAIR] = mixed.astype(BF16)

    def stages(mixed=None, softened=None, scored=None):
        for g in range(groups):
            if mixed is not None:
                mix(mixed, g)
            if softened is not None:
                soften(softened, g)
            if scored is not None:
                score(scored, g)

    range_ref[...] = jnp.ones_like(range_ref)
    stages(scored=0)
    stages(softened=0, scored=1)
    steady = count - 2
    many = max(n for n in range(1, MANY + 1) if steady % n == 0)

    def one(i, carry):
        for j in range(many):
            stages(i * many + j, i * many + j + 1, i * many + j + 2)
        return carry

    if steady == many:
        one(0, 0)
    else:
        lax.fori_loop(0, steady // many, one, 0)
    stages(mixed=count - 2, softened=count - 1)
    stages(mixed=count - 1)
    fine = (jnp.min(range_ref[0]) >= SUM_LOW) & (jnp.max(range_ref[1]) <= SUM_HIGH)

    @pl.when(jnp.logical_not(fine))
    def _():
        def shifted(i, carry):
            for g in range(groups):
                score(i, g)
                soften(i, g, shift=True)
                mix(i, g)
            return carry

        lax.fori_loop(0, count, shifted, 0)


def in_line(first):
    return lambda i: (first + i, (first + i) * UNIT, (first + i - 1) * UNIT, (first + i) * UNIT)


def edge_kernel(
    state_hbm, cond_hbm, ids_hbm, time_hbm, gain_hbm,
    cross_hbm, core_hbm, small_hbm,
    cross_ref, core_ref, small_ref, state_last, cond_last, state_first, cond_first, ids_ref, time_ref, gain_ref, sems,
):
    own = state_hbm.shape[0]
    copies = [
        pltpu.make_async_copy(source, target, sems.at[i])
        for i, (source, target) in enumerate(
            (
                (state_hbm.at[pl.ds(own - BEHIND, BEHIND)], state_last),
                (cond_hbm.at[pl.ds(own - BEHIND, BEHIND)], cond_last),
                (state_hbm.at[pl.ds(0, AHEAD)], state_first),
                (cond_hbm.at[pl.ds(0, AHEAD)], cond_first),
                (ids_hbm, ids_ref),
                (time_hbm, time_ref),
                (gain_hbm, gain_ref),
            )
        )
    ]
    for copy in copies:
        copy.start()
    even = lax.rem(lax.axis_index("seq"), 2) == 0
    for copy in copies:
        copy.wait()

    depth = core_ref.shape[1]

    def number_row(ids):
        blank = jnp.zeros((1, depth - ids.shape[1]), F32)
        return jnp.concatenate([(ids + 1).astype(F32), blank], axis=1)

    vectors = [ref[...].astype(F32).reshape(1, -1) for ref in (time_ref, gain_ref)]
    blank = jnp.zeros((SMALL - 3, depth), F32)
    small_ref[...] = jnp.concatenate([number_row(ids_ref[...]), *vectors, blank], axis=0).astype(BF16)
    leaving = [
        pltpu.make_async_copy(small_ref, small_hbm.at[pl.ds(0, SMALL)], sems.at[7]),
        pltpu.make_async_copy(cross_ref, cross_hbm, sems.at[8]),
        pltpu.make_async_copy(core_ref, core_hbm, sems.at[9]),
    ]
    leaving[0].start()

    def fill(ref, state, cond, ids):
        rows = state.shape[0]
        ref[0:rows, :] = (state[...].astype(F32) + cond[...].astype(F32)).astype(BF16)
        if rows < BEHIND:
            ref[rows:BEHIND, :] = jnp.zeros((BEHIND - rows, depth), BF16)
        ref[BEHIND:, :] = jnp.broadcast_to(number_row(ids), (PAYLOAD - BEHIND, depth)).astype(BF16)

    def fill_both(to_next, to_previous):
        fill(to_next, state_last, cond_last, ids_ref[:, own - BEHIND :])
        fill(to_previous, state_first, cond_first, ids_ref[:, :BEHIND])

    @pl.when(even)
    def _():
        fill_both(core_ref, cross_ref)

    @pl.when(jnp.logical_not(even))
    def _():
        fill_both(cross_ref, core_ref)

    leaving[1].start()
    leaving[2].start()
    for copy in leaving:
        copy.wait()


def own_kernel(
    small_hbm, state_hbm, cond_hbm, wqkv_hbm,
    small_ref, state_ref, cond_ref, q_ref, k_ref, v_ref, seg_ref, bias_ref,
    wk_ref, wv_ref, wq_ref, normed_ref, sems,
):
    own = state_ref.shape[0]
    copies = [
        pltpu.make_async_copy(state_hbm, state_ref, sems.at[0]),
        pltpu.make_async_copy(cond_hbm, cond_ref, sems.at[1]),
        pltpu.make_async_copy(small_hbm.at[pl.ds(0, SMALL)], small_ref, sems.at[5]),
    ]
    weights = [
        pltpu.make_async_copy(wqkv_hbm.at[which], w_ref, sems.at[2 + which])
        for which, w_ref in ((1, wk_ref), (2, wv_ref), (0, wq_ref))
    ]
    for copy in copies + weights[:1]:
        copy.start()
    copies[2].wait()
    gain = small_ref[2:3, :].astype(F32)
    own_segments(small_ref, seg_ref, own)
    build_masks((3, own // UNIT + 1), seg_ref, bias_ref)
    copies[0].wait()
    copies[1].wait()
    for copy in weights[1:]:
        copy.start()

    def hidden(at):
        return state_ref[at, :].astype(F32) + cond_ref[at, :].astype(F32)

    normalize(hidden, normed_ref, gain, 0, own)
    for w_ref, copy, out_ref in zip((wk_ref, wv_ref, wq_ref), weights, (k_ref, v_ref, q_ref)):
        copy.wait()
        project(normed_ref, w_ref, 0, own, out_ref, [(own, 0)])


def rest_kernel(
    cross_ref, core_ref, small_ref, state_ref, cond_ref, q_own, k_own, v_own, seg_own, bias_own,
    wqkv_hbm, wout_hbm,
    out_ref,
    wk_ref, wv_ref, wq_ref, wout, behind_ref, ahead_ref, halo_ref, h_ref, q_edge, k_edge, v_edge,
    normed_ref, q_ref, k_ref, v_ref, att_ref, seg_ref, bias_ref, range_ref, sems, *group_refs,
):
    own = state_ref.shape[0]
    units = own // UNIT
    end = BEHIND + own
    total = end + AHEAD
    weights = [
        pltpu.make_async_copy(wqkv_hbm.at[which], w_ref, sems.at[which])
        for which, w_ref in ((1, wk_ref), (2, wv_ref), (0, wq_ref))
    ]
    wout_copy = pltpu.make_async_copy(wout_hbm, wout, sems.at[3])
    for copy in weights + [wout_copy]:
        copy.start()
    half_time = 0.5 * small_ref[1:2, :].astype(F32)
    gain = small_ref[2:3, :].astype(F32)
    even = lax.rem(lax.axis_index("seq"), 2) == 0

    bias_ref[3 : units + 1] = bias_own[3 : units + 1]
    attend(
        units - 2,
        lambda i: (i + 3, (i + 1) * UNIT, i * UNIT, (i + 3) * UNIT),
        q_own, k_own, v_own, att_ref, bias_ref, range_ref, group_refs,
    )

    def take(before, after):
        behind_ref[...] = before[...]
        ahead_ref[...] = after[...]

    @pl.when(even)
    def _():
        take(cross_ref, core_ref)

    @pl.when(jnp.logical_not(even))
    def _():
        take(core_ref, cross_ref)

    seg_ref[BEHIND:end, :] = seg_own[BEHIND:end, :]
    edge_segments(behind_ref, ahead_ref, seg_ref)
    for unit in (1, 2, units + 1, units + 2):
        build_mask(unit, seg_ref, bias_ref)
    for ref, rows, first in ((behind_ref, BEHIND, 0), (ahead_ref, AHEAD, BEHIND)):
        for at in range(0, rows, ROWS):
            h = ref[at : at + ROWS, :].astype(F32)
            scale = lax.rsqrt(jnp.mean(h * h, axis=-1, keepdims=True) + 1e-06)
            halo_ref[first + at : first + at + ROWS, :] = (h * scale * gain).astype(BF16)
    for ref, whole in ((k_edge, k_own), (v_edge, v_own)):
        ref[BEHIND:EDGE, :] = whole[0 : EDGE - BEHIND, :]
        ref[EDGE : EDGE + BEHIND, :] = whole[own - BEHIND : own, :]
    q_edge[UNIT : 2 * UNIT, :] = q_own[0:UNIT, :]
    q_edge[2 * UNIT : 3 * UNIT, :] = q_own[own - UNIT : own, :]
    clear_spare((k_edge, v_edge))
    both = [(BEHIND, 0), (AHEAD, EDGE + BEHIND)]
    weights[0].wait()
    project(halo_ref, wk_ref, 0, BEHIND + AHEAD, k_edge, both)
    weights[1].wait()
    project(halo_ref, wv_ref, 0, BEHIND + AHEAD, v_edge, both)
    weights[2].wait()
    project(halo_ref, wq_ref, UNIT, BEHIND + AHEAD, q_edge, [(UNIT, 0), (UNIT, 3 * UNIT)])

    def edge_unit(i):
        side = i // 2
        unit = i + 1 + side * (units - 2)
        return unit, i * UNIT, side * EDGE + (i - 2 * side) * UNIT, unit * UNIT

    attend(4, edge_unit, q_edge, k_edge, v_edge, att_ref, bias_ref, range_ref, group_refs)
    wout_copy.wait()
    depth = wout.shape[1]
    for at in range(0, depth, TILE):
        cols = slice(at, at + TILE)
        moved = 0.5 * jnp.dot(att_ref[UNIT:total, :], wout[:, cols], preferred_element_type=F32)
        moved = moved + half_time[:, cols]
        h_ref[UNIT:BEHIND, cols] = behind_ref[UNIT:BEHIND, cols].astype(F32) + moved[:UNIT]
        h_ref[BEHIND:end, cols] = (
            state_ref[:, cols].astype(F32) + cond_ref[:, cols].astype(F32)
        ) + moved[UNIT : UNIT + own]
        h_ref[end:total, cols] = ahead_ref[0:AHEAD, cols].astype(F32) + moved[UNIT + own :]

    normalize(lambda at: h_ref[at, :], normed_ref, gain, UNIT, total)
    project(normed_ref, wk_ref, UNIT, total, k_ref, [(total - UNIT, UNIT)])
    project(normed_ref, wv_ref, UNIT, total, v_ref, [(total - UNIT, UNIT)])
    project(normed_ref, wq_ref, BEHIND, end, q_ref, [(own, BEHIND)])
    attend(units, in_line(2), q_ref, k_ref, v_ref, att_ref, bias_ref, range_ref, group_refs)
    for at in range(0, depth, TILE):
        cols = slice(at, at + TILE)
        moved = jnp.dot(att_ref[BEHIND:end, :], wout[:, cols], preferred_element_type=F32)
        x = h_ref[BEHIND:end, cols] - cond_ref[:, cols].astype(F32) - half_time[:, cols]
        out_ref[:, cols] = (x + 0.5 * moved).astype(BF16)


def clear_spare(refs):
    for ref in refs:
        ref[ref.shape[0] - SPARE :, :] = jnp.zeros((SPARE, ref.shape[1]), ref.dtype)


def one_step(
    final, h_ref, small_ref, behind_ref, ahead_ref, wqkv, wout,
    out_ref,
    normed_ref, q_ref, k_ref, v_ref, att_ref, seg_ref, bias_ref, range_ref, *group_refs,
):
    total = h_ref.shape[0]
    own = total - BEHIND - AHEAD
    kv_first = UNIT if final else 0
    first, last = (BEHIND, BEHIND + own) if final else (UNIT, total)
    own_segments(small_ref, seg_ref, own)
    edge_segments(behind_ref, ahead_ref, seg_ref)
    build_masks((1, total // UNIT), seg_ref, bias_ref)
    clear_spare((k_ref, v_ref))
    gain = small_ref[2:3, :].astype(F32)
    normalize(lambda at: h_ref[at, :], normed_ref, gain, kv_first, total)
    project(normed_ref, wqkv.at[1], kv_first, total, k_ref, [(total - kv_first, kv_first)])
    project(normed_ref, wqkv.at[2], kv_first, total, v_ref, [(total - kv_first, kv_first)])
    project(normed_ref, wqkv.at[0], first, last, q_ref, [(last - first, first)])
    attend(
        (last - first) // UNIT, in_line(first // UNIT),
        q_ref, k_ref, v_ref, att_ref, bias_ref, range_ref, group_refs,
    )
    for at in range(0, wout.shape[1], TILE):
        cols = slice(at, at + TILE)
        out_ref[:, cols] = jnp.dot(
            att_ref[first:last, :], wout[:, cols], preferred_element_type=F32
        ).astype(BF16)


def shards(state, condition, time_vector, norm_gain, w_qkv, w_out, utterance_ids):
    own, depth = state.shape
    width = w_qkv.shape[2]
    total = BEHIND + own + AHEAD
    parts = lax.axis_size("mp")
    count = lax.axis_size("seq")
    ids = utterance_ids.reshape(1, own)
    vmem = pl.BlockSpec(memory_space=pltpu.VMEM)
    hbm = pl.BlockSpec(memory_space=pltpu.HBM)

    def limit(mib):
        return pltpu.CompilerParams(vmem_limit_bytes=int(mib * 2**20))

    cross, core, small = pl.pallas_call(
        edge_kernel,
        out_shape=[jax.ShapeDtypeStruct((rows, depth), BF16) for rows in (PAYLOAD, PAYLOAD, 2 * own)],
        in_specs=[hbm] * 5,
        out_specs=[hbm] * 3,
        scratch_shapes=[pltpu.VMEM((PAYLOAD, depth), BF16)] * 2
        + [pltpu.VMEM((SMALL, depth), BF16)]
        + [pltpu.VMEM((BEHIND, depth), BF16)] * 2
        + [pltpu.VMEM((AHEAD, depth), BF16)] * 2
        + [pltpu.VMEM((1, own), jnp.int32)]
        + [pltpu.VMEM((depth,), BF16)] * 2
        + [pltpu.SemaphoreType.DMA((10,))],
        compiler_params=limit(EDGE_LIMIT),
    )(state, condition, ids, time_vector, norm_gain)
    ends = [(i, i + 1) for i in range(1, count - 1, 2)]
    cross = lax.ppermute(cross, "seq", ends + [(j, i) for i, j in ends])
    ends = [(i, i + 1) for i in range(0, count - 1, 2)]
    core = lax.ppermute(core, "seq", ends + [(j, i) for i, j in ends])

    work = [((total, depth), BF16), ((total, width), BF16)]
    work += [((total + SPARE, width), BF16)] * 2
    work += [
        ((total, width), BF16),
        ((total + SPARE, 128), F32),
        ((total // UNIT, UNIT, WINDOW), F32),
        ((2, UNIT, PAIR), F32),
    ]
    groups = [((FOUR * UNIT, WINDOW), kind) for kind in (F32, BF16) for _ in range(width // (FOUR * HEAD_DIM))]
    groups = [pltpu.VMEM(*one) for one in groups]
    if parts == 1:
        kept = [((SMALL, depth), BF16)] + [(state.shape, BF16)] * 2 + [((own, width), BF16)] * 3
        kept += [((total + SPARE, 128), F32), ((total // UNIT, UNIT, WINDOW), F32)]
        kept = pl.pallas_call(
            own_kernel,
            out_shape=[jax.ShapeDtypeStruct(*one) for one in kept],
            in_specs=[hbm] * 4,
            out_specs=[vmem] * 8,
            scratch_shapes=[pltpu.VMEM((depth, width), BF16)] * 3
            + [pltpu.VMEM((own, depth), BF16), pltpu.SemaphoreType.DMA((6,))],
            compiler_params=limit(OWN_LIMIT),
            cost_estimate=pl.CostEstimate(
                flops=6 * own * depth * width, bytes_accessed=2 * 4 * depth * width, transcendentals=0
            ),
        )(small, state, condition, w_qkv)
        first = [((depth, width), BF16)] * 3 + [(w_out.shape, BF16)] + [((PAYLOAD, depth), BF16)] * 2
        first += [((BEHIND + AHEAD, depth), BF16), ((total, depth), F32)]
        first += [((4 * UNIT, width), BF16)] + [((2 * EDGE, width), BF16)] * 2
        return pl.pallas_call(
            rest_kernel,
            out_shape=jax.ShapeDtypeStruct((own, depth), BF16),
            in_specs=[vmem] * 10 + [hbm] * 2,
            out_specs=vmem,
            scratch_shapes=[pltpu.VMEM(*one) for one in first + work]
            + [pltpu.SemaphoreType.DMA((4,))]
            + groups,
            compiler_params=limit(LIMIT),
        )(cross, core, *kept, w_qkv, w_out)

    even = lax.axis_index("seq") % 2 == 0
    small = small[:SMALL]
    behind = jnp.where(even, cross, core)
    ahead = jnp.where(even, core, cross)

    def terms(h, final):
        rows = own if final else total - UNIT
        mine = pl.pallas_call(
            functools.partial(one_step, final),
            out_shape=jax.ShapeDtypeStruct((rows, depth), BF16),
            in_specs=[vmem] * 6,
            out_specs=vmem,
            scratch_shapes=[pltpu.VMEM(*one) for one in work] + groups,
            compiler_params=limit(LIMIT),
        )(h, small, behind, ahead, w_qkv, w_out)
        return lax.psum(mine, "mp").astype(F32)

    start = state.astype(F32)
    h = jnp.concatenate(
        [behind[:BEHIND].astype(F32), start + condition.astype(F32), ahead[:AHEAD].astype(F32)]
    )
    velocity = terms(h, False)
    later = jnp.pad(velocity, ((UNIT, 0), (0, 0))) * 0.5 + 0.5 * time_vector.astype(F32)
    x = start + 0.5 * velocity[UNIT : UNIT + own] + 0.5 * terms(h + later, True)
    share = depth // parts
    mine = lax.dynamic_slice_in_dim(x, lax.axis_index("mp") * share, share, 1)
    return mine.astype(BF16)


def solution(mesh):
    in_specs = (
        P("seq", None),
        P("seq", None),
        P(),
        P(),
        P(None, None, "mp"),
        P("mp", None),
        P("seq"),
    )
    out_specs = P("seq", "mp")
    return jax.shard_map(shards, mesh=mesh, in_specs=in_specs, out_specs=out_specs, check_vma=False)
```

```python
import functools
import math

import jax
import jax.numpy as jnp
from jax import lax
from jax.experimental import pallas as pl
from jax.experimental.pallas import tpu as pltpu
from jax.sharding import PartitionSpec as P

HEAD_DIM = 64
BLOCK = 24
UNIT = 2 * BLOCK
BEHIND = 4 * BLOCK
AHEAD = 2 * BLOCK
WINDOW = 128
SPARE = WINDOW - 2 * UNIT
EDGE = UNIT + WINDOW
PAIR = 2 * HEAD_DIM
MANY = 8
FOUR = 4
SUM_LOW, SUM_HIGH = 2.0**-60, 2.0**100
SMALL = 16
PAYLOAD = BEHIND + 16
TILE = 256
ROWS = 16
EDGE_LIMIT, OWN_LIMIT, LIMIT = 56, 48, 48
F32 = jnp.float32
BF16 = jnp.bfloat16
NEG = -1e30


def column_of(row):
    n = row.shape[1]
    same = lax.broadcasted_iota(jnp.int32, (n, n), 0) == lax.broadcasted_iota(jnp.int32, (n, n), 1)
    column = jnp.sum(jnp.where(same, row, 0.0), axis=1, keepdims=True)
    return jnp.broadcast_to(column, (n, 128))


def own_segments(small_ref, seg_ref, own):
    for at in range(0, own, 128):
        n = min(128, own - at)
        row = small_ref[0:1, at : at + n].astype(F32)
        seg_ref[BEHIND + at : BEHIND + at + n, :] = column_of(row)


def edge_segments(behind_ref, ahead_ref, seg_ref):
    end = seg_ref.shape[0] - SPARE
    seg_ref[0:BEHIND, :] = column_of(behind_ref[BEHIND : BEHIND + 1, 0:BEHIND].astype(F32))
    seg_ref[end - AHEAD : end, :] = column_of(ahead_ref[BEHIND : BEHIND + 1, 0:AHEAD].astype(F32))
    seg_ref[end : end + SPARE, :] = jnp.full((SPARE, 128), -1.0, F32)


def build_mask(unit, seg_ref, bias_ref):
    start = unit * UNIT
    if not isinstance(unit, int):
        start = pl.multiple_of(start, 16)
    window = seg_ref[pl.ds(start - UNIT, WINDOW), :]
    r = lax.broadcasted_iota(jnp.int32, (WINDOW, WINDOW), 0)
    c = lax.broadcasted_iota(jnp.int32, (WINDOW, WINDOW), 1)
    keys = jnp.sum(jnp.where(r == c, window, 0.0), axis=0, keepdims=True)
    queries = seg_ref[pl.ds(start, UNIT), :]
    row = lax.broadcasted_iota(jnp.int32, (UNIT, WINDOW), 0)
    col = lax.broadcasted_iota(jnp.int32, (UNIT, WINDOW), 1)
    first = jnp.where(row < BLOCK, 0, BLOCK)
    band = (col >= first) & (col < first + 4 * BLOCK)
    bias_ref[unit] = jnp.where(band & (queries == keys), 0.0, NEG)


def build_masks(units, seg_ref, bias_ref):
    for unit in range(*units):
        build_mask(unit, seg_ref, bias_ref)


def normalize(load, normed_ref, gain, first, last):
    groups = (last - first) // ROWS
    many = max(n for n in range(1, 13) if groups % n == 0)

    def one(i, carry):
        for j in range(many):
            at = pl.ds(pl.multiple_of(first + (i * many + j) * ROWS, ROWS), ROWS)
            h = load(at)
            scale = lax.rsqrt(jnp.mean(h * h, axis=-1, keepdims=True) + 1e-06)
            normed_ref[at, :] = (h * scale * gain).astype(BF16)
        return carry

    lax.fori_loop(0, groups // many, one, 0)


def project(normed_ref, w_ref, first, last, out_ref, places):
    width = w_ref.shape[1]
    tile = min(TILE, width)
    for at in range(0, width, tile):
        cols = slice(at, at + tile)
        out = jnp.dot(
            normed_ref[first:last, :], w_ref[:, cols], preferred_element_type=F32
        ).astype(BF16)
        done = 0
        for rows, place in places:
            out_ref[place : place + rows, cols] = out[done : done + rows]
            done += rows


def attend(count, place, q_ref, k_ref, v_ref, att_ref, bias_ref, range_ref, group_refs, shift=False):
    wide = FOUR * HEAD_DIM
    groups = q_ref.shape[1] // wide
    factor = HEAD_DIM**-0.5 * math.log2(math.e)

    def row(start):
        return start if isinstance(start, int) else pl.multiple_of(start, 16)

    score_refs, prob_refs = group_refs[:groups], group_refs[groups:]

    def score(i, g):
        _, q_row, kv_row, _ = place(i)
        rows, window = pl.ds(row(q_row), UNIT), pl.ds(row(kv_row), WINDOW)
        head = lax.broadcasted_iota(jnp.int32, (UNIT, wide), 1) // HEAD_DIM
        lanes = slice(g * wide, (g + 1) * wide)
        q = q_ref[rows, lanes]
        zero = jnp.zeros_like(q)
        stacked = jnp.concatenate([jnp.where(head == j, q, zero) for j in range(FOUR)], axis=0)
        score_refs[g][...] = lax.dot_general(
            stacked, k_ref[window, lanes], (((1,), (1,)), ((), ())), preferred_element_type=F32
        )

    def soften(i, g):
        bias = bias_ref[place(i)[0]]
        low, high = range_ref[0], range_ref[1]
        for j in range(FOUR):
            rows = slice(j * UNIT, (j + 1) * UNIT)
            s = score_refs[g][rows, :] * factor + bias
            if shift:
                s = s - jnp.max(s, axis=-1, keepdims=True)
            expo = jnp.exp2(s)
            total = jnp.sum(expo, axis=-1, keepdims=True)
            low, high = jnp.minimum(low, total), jnp.maximum(high, total)
            prob_refs[g][rows, :] = (expo * pl.reciprocal(total, approx=True)).astype(BF16)
        range_ref[0] = low
        range_ref[1] = high

    def mix(i, g):
        _, _, kv_row, att_row = place(i)
        rows, window = pl.ds(row(att_row), UNIT), pl.ds(row(kv_row), WINDOW)
        one = lax.broadcasted_iota(jnp.int32, (UNIT, PAIR), 1) < HEAD_DIM
        lanes = slice(g * wide, (g + 1) * wide)
        out = jnp.dot(prob_refs[g][...], v_ref[window, lanes], preferred_element_type=F32)
        for p in range(FOUR // 2):
            low, high = 2 * p * UNIT, (2 * p + 1) * UNIT
            cols = slice(p * PAIR, (p + 1) * PAIR)
            mixed = jnp.where(one, out[low : low + UNIT, cols], out[high : high + UNIT, cols])
            att_ref[rows, g * wide + p * PAIR : g * wide + (p + 1) * PAIR] = mixed.astype(BF16)

    def stages(mixed=None, softened=None, scored=None):
        for g in range(groups):
            if mixed is not None:
                mix(mixed, g)
            if softened is not None:
                soften(softened, g)
            if scored is not None:
                score(scored, g)

    if shift:

        def all_stages(i, carry):
            for g in range(groups):
                score(i, g)
                soften(i, g)
                mix(i, g)
            return carry

        lax.fori_loop(0, count, all_stages, 0)
        return

    stages(scored=0)
    stages(softened=0, scored=1)
    steady = count - 2
    many = max(n for n in range(1, MANY + 1) if steady % n == 0)

    def one(i, carry):
        for j in range(many):
            stages(i * many + j, i * many + j + 1, i * many + j + 2)
        return carry

    if steady == many:
        one(0, 0)
    else:
        lax.fori_loop(0, steady // many, one, 0)
    stages(mixed=count - 2, softened=count - 1)
    stages(mixed=count - 1)


def unshifted_first(range_ref, parts):
    range_ref[...] = jnp.ones_like(range_ref)
    for part in parts:
        part(False)
    fine = (jnp.min(range_ref[0]) >= SUM_LOW) & (jnp.max(range_ref[1]) <= SUM_HIGH)

    @pl.when(jnp.logical_not(fine))
    def _():
        for part in parts:
            part(True)


def in_line(first):
    return lambda i: (first + i, (first + i) * UNIT, (first + i - 1) * UNIT, (first + i) * UNIT)


def edge_kernel(
    state_hbm, cond_hbm, ids_hbm, time_hbm, gain_hbm,
    cross_hbm, core_hbm, small_hbm,
    cross_ref, core_ref, small_ref, state_last, cond_last, state_first, cond_first, ids_ref, time_ref, gain_ref, sems,
):
    own = state_hbm.shape[0]
    copies = [
        pltpu.make_async_copy(source, target, sems.at[i])
        for i, (source, target) in enumerate(
            (
                (state_hbm.at[pl.ds(own - BEHIND, BEHIND)], state_last),
                (cond_hbm.at[pl.ds(own - BEHIND, BEHIND)], cond_last),
                (state_hbm.at[pl.ds(0, AHEAD)], state_first),
                (cond_hbm.at[pl.ds(0, AHEAD)], cond_first),
                (ids_hbm, ids_ref),
                (time_hbm, time_ref),
                (gain_hbm, gain_ref),
            )
        )
    ]
    for copy in copies:
        copy.start()
    even = lax.rem(lax.axis_index("seq"), 2) == 0
    for copy in copies:
        copy.wait()

    depth = core_ref.shape[1]

    def number_row(ids):
        blank = jnp.zeros((1, depth - ids.shape[1]), F32)
        return jnp.concatenate([(ids + 1).astype(F32), blank], axis=1)

    vectors = [ref[...].astype(F32).reshape(1, -1) for ref in (time_ref, gain_ref)]
    blank = jnp.zeros((SMALL - 3, depth), F32)
    small_ref[...] = jnp.concatenate([number_row(ids_ref[...]), *vectors, blank], axis=0).astype(BF16)
    leaving = [
        pltpu.make_async_copy(small_ref, small_hbm.at[pl.ds(0, SMALL)], sems.at[7]),
        pltpu.make_async_copy(cross_ref, cross_hbm, sems.at[8]),
        pltpu.make_async_copy(core_ref, core_hbm, sems.at[9]),
    ]
    leaving[0].start()

    def fill(ref, state, cond, ids):
        rows = state.shape[0]
        ref[0:rows, :] = (state[...].astype(F32) + cond[...].astype(F32)).astype(BF16)
        if rows < BEHIND:
            ref[rows:BEHIND, :] = jnp.zeros((BEHIND - rows, depth), BF16)
        ref[BEHIND:, :] = jnp.broadcast_to(number_row(ids), (PAYLOAD - BEHIND, depth)).astype(BF16)

    def fill_both(to_next, to_previous):
        fill(to_next, state_last, cond_last, ids_ref[:, own - BEHIND :])
        fill(to_previous, state_first, cond_first, ids_ref[:, :BEHIND])

    @pl.when(even)
    def _():
        fill_both(core_ref, cross_ref)

    @pl.when(jnp.logical_not(even))
    def _():
        fill_both(cross_ref, core_ref)

    leaving[1].start()
    leaving[2].start()
    for copy in leaving:
        copy.wait()


def own_kernel(
    small_hbm, state_hbm, cond_hbm, wqkv_hbm,
    small_ref, state_ref, cond_ref, q_ref, k_ref, v_ref, seg_ref, bias_ref,
    wk_ref, wv_ref, wq_ref, normed_ref, sems,
):
    own = state_ref.shape[0]
    copies = [
        pltpu.make_async_copy(state_hbm, state_ref, sems.at[0]),
        pltpu.make_async_copy(cond_hbm, cond_ref, sems.at[1]),
        pltpu.make_async_copy(small_hbm.at[pl.ds(0, SMALL)], small_ref, sems.at[5]),
    ]
    weights = [
        pltpu.make_async_copy(wqkv_hbm.at[which], w_ref, sems.at[2 + which])
        for which, w_ref in ((1, wk_ref), (2, wv_ref), (0, wq_ref))
    ]
    for copy in copies + weights[:1]:
        copy.start()
    copies[2].wait()
    gain = small_ref[2:3, :].astype(F32)
    own_segments(small_ref, seg_ref, own)
    build_masks((3, own // UNIT + 1), seg_ref, bias_ref)
    copies[0].wait()
    copies[1].wait()
    for copy in weights[1:]:
        copy.start()

    def hidden(at):
        return state_ref[at, :].astype(F32) + cond_ref[at, :].astype(F32)

    normalize(hidden, normed_ref, gain, 0, own)
    for w_ref, copy, out_ref in zip((wk_ref, wv_ref, wq_ref), weights, (k_ref, v_ref, q_ref)):
        copy.wait()
        project(normed_ref, w_ref, 0, own, out_ref, [(own, 0)])


def rest_kernel(
    cross_ref, core_ref, small_ref, state_ref, cond_ref, q_own, k_own, v_own, seg_own, bias_own,
    wqkv_hbm, wout_hbm,
    out_ref,
    wk_ref, wv_ref, wq_ref, wout, behind_ref, ahead_ref, halo_ref, h_ref, q_edge, k_edge, v_edge,
    normed_ref, q_ref, k_ref, v_ref, att_ref, seg_ref, bias_ref, range_ref, sems, *group_refs,
):
    own = state_ref.shape[0]
    units = own // UNIT
    end = BEHIND + own
    total = end + AHEAD
    weights = [
        pltpu.make_async_copy(wqkv_hbm.at[which], w_ref, sems.at[which])
        for which, w_ref in ((1, wk_ref), (2, wv_ref), (0, wq_ref))
    ]
    wout_copy = pltpu.make_async_copy(wout_hbm, wout, sems.at[3])
    for copy in weights + [wout_copy]:
        copy.start()
    half_time = 0.5 * small_ref[1:2, :].astype(F32)
    gain = small_ref[2:3, :].astype(F32)
    even = lax.rem(lax.axis_index("seq"), 2) == 0
    bias_ref[3 : units + 1] = bias_own[3 : units + 1]

    def interior(shift):
        attend(
            units - 2,
            lambda i: (i + 3, (i + 1) * UNIT, i * UNIT, (i + 3) * UNIT),
            q_own, k_own, v_own, att_ref, bias_ref, range_ref, group_refs, shift,
        )

    def edges(shift):
        def place(i):
            side = i // 2
            unit = i + 1 + side * (units - 2)
            return unit, i * UNIT, side * EDGE + (i - 2 * side) * UNIT, unit * UNIT

        if not shift:
            prepare_edges()
        attend(4, place, q_edge, k_edge, v_edge, att_ref, bias_ref, range_ref, group_refs, shift)

    def prepare_edges():
        behind_ref[...] = jnp.where(even, cross_ref[...], core_ref[...])
        ahead_ref[...] = jnp.where(even, core_ref[...], cross_ref[...])
        seg_ref[BEHIND:end, :] = seg_own[BEHIND:end, :]
        edge_segments(behind_ref, ahead_ref, seg_ref)
        for unit in (1, 2, units + 1, units + 2):
            build_mask(unit, seg_ref, bias_ref)
        for ref, rows, first in ((behind_ref, BEHIND, 0), (ahead_ref, AHEAD, BEHIND)):
            for at in range(0, rows, ROWS):
                h = ref[at : at + ROWS, :].astype(F32)
                scale = lax.rsqrt(jnp.mean(h * h, axis=-1, keepdims=True) + 1e-06)
                halo_ref[first + at : first + at + ROWS, :] = (h * scale * gain).astype(BF16)
        for ref, whole in ((k_edge, k_own), (v_edge, v_own)):
            ref[BEHIND:EDGE, :] = whole[0 : EDGE - BEHIND, :]
            ref[EDGE : EDGE + BEHIND, :] = whole[own - BEHIND : own, :]
        q_edge[UNIT : 2 * UNIT, :] = q_own[0:UNIT, :]
        q_edge[2 * UNIT : 3 * UNIT, :] = q_own[own - UNIT : own, :]
        clear_spare((k_edge, v_edge))
        both = [(BEHIND, 0), (AHEAD, EDGE + BEHIND)]
        for copy in weights:
            copy.wait()
        project(halo_ref, wk_ref, 0, BEHIND + AHEAD, k_edge, both)
        project(halo_ref, wv_ref, 0, BEHIND + AHEAD, v_edge, both)
        project(halo_ref, wq_ref, UNIT, BEHIND + AHEAD, q_edge, [(UNIT, 0), (UNIT, 3 * UNIT)])

    unshifted_first(range_ref, (interior, edges))
    wout_copy.wait()
    depth = wout.shape[1]
    for at in range(0, depth, TILE):
        cols = slice(at, at + TILE)
        moved = 0.5 * jnp.dot(att_ref[UNIT:total, :], wout[:, cols], preferred_element_type=F32)
        moved = moved + half_time[:, cols]
        h_ref[UNIT:BEHIND, cols] = behind_ref[UNIT:BEHIND, cols].astype(F32) + moved[:UNIT]
        h_ref[BEHIND:end, cols] = (
            state_ref[:, cols].astype(F32) + cond_ref[:, cols].astype(F32)
        ) + moved[UNIT : UNIT + own]
        h_ref[end:total, cols] = ahead_ref[0:AHEAD, cols].astype(F32) + moved[UNIT + own :]

    normalize(lambda at: h_ref[at, :], normed_ref, gain, UNIT, total)
    project(normed_ref, wk_ref, UNIT, total, k_ref, [(total - UNIT, UNIT)])
    project(normed_ref, wv_ref, UNIT, total, v_ref, [(total - UNIT, UNIT)])
    project(normed_ref, wq_ref, BEHIND, end, q_ref, [(own, BEHIND)])

    def second(shift):
        attend(units, in_line(2), q_ref, k_ref, v_ref, att_ref, bias_ref, range_ref, group_refs, shift)

    unshifted_first(range_ref, (second,))
    for at in range(0, depth, TILE):
        cols = slice(at, at + TILE)
        moved = jnp.dot(att_ref[BEHIND:end, :], wout[:, cols], preferred_element_type=F32)
        x = h_ref[BEHIND:end, cols] - cond_ref[:, cols].astype(F32) - half_time[:, cols]
        out_ref[:, cols] = (x + 0.5 * moved).astype(BF16)


def clear_spare(refs):
    for ref in refs:
        ref[ref.shape[0] - SPARE :, :] = jnp.zeros((SPARE, ref.shape[1]), ref.dtype)


def one_step(
    final, h_ref, small_ref, behind_ref, ahead_ref, wqkv, wout,
    out_ref,
    normed_ref, q_ref, k_ref, v_ref, att_ref, seg_ref, bias_ref, range_ref, *group_refs,
):
    total = h_ref.shape[0]
    own = total - BEHIND - AHEAD
    kv_first = UNIT if final else 0
    first, last = (BEHIND, BEHIND + own) if final else (UNIT, total)
    own_segments(small_ref, seg_ref, own)
    edge_segments(behind_ref, ahead_ref, seg_ref)
    build_masks((1, total // UNIT), seg_ref, bias_ref)
    clear_spare((k_ref, v_ref))
    gain = small_ref[2:3, :].astype(F32)
    normalize(lambda at: h_ref[at, :], normed_ref, gain, kv_first, total)
    project(normed_ref, wqkv.at[1], kv_first, total, k_ref, [(total - kv_first, kv_first)])
    project(normed_ref, wqkv.at[2], kv_first, total, v_ref, [(total - kv_first, kv_first)])
    project(normed_ref, wqkv.at[0], first, last, q_ref, [(last - first, first)])

    def every(shift):
        attend(
            (last - first) // UNIT, in_line(first // UNIT),
            q_ref, k_ref, v_ref, att_ref, bias_ref, range_ref, group_refs, shift,
        )

    unshifted_first(range_ref, (every,))
    for at in range(0, wout.shape[1], TILE):
        cols = slice(at, at + TILE)
        out_ref[:, cols] = jnp.dot(
            att_ref[first:last, :], wout[:, cols], preferred_element_type=F32
        ).astype(BF16)


def shards(state, condition, time_vector, norm_gain, w_qkv, w_out, utterance_ids):
    own, depth = state.shape
    width = w_qkv.shape[2]
    total = BEHIND + own + AHEAD
    parts = lax.axis_size("mp")
    count = lax.axis_size("seq")
    ids = utterance_ids.reshape(1, own)
    vmem = pl.BlockSpec(memory_space=pltpu.VMEM)
    hbm = pl.BlockSpec(memory_space=pltpu.HBM)

    def limit(mib):
        return pltpu.CompilerParams(vmem_limit_bytes=int(mib * 2**20))

    cross, core, small = pl.pallas_call(
        edge_kernel,
        out_shape=[jax.ShapeDtypeStruct((rows, depth), BF16) for rows in (PAYLOAD, PAYLOAD, 2 * own)],
        in_specs=[hbm] * 5,
        out_specs=[hbm] * 3,
        scratch_shapes=[pltpu.VMEM((PAYLOAD, depth), BF16)] * 2
        + [pltpu.VMEM((SMALL, depth), BF16)]
        + [pltpu.VMEM((BEHIND, depth), BF16)] * 2
        + [pltpu.VMEM((AHEAD, depth), BF16)] * 2
        + [pltpu.VMEM((1, own), jnp.int32)]
        + [pltpu.VMEM((depth,), BF16)] * 2
        + [pltpu.SemaphoreType.DMA((10,))],
        compiler_params=limit(EDGE_LIMIT),
    )(state, condition, ids, time_vector, norm_gain)
    ends = [(i, i + 1) for i in range(1, count - 1, 2)]
    cross = lax.ppermute(cross, "seq", ends + [(j, i) for i, j in ends])
    ends = [(i, i + 1) for i in range(0, count - 1, 2)]
    core = lax.ppermute(core, "seq", ends + [(j, i) for i, j in ends])

    work = [((total, depth), BF16), ((total, width), BF16)]
    work += [((total + SPARE, width), BF16)] * 2
    work += [
        ((total, width), BF16),
        ((total + SPARE, 128), F32),
        ((total // UNIT, UNIT, WINDOW), F32),
        ((2, UNIT, PAIR), F32),
    ]
    groups = [((FOUR * UNIT, WINDOW), kind) for kind in (F32, BF16) for _ in range(width // (FOUR * HEAD_DIM))]
    groups = [pltpu.VMEM(*one) for one in groups]
    if parts == 1:
        kept = [((SMALL, depth), BF16)] + [(state.shape, BF16)] * 2 + [((own, width), BF16)] * 3
        kept += [((total + SPARE, 128), F32), ((total // UNIT, UNIT, WINDOW), F32)]
        kept = pl.pallas_call(
            own_kernel,
            out_shape=[jax.ShapeDtypeStruct(*one) for one in kept],
            in_specs=[hbm] * 4,
            out_specs=[vmem] * 8,
            scratch_shapes=[pltpu.VMEM((depth, width), BF16)] * 3
            + [pltpu.VMEM((own, depth), BF16), pltpu.SemaphoreType.DMA((6,))],
            compiler_params=limit(OWN_LIMIT),
            cost_estimate=pl.CostEstimate(
                flops=6 * own * depth * width, bytes_accessed=2 * 4 * depth * width, transcendentals=0
            ),
        )(small, state, condition, w_qkv)
        first = [((depth, width), BF16)] * 3 + [(w_out.shape, BF16)] + [((PAYLOAD, depth), BF16)] * 2
        first += [((BEHIND + AHEAD, depth), BF16), ((total, depth), F32)]
        first += [((4 * UNIT, width), BF16)] + [((2 * EDGE, width), BF16)] * 2
        return pl.pallas_call(
            rest_kernel,
            out_shape=jax.ShapeDtypeStruct((own, depth), BF16),
            in_specs=[vmem] * 10 + [hbm] * 2,
            out_specs=vmem,
            scratch_shapes=[pltpu.VMEM(*one) for one in first + work]
            + [pltpu.SemaphoreType.DMA((4,))]
            + groups,
            compiler_params=limit(LIMIT),
        )(cross, core, *kept, w_qkv, w_out)

    even = lax.axis_index("seq") % 2 == 0
    small = small[:SMALL]
    behind = jnp.where(even, cross, core)
    ahead = jnp.where(even, core, cross)

    def terms(h, final):
        rows = own if final else total - UNIT
        mine = pl.pallas_call(
            functools.partial(one_step, final),
            out_shape=jax.ShapeDtypeStruct((rows, depth), BF16),
            in_specs=[vmem] * 6,
            out_specs=vmem,
            scratch_shapes=[pltpu.VMEM(*one) for one in work] + groups,
            compiler_params=limit(LIMIT),
        )(h, small, behind, ahead, w_qkv, w_out)
        return lax.psum(mine, "mp").astype(F32)

    start = state.astype(F32)
    h = jnp.concatenate(
        [behind[:BEHIND].astype(F32), start + condition.astype(F32), ahead[:AHEAD].astype(F32)]
    )
    velocity = terms(h, False)
    later = jnp.pad(velocity, ((UNIT, 0), (0, 0))) * 0.5 + 0.5 * time_vector.astype(F32)
    x = start + 0.5 * velocity[UNIT : UNIT + own] + 0.5 * terms(h + later, True)
    share = depth // parts
    mine = lax.dynamic_slice_in_dim(x, lax.axis_index("mp") * share, share, 1)
    return mine.astype(BF16)


def solution(mesh):
    in_specs = (
        P("seq", None),
        P("seq", None),
        P(),
        P(),
        P(None, None, "mp"),
        P("mp", None),
        P("seq"),
    )
    out_specs = P("seq", "mp")
    return jax.shard_map(shards, mesh=mesh, in_specs=in_specs, out_specs=out_specs, check_vma=False)
```

```python
import functools
import math

import jax
import jax.numpy as jnp
from jax import lax
from jax.experimental import pallas as pl
from jax.experimental.pallas import tpu as pltpu
from jax.sharding import PartitionSpec as P

HEAD_DIM = 64
BLOCK = 24
UNIT = 2 * BLOCK
BEHIND = 4 * BLOCK
AHEAD = 2 * BLOCK
WINDOW = 128
SPARE = WINDOW - 2 * UNIT
EDGE = UNIT + WINDOW
PAIR = 2 * HEAD_DIM
MANY = 3
FOUR = 4
SUM_LOW, SUM_HIGH = 2.0**-60, 2.0**100
SMALL = 16
PAYLOAD = BEHIND + 16
TILE = 256
ROWS = 16
EDGE_LIMIT, OWN_LIMIT, LIMIT = 56, 48, 48
F32 = jnp.float32
BF16 = jnp.bfloat16
NEG = -1e30


def column_of(row):
    n = row.shape[1]
    same = lax.broadcasted_iota(jnp.int32, (n, n), 0) == lax.broadcasted_iota(jnp.int32, (n, n), 1)
    column = jnp.sum(jnp.where(same, row, 0.0), axis=1, keepdims=True)
    return jnp.broadcast_to(column, (n, 128))


def own_segments(small_ref, seg_ref, own):
    for at in range(0, own, 128):
        n = min(128, own - at)
        row = small_ref[0:1, at : at + n].astype(F32)
        seg_ref[BEHIND + at : BEHIND + at + n, :] = column_of(row)


def edge_segments(behind_ref, ahead_ref, seg_ref):
    end = seg_ref.shape[0] - SPARE
    seg_ref[0:BEHIND, :] = column_of(behind_ref[BEHIND : BEHIND + 1, 0:BEHIND].astype(F32))
    seg_ref[end - AHEAD : end, :] = column_of(ahead_ref[BEHIND : BEHIND + 1, 0:AHEAD].astype(F32))
    seg_ref[end : end + SPARE, :] = jnp.full((SPARE, 128), -1.0, F32)


def build_mask(unit, seg_ref, bias_ref):
    start = unit * UNIT
    if not isinstance(unit, int):
        start = pl.multiple_of(start, 16)
    window = seg_ref[pl.ds(start - UNIT, WINDOW), :]
    r = lax.broadcasted_iota(jnp.int32, (WINDOW, WINDOW), 0)
    c = lax.broadcasted_iota(jnp.int32, (WINDOW, WINDOW), 1)
    keys = jnp.sum(jnp.where(r == c, window, 0.0), axis=0, keepdims=True)
    queries = seg_ref[pl.ds(start, UNIT), :]
    row = lax.broadcasted_iota(jnp.int32, (UNIT, WINDOW), 0)
    col = lax.broadcasted_iota(jnp.int32, (UNIT, WINDOW), 1)
    first = jnp.where(row < BLOCK, 0, BLOCK)
    band = (col >= first) & (col < first + 4 * BLOCK)
    bias_ref[unit] = jnp.where(band & (queries == keys), 0.0, NEG)


def build_masks(units, seg_ref, bias_ref):
    for unit in range(*units):
        build_mask(unit, seg_ref, bias_ref)


def normalize(load, normed_ref, gain, first, last):
    groups = (last - first) // ROWS
    many = max(n for n in range(1, 13) if groups % n == 0)

    def one(i, carry):
        for j in range(many):
            at = pl.ds(pl.multiple_of(first + (i * many + j) * ROWS, ROWS), ROWS)
            h = load(at)
            scale = lax.rsqrt(jnp.mean(h * h, axis=-1, keepdims=True) + 1e-06)
            normed_ref[at, :] = (h * scale * gain).astype(BF16)
        return carry

    lax.fori_loop(0, groups // many, one, 0)


def column_tiles(width, work):
    tile = min(TILE, width)
    if width <= 2 * tile:
        for at in range(0, width, tile):
            work(pl.ds(at, tile))
        return

    def one(i, carry):
        for j in range(2):
            work(pl.ds(pl.multiple_of((2 * i + j) * tile, tile), tile))
        return carry

    lax.fori_loop(0, width // (2 * tile), one, 0)


def project(normed_ref, w_ref, first, last, out_ref, places):
    def work(cols):
        out = jnp.dot(
            normed_ref[first:last, :], w_ref[:, cols], preferred_element_type=F32
        ).astype(BF16)
        done = 0
        for rows, place in places:
            out_ref[place : place + rows, cols] = out[done : done + rows]
            done += rows

    column_tiles(w_ref.shape[1], work)


def attend(count, place, q_ref, k_ref, v_ref, att_ref, bias_ref, range_ref, group_refs):
    wide = FOUR * HEAD_DIM
    groups = q_ref.shape[1] // wide
    factor = HEAD_DIM**-0.5 * math.log2(math.e)

    def row(start):
        return start if isinstance(start, int) else pl.multiple_of(start, 16)

    score_refs, prob_refs = group_refs[:groups], group_refs[groups:]

    def score(i, g):
        _, q_row, kv_row, _ = place(i)
        rows, window = pl.ds(row(q_row), UNIT), pl.ds(row(kv_row), WINDOW)
        head = lax.broadcasted_iota(jnp.int32, (UNIT, wide), 1) // HEAD_DIM
        lanes = slice(g * wide, (g + 1) * wide)
        q = q_ref[rows, lanes]
        zero = jnp.zeros_like(q)
        stacked = jnp.concatenate([jnp.where(head == j, q, zero) for j in range(FOUR)], axis=0)
        score_refs[g][...] = lax.dot_general(
            stacked, k_ref[window, lanes], (((1,), (1,)), ((), ())), preferred_element_type=F32
        )

    def soften(i, g, shift=False):
        bias = bias_ref[place(i)[0]]
        low, high = range_ref[0], range_ref[1]
        for j in range(FOUR):
            rows = slice(j * UNIT, (j + 1) * UNIT)
            s = score_refs[g][rows, :] * factor + bias
            if shift:
                s = s - jnp.max(s, axis=-1, keepdims=True)
            expo = jnp.exp2(s)
            total = jnp.sum(expo, axis=-1, keepdims=True)
            low, high = jnp.minimum(low, total), jnp.maximum(high, total)
            prob_refs[g][rows, :] = (expo * pl.reciprocal(total, approx=True)).astype(BF16)
        range_ref[0] = low
        range_ref[1] = high

    def mix(i, g):
        _, _, kv_row, att_row = place(i)
        rows, window = pl.ds(row(att_row), UNIT), pl.ds(row(kv_row), WINDOW)
        one = lax.broadcasted_iota(jnp.int32, (UNIT, PAIR), 1) < HEAD_DIM
        lanes = slice(g * wide, (g + 1) * wide)
        out = jnp.dot(prob_refs[g][...], v_ref[window, lanes], preferred_element_type=F32)
        for p in range(FOUR // 2):
            low, high = 2 * p * UNIT, (2 * p + 1) * UNIT
            cols = slice(p * PAIR, (p + 1) * PAIR)
            mixed = jnp.where(one, out[low : low + UNIT, cols], out[high : high + UNIT, cols])
            att_ref[rows, g * wide + p * PAIR : g * wide + (p + 1) * PAIR] = mixed.astype(BF16)

    def stages(mixed=None, softened=None, scored=None):
        for g in range(groups):
            if mixed is not None:
                mix(mixed, g)
            if softened is not None:
                soften(softened, g)
            if scored is not None:
                score(scored, g)

    range_ref[...] = jnp.ones_like(range_ref)
    stages(scored=0)
    stages(softened=0, scored=1)
    steady = count - 2
    many = max(n for n in range(1, MANY + 1) if steady % n == 0)

    def one(i, carry):
        for j in range(many):
            stages(i * many + j, i * many + j + 1, i * many + j + 2)
        return carry

    if steady == many:
        one(0, 0)
    else:
        lax.fori_loop(0, steady // many, one, 0)
    stages(mixed=count - 2, softened=count - 1)
    stages(mixed=count - 1)
    fine = (jnp.min(range_ref[0]) >= SUM_LOW) & (jnp.max(range_ref[1]) <= SUM_HIGH)

    @pl.when(jnp.logical_not(fine))
    def _():
        def shifted(i, carry):
            for g in range(groups):
                score(i, g)
                soften(i, g, shift=True)
                mix(i, g)
            return carry

        lax.fori_loop(0, count, shifted, 0)


def in_line(first):
    return lambda i: (first + i, (first + i) * UNIT, (first + i - 1) * UNIT, (first + i) * UNIT)


def edge_kernel(
    state_hbm, cond_hbm, ids_hbm, time_hbm, gain_hbm,
    cross_hbm, core_hbm, small_hbm,
    cross_ref, core_ref, small_ref, state_last, cond_last, state_first, cond_first, ids_ref, time_ref, gain_ref, sems,
):
    own = state_hbm.shape[0]
    copies = [
        pltpu.make_async_copy(source, target, sems.at[i])
        for i, (source, target) in enumerate(
            (
                (state_hbm.at[pl.ds(own - BEHIND, BEHIND)], state_last),
                (cond_hbm.at[pl.ds(own - BEHIND, BEHIND)], cond_last),
                (state_hbm.at[pl.ds(0, AHEAD)], state_first),
                (cond_hbm.at[pl.ds(0, AHEAD)], cond_first),
                (ids_hbm, ids_ref),
                (time_hbm, time_ref),
                (gain_hbm, gain_ref),
            )
        )
    ]
    for copy in copies:
        copy.start()
    even = lax.rem(lax.axis_index("seq"), 2) == 0
    for copy in copies:
        copy.wait()

    depth = core_ref.shape[1]

    def number_row(ids):
        blank = jnp.zeros((1, depth - ids.shape[1]), F32)
        return jnp.concatenate([(ids + 1).astype(F32), blank], axis=1)

    vectors = [ref[...].astype(F32).reshape(1, -1) for ref in (time_ref, gain_ref)]
    blank = jnp.zeros((SMALL - 3, depth), F32)
    small_ref[...] = jnp.concatenate([number_row(ids_ref[...]), *vectors, blank], axis=0).astype(BF16)
    leaving = [
        pltpu.make_async_copy(small_ref, small_hbm.at[pl.ds(0, SMALL)], sems.at[7]),
        pltpu.make_async_copy(cross_ref, cross_hbm, sems.at[8]),
        pltpu.make_async_copy(core_ref, core_hbm, sems.at[9]),
    ]
    leaving[0].start()

    def fill(ref, state, cond, ids):
        rows = state.shape[0]
        ref[0:rows, :] = (state[...].astype(F32) + cond[...].astype(F32)).astype(BF16)
        if rows < BEHIND:
            ref[rows:BEHIND, :] = jnp.zeros((BEHIND - rows, depth), BF16)
        ref[BEHIND:, :] = jnp.broadcast_to(number_row(ids), (PAYLOAD - BEHIND, depth)).astype(BF16)

    def fill_both(to_next, to_previous):
        fill(to_next, state_last, cond_last, ids_ref[:, own - BEHIND :])
        fill(to_previous, state_first, cond_first, ids_ref[:, :BEHIND])

    @pl.when(even)
    def _():
        fill_both(core_ref, cross_ref)

    @pl.when(jnp.logical_not(even))
    def _():
        fill_both(cross_ref, core_ref)

    leaving[1].start()
    leaving[2].start()
    for copy in leaving:
        copy.wait()


def own_kernel(
    small_hbm, state_hbm, cond_hbm, wqkv_hbm,
    small_ref, state_ref, cond_ref, q_ref, k_ref, v_ref, seg_ref, bias_ref,
    wk_ref, wv_ref, wq_ref, normed_ref, sems,
):
    own = state_ref.shape[0]
    copies = [
        pltpu.make_async_copy(state_hbm, state_ref, sems.at[0]),
        pltpu.make_async_copy(cond_hbm, cond_ref, sems.at[1]),
        pltpu.make_async_copy(small_hbm.at[pl.ds(0, SMALL)], small_ref, sems.at[5]),
    ]
    weights = [
        pltpu.make_async_copy(wqkv_hbm.at[which], w_ref, sems.at[2 + which])
        for which, w_ref in ((1, wk_ref), (2, wv_ref), (0, wq_ref))
    ]
    for copy in copies + weights[:1]:
        copy.start()
    copies[2].wait()
    gain = small_ref[2:3, :].astype(F32)
    own_segments(small_ref, seg_ref, own)
    build_masks((3, own // UNIT + 1), seg_ref, bias_ref)
    copies[0].wait()
    copies[1].wait()
    for copy in weights[1:]:
        copy.start()

    def hidden(at):
        return state_ref[at, :].astype(F32) + cond_ref[at, :].astype(F32)

    normalize(hidden, normed_ref, gain, 0, own)
    for w_ref, copy, out_ref in zip((wk_ref, wv_ref, wq_ref), weights, (k_ref, v_ref, q_ref)):
        copy.wait()
        project(normed_ref, w_ref, 0, own, out_ref, [(own, 0)])


def rest_kernel(
    cross_ref, core_ref, small_ref, state_ref, cond_ref, q_own, k_own, v_own, seg_own, bias_own,
    wqkv_hbm, wout_hbm,
    out_ref,
    wk_ref, wv_ref, wq_ref, wout, behind_ref, ahead_ref, halo_ref, h_ref, q_edge, k_edge, v_edge,
    normed_ref, q_ref, k_ref, v_ref, att_ref, seg_ref, bias_ref, range_ref, sems, *group_refs,
):
    own = state_ref.shape[0]
    units = own // UNIT
    end = BEHIND + own
    total = end + AHEAD
    weights = [
        pltpu.make_async_copy(wqkv_hbm.at[which], w_ref, sems.at[which])
        for which, w_ref in ((1, wk_ref), (2, wv_ref), (0, wq_ref))
    ]
    wout_copy = pltpu.make_async_copy(wout_hbm, wout, sems.at[3])
    for copy in weights + [wout_copy]:
        copy.start()
    gain = small_ref[2:3, :].astype(F32)
    even = lax.rem(lax.axis_index("seq"), 2) == 0

    bias_ref[3 : units + 1] = bias_own[3 : units + 1]
    attend(
        units - 2,
        lambda i: (i + 3, (i + 1) * UNIT, i * UNIT, (i + 3) * UNIT),
        q_own, k_own, v_own, att_ref, bias_ref, range_ref, group_refs,
    )

    def take(before, after):
        behind_ref[...] = before[...]
        ahead_ref[...] = after[...]

    @pl.when(even)
    def _():
        take(cross_ref, core_ref)

    @pl.when(jnp.logical_not(even))
    def _():
        take(core_ref, cross_ref)

    seg_ref[BEHIND:end, :] = seg_own[BEHIND:end, :]
    edge_segments(behind_ref, ahead_ref, seg_ref)
    for unit in (1, 2, units + 1, units + 2):
        build_mask(unit, seg_ref, bias_ref)
    for ref, rows, first in ((behind_ref, BEHIND, 0), (ahead_ref, AHEAD, BEHIND)):
        for at in range(0, rows, ROWS):
            h = ref[at : at + ROWS, :].astype(F32)
            scale = lax.rsqrt(jnp.mean(h * h, axis=-1, keepdims=True) + 1e-06)
            halo_ref[first + at : first + at + ROWS, :] = (h * scale * gain).astype(BF16)
    for ref, whole in ((k_edge, k_own), (v_edge, v_own)):
        ref[BEHIND:EDGE, :] = whole[0 : EDGE - BEHIND, :]
        ref[EDGE : EDGE + BEHIND, :] = whole[own - BEHIND : own, :]
    q_edge[UNIT : 2 * UNIT, :] = q_own[0:UNIT, :]
    q_edge[2 * UNIT : 3 * UNIT, :] = q_own[own - UNIT : own, :]
    clear_spare((k_edge, v_edge))
    both = [(BEHIND, 0), (AHEAD, EDGE + BEHIND)]
    weights[0].wait()
    project(halo_ref, wk_ref, 0, BEHIND + AHEAD, k_edge, both)
    weights[1].wait()
    project(halo_ref, wv_ref, 0, BEHIND + AHEAD, v_edge, both)
    weights[2].wait()
    project(halo_ref, wq_ref, UNIT, BEHIND + AHEAD, q_edge, [(UNIT, 0), (UNIT, 3 * UNIT)])

    def edge_unit(i):
        side = i // 2
        unit = i + 1 + side * (units - 2)
        return unit, i * UNIT, side * EDGE + (i - 2 * side) * UNIT, unit * UNIT

    attend(4, edge_unit, q_edge, k_edge, v_edge, att_ref, bias_ref, range_ref, group_refs)
    wout_copy.wait()
    depth = wout.shape[1]

    def first_velocity(cols):
        moved = 0.5 * jnp.dot(att_ref[UNIT:total, :], wout[:, cols], preferred_element_type=F32)
        moved = moved + 0.5 * small_ref[1:2, cols].astype(F32)
        h_ref[UNIT:BEHIND, cols] = behind_ref[UNIT:BEHIND, cols].astype(F32) + moved[:UNIT]
        h_ref[BEHIND:end, cols] = (
            state_ref[:, cols].astype(F32) + cond_ref[:, cols].astype(F32)
        ) + moved[UNIT : UNIT + own]
        h_ref[end:total, cols] = ahead_ref[0:AHEAD, cols].astype(F32) + moved[UNIT + own :]

    column_tiles(depth, first_velocity)
    normalize(lambda at: h_ref[at, :], normed_ref, gain, UNIT, total)
    project(normed_ref, wk_ref, UNIT, total, k_ref, [(total - UNIT, UNIT)])
    project(normed_ref, wv_ref, UNIT, total, v_ref, [(total - UNIT, UNIT)])
    project(normed_ref, wq_ref, BEHIND, end, q_ref, [(own, BEHIND)])
    attend(units, in_line(2), q_ref, k_ref, v_ref, att_ref, bias_ref, range_ref, group_refs)

    def second_velocity(cols):
        moved = jnp.dot(att_ref[BEHIND:end, :], wout[:, cols], preferred_element_type=F32)
        half_time = 0.5 * small_ref[1:2, cols].astype(F32)
        x = h_ref[BEHIND:end, cols] - cond_ref[:, cols].astype(F32) - half_time
        out_ref[:, cols] = (x + 0.5 * moved).astype(BF16)

    column_tiles(depth, second_velocity)


def clear_spare(refs):
    for ref in refs:
        ref[ref.shape[0] - SPARE :, :] = jnp.zeros((SPARE, ref.shape[1]), ref.dtype)


def one_step(
    final, h_ref, small_ref, behind_ref, ahead_ref, wqkv, wout,
    out_ref,
    normed_ref, q_ref, k_ref, v_ref, att_ref, seg_ref, bias_ref, range_ref, *group_refs,
):
    total = h_ref.shape[0]
    own = total - BEHIND - AHEAD
    kv_first = UNIT if final else 0
    first, last = (BEHIND, BEHIND + own) if final else (UNIT, total)
    own_segments(small_ref, seg_ref, own)
    edge_segments(behind_ref, ahead_ref, seg_ref)
    build_masks((1, total // UNIT), seg_ref, bias_ref)
    clear_spare((k_ref, v_ref))
    gain = small_ref[2:3, :].astype(F32)
    normalize(lambda at: h_ref[at, :], normed_ref, gain, kv_first, total)
    project(normed_ref, wqkv.at[1], kv_first, total, k_ref, [(total - kv_first, kv_first)])
    project(normed_ref, wqkv.at[2], kv_first, total, v_ref, [(total - kv_first, kv_first)])
    project(normed_ref, wqkv.at[0], first, last, q_ref, [(last - first, first)])
    attend(
        (last - first) // UNIT, in_line(first // UNIT),
        q_ref, k_ref, v_ref, att_ref, bias_ref, range_ref, group_refs,
    )
    for at in range(0, wout.shape[1], TILE):
        cols = slice(at, at + TILE)
        out_ref[:, cols] = jnp.dot(
            att_ref[first:last, :], wout[:, cols], preferred_element_type=F32
        ).astype(BF16)


def shards(state, condition, time_vector, norm_gain, w_qkv, w_out, utterance_ids):
    own, depth = state.shape
    width = w_qkv.shape[2]
    total = BEHIND + own + AHEAD
    parts = lax.axis_size("mp")
    count = lax.axis_size("seq")
    ids = utterance_ids.reshape(1, own)
    vmem = pl.BlockSpec(memory_space=pltpu.VMEM)
    hbm = pl.BlockSpec(memory_space=pltpu.HBM)

    def limit(mib):
        return pltpu.CompilerParams(vmem_limit_bytes=int(mib * 2**20))

    cross, core, small = pl.pallas_call(
        edge_kernel,
        out_shape=[jax.ShapeDtypeStruct((rows, depth), BF16) for rows in (PAYLOAD, PAYLOAD, 2 * own)],
        in_specs=[hbm] * 5,
        out_specs=[hbm] * 3,
        scratch_shapes=[pltpu.VMEM((PAYLOAD, depth), BF16)] * 2
        + [pltpu.VMEM((SMALL, depth), BF16)]
        + [pltpu.VMEM((BEHIND, depth), BF16)] * 2
        + [pltpu.VMEM((AHEAD, depth), BF16)] * 2
        + [pltpu.VMEM((1, own), jnp.int32)]
        + [pltpu.VMEM((depth,), BF16)] * 2
        + [pltpu.SemaphoreType.DMA((10,))],
        compiler_params=limit(EDGE_LIMIT),
    )(state, condition, ids, time_vector, norm_gain)
    ends = [(i, i + 1) for i in range(1, count - 1, 2)]
    cross = lax.ppermute(cross, "seq", ends + [(j, i) for i, j in ends])
    ends = [(i, i + 1) for i in range(0, count - 1, 2)]
    core = lax.ppermute(core, "seq", ends + [(j, i) for i, j in ends])

    work = [((total, depth), BF16), ((total, width), BF16)]
    work += [((total + SPARE, width), BF16)] * 2
    work += [
        ((total, width), BF16),
        ((total + SPARE, 128), F32),
        ((total // UNIT, UNIT, WINDOW), F32),
        ((2, UNIT, PAIR), F32),
    ]
    groups = [((FOUR * UNIT, WINDOW), kind) for kind in (F32, BF16) for _ in range(width // (FOUR * HEAD_DIM))]
    groups = [pltpu.VMEM(*one) for one in groups]
    if parts == 1:
        kept = [((SMALL, depth), BF16)] + [(state.shape, BF16)] * 2 + [((own, width), BF16)] * 3
        kept += [((total + SPARE, 128), F32), ((total // UNIT, UNIT, WINDOW), F32)]
        kept = pl.pallas_call(
            own_kernel,
            out_shape=[jax.ShapeDtypeStruct(*one) for one in kept],
            in_specs=[hbm] * 4,
            out_specs=[vmem] * 8,
            scratch_shapes=[pltpu.VMEM((depth, width), BF16)] * 3
            + [pltpu.VMEM((own, depth), BF16), pltpu.SemaphoreType.DMA((6,))],
            compiler_params=limit(OWN_LIMIT),
            cost_estimate=pl.CostEstimate(
                flops=6 * own * depth * width, bytes_accessed=2 * 4 * depth * width, transcendentals=0
            ),
        )(small, state, condition, w_qkv)
        first = [((depth, width), BF16)] * 3 + [(w_out.shape, BF16)] + [((PAYLOAD, depth), BF16)] * 2
        first += [((BEHIND + AHEAD, depth), BF16), ((total, depth), F32)]
        first += [((4 * UNIT, width), BF16)] + [((2 * EDGE, width), BF16)] * 2
        return pl.pallas_call(
            rest_kernel,
            out_shape=jax.ShapeDtypeStruct((own, depth), BF16),
            in_specs=[vmem] * 10 + [hbm] * 2,
            out_specs=vmem,
            scratch_shapes=[pltpu.VMEM(*one) for one in first + work]
            + [pltpu.SemaphoreType.DMA((4,))]
            + groups,
            compiler_params=limit(LIMIT),
        )(cross, core, *kept, w_qkv, w_out)

    even = lax.axis_index("seq") % 2 == 0
    small = small[:SMALL]
    behind = jnp.where(even, cross, core)
    ahead = jnp.where(even, core, cross)

    def terms(h, final):
        rows = own if final else total - UNIT
        mine = pl.pallas_call(
            functools.partial(one_step, final),
            out_shape=jax.ShapeDtypeStruct((rows, depth), BF16),
            in_specs=[vmem] * 6,
            out_specs=vmem,
            scratch_shapes=[pltpu.VMEM(*one) for one in work] + groups,
            compiler_params=limit(LIMIT),
        )(h, small, behind, ahead, w_qkv, w_out)
        return lax.psum(mine, "mp").astype(F32)

    start = state.astype(F32)
    h = jnp.concatenate(
        [behind[:BEHIND].astype(F32), start + condition.astype(F32), ahead[:AHEAD].astype(F32)]
    )
    velocity = terms(h, False)
    later = jnp.pad(velocity, ((UNIT, 0), (0, 0))) * 0.5 + 0.5 * time_vector.astype(F32)
    x = start + 0.5 * velocity[UNIT : UNIT + own] + 0.5 * terms(h + later, True)
    share = depth // parts
    mine = lax.dynamic_slice_in_dim(x, lax.axis_index("mp") * share, share, 1)
    return mine.astype(BF16)


def solution(mesh):
    in_specs = (
        P("seq", None),
        P("seq", None),
        P(),
        P(),
        P(None, None, "mp"),
        P("mp", None),
        P("seq"),
    )
    out_specs = P("seq", "mp")
    return jax.shard_map(shards, mesh=mesh, in_specs=in_specs, out_specs=out_specs, check_vma=False)
```

```python
import functools
import math

import jax
import jax.numpy as jnp
from jax import lax
from jax.experimental import pallas as pl
from jax.experimental.pallas import tpu as pltpu
from jax.sharding import PartitionSpec as P

HEAD_DIM = 64
BLOCK = 24
UNIT = 2 * BLOCK
BEHIND = 4 * BLOCK
AHEAD = 2 * BLOCK
WINDOW = 128
SPARE = WINDOW - 2 * UNIT
EDGE = UNIT + WINDOW
PAIR = 2 * HEAD_DIM
MANY = 8
FOUR = 4
SUM_LOW, SUM_HIGH = 2.0**-60, 2.0**100
SMALL = 16
PAYLOAD = BEHIND + 16
TILE = 256
ROWS = 16
MANY_ROWS = 640
EDGE_LIMIT, OWN_LIMIT, LIMIT = 56, 48, 48
F32 = jnp.float32
BF16 = jnp.bfloat16
NEG = -1e30


def column_of(row):
    n = row.shape[1]
    same = lax.broadcasted_iota(jnp.int32, (n, n), 0) == lax.broadcasted_iota(jnp.int32, (n, n), 1)
    column = jnp.sum(jnp.where(same, row, 0.0), axis=1, keepdims=True)
    return jnp.broadcast_to(column, (n, 128))


def own_segments(small_ref, seg_ref, own):
    for at in range(0, own, 128):
        n = min(128, own - at)
        row = small_ref[0:1, at : at + n].astype(F32)
        seg_ref[BEHIND + at : BEHIND + at + n, :] = column_of(row)


def edge_segments(behind_ref, ahead_ref, seg_ref):
    end = seg_ref.shape[0] - SPARE
    seg_ref[0:BEHIND, :] = column_of(behind_ref[BEHIND : BEHIND + 1, 0:BEHIND].astype(F32))
    seg_ref[end - AHEAD : end, :] = column_of(ahead_ref[BEHIND : BEHIND + 1, 0:AHEAD].astype(F32))
    seg_ref[end : end + SPARE, :] = jnp.full((SPARE, 128), -1.0, F32)


def build_mask(unit, seg_ref, bias_ref):
    start = unit * UNIT
    if not isinstance(unit, int):
        start = pl.multiple_of(start, 16)
    window = seg_ref[pl.ds(start - UNIT, WINDOW), :]
    r = lax.broadcasted_iota(jnp.int32, (WINDOW, WINDOW), 0)
    c = lax.broadcasted_iota(jnp.int32, (WINDOW, WINDOW), 1)
    keys = jnp.sum(jnp.where(r == c, window, 0.0), axis=0, keepdims=True)
    queries = seg_ref[pl.ds(start, UNIT), :]
    row = lax.broadcasted_iota(jnp.int32, (UNIT, WINDOW), 0)
    col = lax.broadcasted_iota(jnp.int32, (UNIT, WINDOW), 1)
    first = jnp.where(row < BLOCK, 0, BLOCK)
    band = (col >= first) & (col < first + 4 * BLOCK)
    bias_ref[unit] = jnp.where(band & (queries == keys), 0.0, NEG)


def build_masks(units, seg_ref, bias_ref):
    for unit in range(*units):
        build_mask(unit, seg_ref, bias_ref)


def normalize(load, normed_ref, gain, first, last):
    groups = (last - first) // ROWS
    many = max(n for n in range(1, MANY_ROWS // ROWS + 1) if groups % n == 0)

    def one(i, carry):
        for j in range(many):
            start = first + (i * many + j) * ROWS
            at = pl.ds(start if isinstance(start, int) else pl.multiple_of(start, ROWS), ROWS)
            h = load(at)
            scale = lax.rsqrt(jnp.mean(h * h, axis=-1, keepdims=True) + 1e-06)
            normed_ref[at, :] = (h * scale * gain).astype(BF16)
        return carry

    if groups == many:
        one(0, 0)
    else:
        lax.fori_loop(0, groups // many, one, 0)


def project(normed_ref, w_ref, first, last, out_ref, places):
    width = w_ref.shape[1]
    tile = min(TILE, width)
    for at in range(0, width, tile):
        cols = slice(at, at + tile)
        out = jnp.dot(
            normed_ref[first:last, :], w_ref[:, cols], preferred_element_type=F32
        ).astype(BF16)
        done = 0
        for rows, place in places:
            out_ref[place : place + rows, cols] = out[done : done + rows]
            done += rows


def attend(count, place, q_ref, k_ref, v_ref, att_ref, bias_ref, range_ref, group_refs):
    wide = FOUR * HEAD_DIM
    groups = q_ref.shape[1] // wide
    factor = HEAD_DIM**-0.5 * math.log2(math.e)

    def row(start):
        return start if isinstance(start, int) else pl.multiple_of(start, 16)

    score_refs, prob_refs = group_refs[:groups], group_refs[groups:]

    def score(i, g):
        _, q_row, kv_row, _ = place(i)
        rows, window = pl.ds(row(q_row), UNIT), pl.ds(row(kv_row), WINDOW)
        head = lax.broadcasted_iota(jnp.int32, (UNIT, wide), 1) // HEAD_DIM
        lanes = slice(g * wide, (g + 1) * wide)
        q = q_ref[rows, lanes]
        zero = jnp.zeros_like(q)
        stacked = jnp.concatenate([jnp.where(head == j, q, zero) for j in range(FOUR)], axis=0)
        score_refs[g][...] = lax.dot_general(
            stacked, k_ref[window, lanes], (((1,), (1,)), ((), ())), preferred_element_type=F32
        )

    def soften(i, g, shift=False):
        bias = bias_ref[place(i)[0]]
        low, high = range_ref[0], range_ref[1]
        for j in range(FOUR):
            rows = slice(j * UNIT, (j + 1) * UNIT)
            s = score_refs[g][rows, :] * factor + bias
            if shift:
                s = s - jnp.max(s, axis=-1, keepdims=True)
            expo = jnp.exp2(s)
            total = jnp.sum(expo, axis=-1, keepdims=True)
            low, high = jnp.minimum(low, total), jnp.maximum(high, total)
            prob_refs[g][rows, :] = (expo * pl.reciprocal(total, approx=True)).astype(BF16)
        range_ref[0] = low
        range_ref[1] = high

    def mix(i, g):
        _, _, kv_row, att_row = place(i)
        rows, window = pl.ds(row(att_row), UNIT), pl.ds(row(kv_row), WINDOW)
        one = lax.broadcasted_iota(jnp.int32, (UNIT, PAIR), 1) < HEAD_DIM
        lanes = slice(g * wide, (g + 1) * wide)
        out = jnp.dot(prob_refs[g][...], v_ref[window, lanes], preferred_element_type=F32)
        for p in range(FOUR // 2):
            low, high = 2 * p * UNIT, (2 * p + 1) * UNIT
            cols = slice(p * PAIR, (p + 1) * PAIR)
            mixed = jnp.where(one, out[low : low + UNIT, cols], out[high : high + UNIT, cols])
            att_ref[rows, g * wide + p * PAIR : g * wide + (p + 1) * PAIR] = mixed.astype(BF16)

    def stages(mixed=None, softened=None, scored=None):
        for g in range(groups):
            if mixed is not None:
                mix(mixed, g)
            if softened is not None:
                soften(softened, g)
            if scored is not None:
                score(scored, g)

    range_ref[...] = jnp.ones_like(range_ref)
    stages(scored=0)
    stages(softened=0, scored=1)
    steady = count - 2
    many = max(n for n in range(1, MANY + 1) if steady % n == 0)

    def one(i, carry):
        for j in range(many):
            stages(i * many + j, i * many + j + 1, i * many + j + 2)
        return carry

    if steady == many:
        one(0, 0)
    else:
        lax.fori_loop(0, steady // many, one, 0)
    stages(mixed=count - 2, softened=count - 1)
    stages(mixed=count - 1)
    fine = (jnp.min(range_ref[0]) >= SUM_LOW) & (jnp.max(range_ref[1]) <= SUM_HIGH)

    @pl.when(jnp.logical_not(fine))
    def _():
        def shifted(i, carry):
            for g in range(groups):
                score(i, g)
                soften(i, g, shift=True)
                mix(i, g)
            return carry

        lax.fori_loop(0, count, shifted, 0)


def in_line(first):
    return lambda i: (first + i, (first + i) * UNIT, (first + i - 1) * UNIT, (first + i) * UNIT)


def edge_kernel(
    state_hbm, cond_hbm, ids_hbm, time_hbm, gain_hbm,
    cross_hbm, core_hbm, small_hbm,
    cross_ref, core_ref, small_ref, state_last, cond_last, state_first, cond_first, ids_ref, time_ref, gain_ref, sems,
):
    own = state_hbm.shape[0]
    copies = [
        pltpu.make_async_copy(source, target, sems.at[i])
        for i, (source, target) in enumerate(
            (
                (state_hbm.at[pl.ds(own - BEHIND, BEHIND)], state_last),
                (cond_hbm.at[pl.ds(own - BEHIND, BEHIND)], cond_last),
                (state_hbm.at[pl.ds(0, AHEAD)], state_first),
                (cond_hbm.at[pl.ds(0, AHEAD)], cond_first),
                (ids_hbm, ids_ref),
                (time_hbm, time_ref),
                (gain_hbm, gain_ref),
            )
        )
    ]
    for copy in copies:
        copy.start()
    even = lax.rem(lax.axis_index("seq"), 2) == 0
    for copy in copies:
        copy.wait()

    depth = core_ref.shape[1]

    def number_row(ids):
        blank = jnp.zeros((1, depth - ids.shape[1]), F32)
        return jnp.concatenate([(ids + 1).astype(F32), blank], axis=1)

    vectors = [ref[...].astype(F32).reshape(1, -1) for ref in (time_ref, gain_ref)]
    blank = jnp.zeros((SMALL - 3, depth), F32)
    small_ref[...] = jnp.concatenate([number_row(ids_ref[...]), *vectors, blank], axis=0).astype(BF16)
    leaving = [
        pltpu.make_async_copy(small_ref, small_hbm.at[pl.ds(0, SMALL)], sems.at[7]),
        pltpu.make_async_copy(cross_ref, cross_hbm, sems.at[8]),
        pltpu.make_async_copy(core_ref, core_hbm, sems.at[9]),
    ]
    leaving[0].start()

    def fill(ref, state, cond, ids):
        rows = state.shape[0]
        ref[0:rows, :] = (state[...].astype(F32) + cond[...].astype(F32)).astype(BF16)
        if rows < BEHIND:
            ref[rows:BEHIND, :] = jnp.zeros((BEHIND - rows, depth), BF16)
        ref[BEHIND:, :] = jnp.broadcast_to(number_row(ids), (PAYLOAD - BEHIND, depth)).astype(BF16)

    def fill_both(to_next, to_previous):
        fill(to_next, state_last, cond_last, ids_ref[:, own - BEHIND :])
        fill(to_previous, state_first, cond_first, ids_ref[:, :BEHIND])

    @pl.when(even)
    def _():
        fill_both(core_ref, cross_ref)

    @pl.when(jnp.logical_not(even))
    def _():
        fill_both(cross_ref, core_ref)

    leaving[1].start()
    leaving[2].start()
    for copy in leaving:
        copy.wait()


def own_kernel(
    small_hbm, state_hbm, cond_hbm, wqkv_hbm,
    small_ref, state_ref, cond_ref, q_ref, k_ref, v_ref, seg_ref, bias_ref,
    wk_ref, wv_ref, wq_ref, normed_ref, sems,
):
    own = state_ref.shape[0]
    copies = [
        pltpu.make_async_copy(state_hbm, state_ref, sems.at[0]),
        pltpu.make_async_copy(cond_hbm, cond_ref, sems.at[1]),
        pltpu.make_async_copy(small_hbm.at[pl.ds(0, SMALL)], small_ref, sems.at[5]),
    ]
    weights = [
        pltpu.make_async_copy(wqkv_hbm.at[which], w_ref, sems.at[2 + which])
        for which, w_ref in ((1, wk_ref), (2, wv_ref), (0, wq_ref))
    ]
    for copy in copies + weights[:1]:
        copy.start()
    copies[2].wait()
    gain = small_ref[2:3, :].astype(F32)
    own_segments(small_ref, seg_ref, own)
    build_masks((3, own // UNIT + 1), seg_ref, bias_ref)
    copies[0].wait()
    copies[1].wait()
    for copy in weights[1:]:
        copy.start()

    def hidden(at):
        return state_ref[at, :].astype(F32) + cond_ref[at, :].astype(F32)

    normalize(hidden, normed_ref, gain, 0, own)
    for w_ref, copy, out_ref in zip((wk_ref, wv_ref, wq_ref), weights, (k_ref, v_ref, q_ref)):
        copy.wait()
        project(normed_ref, w_ref, 0, own, out_ref, [(own, 0)])


def rest_kernel(
    cross_ref, core_ref, small_ref, state_ref, cond_ref, q_own, k_own, v_own, seg_own, bias_own,
    wqkv_hbm, wout_hbm,
    out_ref,
    wk_ref, wv_ref, wq_ref, wout, behind_ref, ahead_ref, halo_ref, h_ref, q_edge, k_edge, v_edge,
    normed_ref, q_ref, k_ref, v_ref, att_ref, seg_ref, bias_ref, range_ref, sems, *group_refs,
):
    own = state_ref.shape[0]
    units = own // UNIT
    end = BEHIND + own
    total = end + AHEAD
    weights = [
        pltpu.make_async_copy(wqkv_hbm.at[which], w_ref, sems.at[which])
        for which, w_ref in ((1, wk_ref), (2, wv_ref), (0, wq_ref))
    ]
    wout_copy = pltpu.make_async_copy(wout_hbm, wout, sems.at[3])
    for copy in weights:
        copy.start()
    half_time = 0.5 * small_ref[1:2, :].astype(F32)
    gain = small_ref[2:3, :].astype(F32)
    even = lax.rem(lax.axis_index("seq"), 2) == 0

    bias_ref[3 : units + 1] = bias_own[3 : units + 1]
    attend(
        units - 2,
        lambda i: (i + 3, (i + 1) * UNIT, i * UNIT, (i + 3) * UNIT),
        q_own, k_own, v_own, att_ref, bias_ref, range_ref, group_refs,
    )

    def take(before, after):
        behind_ref[...] = before[...]
        ahead_ref[...] = after[...]

    @pl.when(even)
    def _():
        take(cross_ref, core_ref)

    @pl.when(jnp.logical_not(even))
    def _():
        take(core_ref, cross_ref)

    seg_ref[BEHIND:end, :] = seg_own[BEHIND:end, :]
    edge_segments(behind_ref, ahead_ref, seg_ref)
    for unit in (1, 2, units + 1, units + 2):
        build_mask(unit, seg_ref, bias_ref)
    for ref, rows, first in ((behind_ref, BEHIND, 0), (ahead_ref, AHEAD, BEHIND)):
        for at in range(0, rows, ROWS):
            h = ref[at : at + ROWS, :].astype(F32)
            scale = lax.rsqrt(jnp.mean(h * h, axis=-1, keepdims=True) + 1e-06)
            halo_ref[first + at : first + at + ROWS, :] = (h * scale * gain).astype(BF16)
    for ref, whole in ((k_edge, k_own), (v_edge, v_own)):
        ref[BEHIND:EDGE, :] = whole[0 : EDGE - BEHIND, :]
        ref[EDGE : EDGE + BEHIND, :] = whole[own - BEHIND : own, :]
    q_edge[UNIT : 2 * UNIT, :] = q_own[0:UNIT, :]
    q_edge[2 * UNIT : 3 * UNIT, :] = q_own[own - UNIT : own, :]
    clear_spare((k_edge, v_edge))
    both = [(BEHIND, 0), (AHEAD, EDGE + BEHIND)]
    weights[0].wait()
    wout_copy.start()
    project(halo_ref, wk_ref, 0, BEHIND + AHEAD, k_edge, both)
    weights[1].wait()
    project(halo_ref, wv_ref, 0, BEHIND + AHEAD, v_edge, both)
    weights[2].wait()
    project(halo_ref, wq_ref, UNIT, BEHIND + AHEAD, q_edge, [(UNIT, 0), (UNIT, 3 * UNIT)])

    def edge_unit(i):
        side = i // 2
        unit = i + 1 + side * (units - 2)
        return unit, i * UNIT, side * EDGE + (i - 2 * side) * UNIT, unit * UNIT

    attend(4, edge_unit, q_edge, k_edge, v_edge, att_ref, bias_ref, range_ref, group_refs)
    wout_copy.wait()
    depth = wout.shape[1]
    for at in range(0, depth, TILE):
        cols = slice(at, at + TILE)
        moved = 0.5 * jnp.dot(att_ref[UNIT:total, :], wout[:, cols], preferred_element_type=F32)
        moved = moved + half_time[:, cols]
        h_ref[UNIT:BEHIND, cols] = behind_ref[UNIT:BEHIND, cols].astype(F32) + moved[:UNIT]
        h_ref[BEHIND:end, cols] = (
            state_ref[:, cols].astype(F32) + cond_ref[:, cols].astype(F32)
        ) + moved[UNIT : UNIT + own]
        h_ref[end:total, cols] = ahead_ref[0:AHEAD, cols].astype(F32) + moved[UNIT + own :]

    normalize(lambda at: h_ref[at, :], normed_ref, gain, UNIT, total)
    project(normed_ref, wk_ref, UNIT, total, k_ref, [(total - UNIT, UNIT)])
    project(normed_ref, wv_ref, UNIT, total, v_ref, [(total - UNIT, UNIT)])
    project(normed_ref, wq_ref, BEHIND, end, q_ref, [(own, BEHIND)])
    attend(units, in_line(2), q_ref, k_ref, v_ref, att_ref, bias_ref, range_ref, group_refs)
    for at in range(0, depth, TILE):
        cols = slice(at, at + TILE)
        moved = jnp.dot(att_ref[BEHIND:end, :], wout[:, cols], preferred_element_type=F32)
        x = h_ref[BEHIND:end, cols] - cond_ref[:, cols].astype(F32) - half_time[:, cols]
        out_ref[:, cols] = (x + 0.5 * moved).astype(BF16)


def clear_spare(refs):
    for ref in refs:
        ref[ref.shape[0] - SPARE :, :] = jnp.zeros((SPARE, ref.shape[1]), ref.dtype)


def one_step(
    final, h_ref, small_ref, behind_ref, ahead_ref, wqkv, wout,
    out_ref,
    normed_ref, q_ref, k_ref, v_ref, att_ref, seg_ref, bias_ref, range_ref, *group_refs,
):
    total = h_ref.shape[0]
    own = total - BEHIND - AHEAD
    kv_first = UNIT if final else 0
    first, last = (BEHIND, BEHIND + own) if final else (UNIT, total)
    own_segments(small_ref, seg_ref, own)
    edge_segments(behind_ref, ahead_ref, seg_ref)
    build_masks((1, total // UNIT), seg_ref, bias_ref)
    clear_spare((k_ref, v_ref))
    gain = small_ref[2:3, :].astype(F32)
    normalize(lambda at: h_ref[at, :], normed_ref, gain, kv_first, total)
    project(normed_ref, wqkv.at[1], kv_first, total, k_ref, [(total - kv_first, kv_first)])
    project(normed_ref, wqkv.at[2], kv_first, total, v_ref, [(total - kv_first, kv_first)])
    project(normed_ref, wqkv.at[0], first, last, q_ref, [(last - first, first)])
    attend(
        (last - first) // UNIT, in_line(first // UNIT),
        q_ref, k_ref, v_ref, att_ref, bias_ref, range_ref, group_refs,
    )
    for at in range(0, wout.shape[1], TILE):
        cols = slice(at, at + TILE)
        out_ref[:, cols] = jnp.dot(
            att_ref[first:last, :], wout[:, cols], preferred_element_type=F32
        ).astype(BF16)


def shards(state, condition, time_vector, norm_gain, w_qkv, w_out, utterance_ids):
    own, depth = state.shape
    width = w_qkv.shape[2]
    total = BEHIND + own + AHEAD
    parts = lax.axis_size("mp")
    count = lax.axis_size("seq")
    ids = utterance_ids.reshape(1, own)
    vmem = pl.BlockSpec(memory_space=pltpu.VMEM)
    hbm = pl.BlockSpec(memory_space=pltpu.HBM)

    def limit(mib):
        return pltpu.CompilerParams(vmem_limit_bytes=int(mib * 2**20))

    cross, core, small = pl.pallas_call(
        edge_kernel,
        out_shape=[jax.ShapeDtypeStruct((rows, depth), BF16) for rows in (PAYLOAD, PAYLOAD, 2 * own)],
        in_specs=[hbm] * 5,
        out_specs=[hbm] * 3,
        scratch_shapes=[pltpu.VMEM((PAYLOAD, depth), BF16)] * 2
        + [pltpu.VMEM((SMALL, depth), BF16)]
        + [pltpu.VMEM((BEHIND, depth), BF16)] * 2
        + [pltpu.VMEM((AHEAD, depth), BF16)] * 2
        + [pltpu.VMEM((1, own), jnp.int32)]
        + [pltpu.VMEM((depth,), BF16)] * 2
        + [pltpu.SemaphoreType.DMA((10,))],
        compiler_params=limit(EDGE_LIMIT),
    )(state, condition, ids, time_vector, norm_gain)
    ends = [(i, i + 1) for i in range(1, count - 1, 2)]
    cross = lax.ppermute(cross, "seq", ends + [(j, i) for i, j in ends])
    ends = [(i, i + 1) for i in range(0, count - 1, 2)]
    core = lax.ppermute(core, "seq", ends + [(j, i) for i, j in ends])

    work = [((total, depth), BF16), ((total, width), BF16)]
    work += [((total + SPARE, width), BF16)] * 2
    work += [
        ((total, width), BF16),
        ((total + SPARE, 128), F32),
        ((total // UNIT, UNIT, WINDOW), F32),
        ((2, UNIT, PAIR), F32),
    ]
    groups = [((FOUR * UNIT, WINDOW), kind) for kind in (F32, BF16) for _ in range(width // (FOUR * HEAD_DIM))]
    groups = [pltpu.VMEM(*one) for one in groups]
    if parts == 1:
        kept = [((SMALL, depth), BF16)] + [(state.shape, BF16)] * 2 + [((own, width), BF16)] * 3
        kept += [((total + SPARE, 128), F32), ((total // UNIT, UNIT, WINDOW), F32)]
        kept = pl.pallas_call(
            own_kernel,
            out_shape=[jax.ShapeDtypeStruct(*one) for one in kept],
            in_specs=[hbm] * 4,
            out_specs=[vmem] * 8,
            scratch_shapes=[pltpu.VMEM((depth, width), BF16)] * 3
            + [pltpu.VMEM((own, depth), BF16), pltpu.SemaphoreType.DMA((6,))],
            compiler_params=limit(OWN_LIMIT),
            cost_estimate=pl.CostEstimate(
                flops=6 * own * depth * width, bytes_accessed=2 * 4 * depth * width, transcendentals=0
            ),
        )(small, state, condition, w_qkv)
        first = [((depth, width), BF16)] * 3 + [(w_out.shape, BF16)] + [((PAYLOAD, depth), BF16)] * 2
        first += [((BEHIND + AHEAD, depth), BF16), ((total, depth), F32)]
        first += [((4 * UNIT, width), BF16)] + [((2 * EDGE, width), BF16)] * 2
        return pl.pallas_call(
            rest_kernel,
            out_shape=jax.ShapeDtypeStruct((own, depth), BF16),
            in_specs=[vmem] * 10 + [hbm] * 2,
            out_specs=vmem,
            scratch_shapes=[pltpu.VMEM(*one) for one in first + work]
            + [pltpu.SemaphoreType.DMA((4,))]
            + groups,
            compiler_params=limit(LIMIT),
        )(cross, core, *kept, w_qkv, w_out)

    even = lax.axis_index("seq") % 2 == 0
    small = small[:SMALL]
    behind = jnp.where(even, cross, core)
    ahead = jnp.where(even, core, cross)

    def terms(h, final):
        rows = own if final else total - UNIT
        mine = pl.pallas_call(
            functools.partial(one_step, final),
            out_shape=jax.ShapeDtypeStruct((rows, depth), BF16),
            in_specs=[vmem] * 6,
            out_specs=vmem,
            scratch_shapes=[pltpu.VMEM(*one) for one in work] + groups,
            compiler_params=limit(LIMIT),
        )(h, small, behind, ahead, w_qkv, w_out)
        return lax.psum(mine, "mp").astype(F32)

    start = state.astype(F32)
    h = jnp.concatenate(
        [behind[:BEHIND].astype(F32), start + condition.astype(F32), ahead[:AHEAD].astype(F32)]
    )
    velocity = terms(h, False)
    later = jnp.pad(velocity, ((UNIT, 0), (0, 0))) * 0.5 + 0.5 * time_vector.astype(F32)
    x = start + 0.5 * velocity[UNIT : UNIT + own] + 0.5 * terms(h + later, True)
    share = depth // parts
    mine = lax.dynamic_slice_in_dim(x, lax.axis_index("mp") * share, share, 1)
    return mine.astype(BF16)


def solution(mesh):
    in_specs = (
        P("seq", None),
        P("seq", None),
        P(),
        P(),
        P(None, None, "mp"),
        P("mp", None),
        P("seq"),
    )
    out_specs = P("seq", "mp")
    return jax.shard_map(shards, mesh=mesh, in_specs=in_specs, out_specs=out_specs, check_vma=False)
```

```python
import functools
import math

import jax
import jax.numpy as jnp
from jax import lax
from jax.experimental import pallas as pl
from jax.experimental.pallas import tpu as pltpu
from jax.sharding import PartitionSpec as P

HEAD_DIM = 64
BLOCK = 24
UNIT = 2 * BLOCK
BEHIND = 4 * BLOCK
AHEAD = 2 * BLOCK
WINDOW = 128
SPARE = WINDOW - 2 * UNIT
EDGE = UNIT + WINDOW
PAIR = 2 * HEAD_DIM
MANY = 8
FOUR = 4
SUM_LOW, SUM_HIGH = 2.0**-60, 2.0**100
SMALL = 16
PAYLOAD = BEHIND + 16
TILE = 256
ROWS = 16
MANY_ROWS = 640
EDGE_LIMIT, OWN_LIMIT, LIMIT = 56, 48, 48
F32 = jnp.float32
BF16 = jnp.bfloat16
NEG = -1e30


def column_of(row):
    n = row.shape[1]
    same = lax.broadcasted_iota(jnp.int32, (n, n), 0) == lax.broadcasted_iota(jnp.int32, (n, n), 1)
    column = jnp.sum(jnp.where(same, row, 0.0), axis=1, keepdims=True)
    return jnp.broadcast_to(column, (n, 128))


def own_segments(small_ref, seg_ref, own):
    for at in range(0, own, 128):
        n = min(128, own - at)
        row = small_ref[0:1, at : at + n].astype(F32)
        seg_ref[BEHIND + at : BEHIND + at + n, :] = column_of(row)


def edge_segments(behind_ref, ahead_ref, seg_ref):
    end = seg_ref.shape[0] - SPARE
    seg_ref[0:BEHIND, :] = column_of(behind_ref[BEHIND : BEHIND + 1, 0:BEHIND].astype(F32))
    seg_ref[end - AHEAD : end, :] = column_of(ahead_ref[BEHIND : BEHIND + 1, 0:AHEAD].astype(F32))
    seg_ref[end : end + SPARE, :] = jnp.full((SPARE, 128), -1.0, F32)


def build_mask(unit, seg_ref, bias_ref):
    start = unit * UNIT
    if not isinstance(unit, int):
        start = pl.multiple_of(start, 16)
    window = seg_ref[pl.ds(start - UNIT, WINDOW), :]
    r = lax.broadcasted_iota(jnp.int32, (WINDOW, WINDOW), 0)
    c = lax.broadcasted_iota(jnp.int32, (WINDOW, WINDOW), 1)
    keys = jnp.sum(jnp.where(r == c, window, 0.0), axis=0, keepdims=True)
    queries = seg_ref[pl.ds(start, UNIT), :]
    row = lax.broadcasted_iota(jnp.int32, (UNIT, WINDOW), 0)
    col = lax.broadcasted_iota(jnp.int32, (UNIT, WINDOW), 1)
    first = jnp.where(row < BLOCK, 0, BLOCK)
    band = (col >= first) & (col < first + 4 * BLOCK)
    bias_ref[unit] = jnp.where(band & (queries == keys), 0.0, NEG)


def build_masks(units, seg_ref, bias_ref):
    for unit in range(*units):
        build_mask(unit, seg_ref, bias_ref)


def normalize(load, normed_ref, gain, first, last):
    groups = (last - first) // ROWS
    many = max(n for n in range(1, MANY_ROWS // ROWS + 1) if groups % n == 0)

    def one(i, carry):
        for j in range(many):
            start = first + (i * many + j) * ROWS
            at = pl.ds(start if isinstance(start, int) else pl.multiple_of(start, ROWS), ROWS)
            h = load(at)
            scale = lax.rsqrt(jnp.mean(h * h, axis=-1, keepdims=True) + 1e-06)
            normed_ref[at, :] = (h * scale * gain).astype(BF16)
        return carry

    if groups == many:
        one(0, 0)
    else:
        lax.fori_loop(0, groups // many, one, 0)


def project(normed_ref, w_ref, first, last, out_ref, places):
    width = w_ref.shape[1]
    tile = min(TILE, width)
    for at in range(0, width, tile):
        cols = slice(at, at + tile)
        out = jnp.dot(
            normed_ref[first:last, :], w_ref[:, cols], preferred_element_type=F32
        ).astype(BF16)
        done = 0
        for rows, place in places:
            out_ref[place : place + rows, cols] = out[done : done + rows]
            done += rows


def attend(count, place, q_ref, k_ref, v_ref, att_ref, bias_ref, range_ref, group_refs, shift=False):
    wide = FOUR * HEAD_DIM
    groups = q_ref.shape[1] // wide
    factor = HEAD_DIM**-0.5 * math.log2(math.e)

    def row(start):
        return start if isinstance(start, int) else pl.multiple_of(start, 16)

    score_refs, prob_refs = group_refs[:groups], group_refs[groups:]

    def score(i, g):
        _, q_row, kv_row, _ = place(i)
        rows, window = pl.ds(row(q_row), UNIT), pl.ds(row(kv_row), WINDOW)
        head = lax.broadcasted_iota(jnp.int32, (UNIT, wide), 1) // HEAD_DIM
        lanes = slice(g * wide, (g + 1) * wide)
        q = q_ref[rows, lanes]
        zero = jnp.zeros_like(q)
        stacked = jnp.concatenate([jnp.where(head == j, q, zero) for j in range(FOUR)], axis=0)
        score_refs[g][...] = lax.dot_general(
            stacked, k_ref[window, lanes], (((1,), (1,)), ((), ())), preferred_element_type=F32
        )

    def soften(i, g):
        bias = bias_ref[place(i)[0]]
        low, high = range_ref[0], range_ref[1]
        for j in range(FOUR):
            rows = slice(j * UNIT, (j + 1) * UNIT)
            s = score_refs[g][rows, :] * factor + bias
            if shift:
                s = s - jnp.max(s, axis=-1, keepdims=True)
            expo = jnp.exp2(s)
            total = jnp.sum(expo, axis=-1, keepdims=True)
            low, high = jnp.minimum(low, total), jnp.maximum(high, total)
            prob_refs[g][rows, :] = (expo * pl.reciprocal(total, approx=True)).astype(BF16)
        range_ref[0] = low
        range_ref[1] = high

    def mix(i, g):
        _, _, kv_row, att_row = place(i)
        rows, window = pl.ds(row(att_row), UNIT), pl.ds(row(kv_row), WINDOW)
        one = lax.broadcasted_iota(jnp.int32, (UNIT, PAIR), 1) < HEAD_DIM
        lanes = slice(g * wide, (g + 1) * wide)
        out = jnp.dot(prob_refs[g][...], v_ref[window, lanes], preferred_element_type=F32)
        for p in range(FOUR // 2):
            low, high = 2 * p * UNIT, (2 * p + 1) * UNIT
            cols = slice(p * PAIR, (p + 1) * PAIR)
            mixed = jnp.where(one, out[low : low + UNIT, cols], out[high : high + UNIT, cols])
            att_ref[rows, g * wide + p * PAIR : g * wide + (p + 1) * PAIR] = mixed.astype(BF16)

    def stages(mixed=None, softened=None, scored=None):
        for g in range(groups):
            if mixed is not None:
                mix(mixed, g)
            if softened is not None:
                soften(softened, g)
            if scored is not None:
                score(scored, g)

    if shift:

        def all_stages(i, carry):
            for g in range(groups):
                score(i, g)
                soften(i, g)
                mix(i, g)
            return carry

        lax.fori_loop(0, count, all_stages, 0)
        return

    stages(scored=0)
    stages(softened=0, scored=1)
    steady = count - 2
    many = max(n for n in range(1, MANY + 1) if steady % n == 0)

    def one(i, carry):
        for j in range(many):
            stages(i * many + j, i * many + j + 1, i * many + j + 2)
        return carry

    if steady == many:
        one(0, 0)
    else:
        lax.fori_loop(0, steady // many, one, 0)
    stages(mixed=count - 2, softened=count - 1)
    stages(mixed=count - 1)


def unshifted_first(range_ref, parts, between=None):
    range_ref[...] = jnp.ones_like(range_ref)
    for i, part in enumerate(parts):
        if i > 0:
            between()
        part(False)
    fine = (jnp.min(range_ref[0]) >= SUM_LOW) & (jnp.max(range_ref[1]) <= SUM_HIGH)

    @pl.when(jnp.logical_not(fine))
    def _():
        for part in parts:
            part(True)


def in_line(first):
    return lambda i: (first + i, (first + i) * UNIT, (first + i - 1) * UNIT, (first + i) * UNIT)


def edge_kernel(
    state_hbm, cond_hbm, ids_hbm, time_hbm, gain_hbm,
    cross_hbm, core_hbm, small_hbm,
    cross_ref, core_ref, small_ref, state_last, cond_last, state_first, cond_first, ids_ref, time_ref, gain_ref, sems,
):
    own = state_hbm.shape[0]
    copies = [
        pltpu.make_async_copy(source, target, sems.at[i])
        for i, (source, target) in enumerate(
            (
                (state_hbm.at[pl.ds(own - BEHIND, BEHIND)], state_last),
                (cond_hbm.at[pl.ds(own - BEHIND, BEHIND)], cond_last),
                (state_hbm.at[pl.ds(0, AHEAD)], state_first),
                (cond_hbm.at[pl.ds(0, AHEAD)], cond_first),
                (ids_hbm, ids_ref),
                (time_hbm, time_ref),
                (gain_hbm, gain_ref),
            )
        )
    ]
    for copy in copies:
        copy.start()
    even = lax.rem(lax.axis_index("seq"), 2) == 0
    for copy in copies[4:]:
        copy.wait()

    depth = core_ref.shape[1]

    def number_row(ids):
        blank = jnp.zeros((1, depth - ids.shape[1]), F32)
        return jnp.concatenate([(ids + 1).astype(F32), blank], axis=1)

    vectors = [ref[...].astype(F32).reshape(1, -1) for ref in (time_ref, gain_ref)]
    blank = jnp.zeros((SMALL - 3, depth), F32)
    small_ref[...] = jnp.concatenate([number_row(ids_ref[...]), *vectors, blank], axis=0).astype(BF16)
    leaving = [
        pltpu.make_async_copy(small_ref, small_hbm.at[pl.ds(0, SMALL)], sems.at[7]),
        pltpu.make_async_copy(cross_ref, cross_hbm, sems.at[8]),
        pltpu.make_async_copy(core_ref, core_hbm, sems.at[9]),
    ]
    leaving[0].start()
    for copy in copies[:4]:
        copy.wait()

    def fill(ref, state, cond, ids):
        rows = state.shape[0]
        ref[0:rows, :] = (state[...].astype(F32) + cond[...].astype(F32)).astype(BF16)
        if rows < BEHIND:
            ref[rows:BEHIND, :] = jnp.zeros((BEHIND - rows, depth), BF16)
        ref[BEHIND:, :] = jnp.broadcast_to(number_row(ids), (PAYLOAD - BEHIND, depth)).astype(BF16)

    def fill_both(to_next, to_previous):
        fill(to_next, state_last, cond_last, ids_ref[:, own - BEHIND :])
        fill(to_previous, state_first, cond_first, ids_ref[:, :BEHIND])

    @pl.when(even)
    def _():
        fill_both(core_ref, cross_ref)

    @pl.when(jnp.logical_not(even))
    def _():
        fill_both(cross_ref, core_ref)

    leaving[1].start()
    leaving[2].start()
    for copy in leaving:
        copy.wait()


def own_kernel(
    small_hbm, state_hbm, cond_hbm, wqkv_hbm,
    small_ref, state_ref, cond_ref, q_ref, k_ref, v_ref, seg_ref, bias_ref,
    wk_ref, wv_ref, wq_ref, normed_ref, sems,
):
    own = state_ref.shape[0]
    copies = [
        pltpu.make_async_copy(state_hbm, state_ref, sems.at[0]),
        pltpu.make_async_copy(cond_hbm, cond_ref, sems.at[1]),
        pltpu.make_async_copy(small_hbm.at[pl.ds(0, SMALL)], small_ref, sems.at[5]),
    ]
    weights = [
        pltpu.make_async_copy(wqkv_hbm.at[which], w_ref, sems.at[2 + which])
        for which, w_ref in ((1, wk_ref), (2, wv_ref), (0, wq_ref))
    ]
    for copy in copies + weights[:1]:
        copy.start()
    copies[2].wait()
    gain = small_ref[2:3, :].astype(F32)
    own_segments(small_ref, seg_ref, own)
    build_masks((3, own // UNIT + 1), seg_ref, bias_ref)
    copies[0].wait()
    copies[1].wait()
    for copy in weights[1:]:
        copy.start()

    def hidden(at):
        return state_ref[at, :].astype(F32) + cond_ref[at, :].astype(F32)

    normalize(hidden, normed_ref, gain, 0, own)
    for w_ref, copy, out_ref in zip((wk_ref, wv_ref, wq_ref), weights, (k_ref, v_ref, q_ref)):
        copy.wait()
        project(normed_ref, w_ref, 0, own, out_ref, [(own, 0)])


def rest_kernel(
    cross_ref, core_ref, small_ref, state_ref, cond_ref, q_own, k_own, v_own, seg_own, bias_own,
    wqkv_hbm, wout_hbm,
    out_ref,
    wk_ref, wv_ref, wq_ref, wout, behind_ref, ahead_ref, halo_ref, h_ref, q_edge, k_edge, v_edge,
    normed_ref, q_ref, k_ref, v_ref, att_ref, seg_ref, bias_ref, range_ref, sems, *group_refs,
):
    own = state_ref.shape[0]
    units = own // UNIT
    end = BEHIND + own
    total = end + AHEAD
    weights = [
        pltpu.make_async_copy(wqkv_hbm.at[which], w_ref, sems.at[which])
        for which, w_ref in ((1, wk_ref), (2, wv_ref), (0, wq_ref))
    ]
    wout_copy = pltpu.make_async_copy(wout_hbm, wout, sems.at[3])
    for copy in weights:
        copy.start()
    half_time = 0.5 * small_ref[1:2, :].astype(F32)
    gain = small_ref[2:3, :].astype(F32)
    even = lax.rem(lax.axis_index("seq"), 2) == 0

    bias_ref[3 : units + 1] = bias_own[3 : units + 1]

    def interior(shift):
        attend(
            units - 2,
            lambda i: (i + 3, (i + 1) * UNIT, i * UNIT, (i + 3) * UNIT),
            q_own, k_own, v_own, att_ref, bias_ref, range_ref, group_refs, shift,
        )

    def prepare_edges():
        def take(before, after):
            behind_ref[...] = before[...]
            ahead_ref[...] = after[...]

        @pl.when(even)
        def _():
            take(cross_ref, core_ref)

        @pl.when(jnp.logical_not(even))
        def _():
            take(core_ref, cross_ref)

        seg_ref[BEHIND:end, :] = seg_own[BEHIND:end, :]
        edge_segments(behind_ref, ahead_ref, seg_ref)
        for unit in (1, 2, units + 1, units + 2):
            build_mask(unit, seg_ref, bias_ref)
        for ref, rows, first in ((behind_ref, BEHIND, 0), (ahead_ref, AHEAD, BEHIND)):
            for at in range(0, rows, ROWS):
                h = ref[at : at + ROWS, :].astype(F32)
                scale = lax.rsqrt(jnp.mean(h * h, axis=-1, keepdims=True) + 1e-06)
                halo_ref[first + at : first + at + ROWS, :] = (h * scale * gain).astype(BF16)
        for ref, whole in ((k_edge, k_own), (v_edge, v_own)):
            ref[BEHIND:EDGE, :] = whole[0 : EDGE - BEHIND, :]
            ref[EDGE : EDGE + BEHIND, :] = whole[own - BEHIND : own, :]
        q_edge[UNIT : 2 * UNIT, :] = q_own[0:UNIT, :]
        q_edge[2 * UNIT : 3 * UNIT, :] = q_own[own - UNIT : own, :]
        clear_spare((k_edge, v_edge))
        both = [(BEHIND, 0), (AHEAD, EDGE + BEHIND)]
        weights[0].wait()
        wout_copy.start()
        project(halo_ref, wk_ref, 0, BEHIND + AHEAD, k_edge, both)
        weights[1].wait()
        project(halo_ref, wv_ref, 0, BEHIND + AHEAD, v_edge, both)
        weights[2].wait()
        project(halo_ref, wq_ref, UNIT, BEHIND + AHEAD, q_edge, [(UNIT, 0), (UNIT, 3 * UNIT)])

    def edge_unit(i):
        side = i // 2
        unit = i + 1 + side * (units - 2)
        return unit, i * UNIT, side * EDGE + (i - 2 * side) * UNIT, unit * UNIT

    def edges(shift):
        attend(4, edge_unit, q_edge, k_edge, v_edge, att_ref, bias_ref, range_ref, group_refs, shift)

    unshifted_first(range_ref, (interior, edges), prepare_edges)
    wout_copy.wait()
    depth = wout.shape[1]
    for at in range(0, depth, TILE):
        cols = slice(at, at + TILE)
        moved = 0.5 * jnp.dot(att_ref[UNIT:total, :], wout[:, cols], preferred_element_type=F32)
        moved = moved + half_time[:, cols]
        h_ref[UNIT:BEHIND, cols] = behind_ref[UNIT:BEHIND, cols].astype(F32) + moved[:UNIT]
        h_ref[BEHIND:end, cols] = (
            state_ref[:, cols].astype(F32) + cond_ref[:, cols].astype(F32)
        ) + moved[UNIT : UNIT + own]
        h_ref[end:total, cols] = ahead_ref[0:AHEAD, cols].astype(F32) + moved[UNIT + own :]

    normalize(lambda at: h_ref[at, :], normed_ref, gain, UNIT, total)
    project(normed_ref, wk_ref, UNIT, total, k_ref, [(total - UNIT, UNIT)])
    project(normed_ref, wv_ref, UNIT, total, v_ref, [(total - UNIT, UNIT)])
    project(normed_ref, wq_ref, BEHIND, end, q_ref, [(own, BEHIND)])

    def second(shift):
        attend(units, in_line(2), q_ref, k_ref, v_ref, att_ref, bias_ref, range_ref, group_refs, shift)

    unshifted_first(range_ref, (second,))
    for at in range(0, depth, TILE):
        cols = slice(at, at + TILE)
        moved = jnp.dot(att_ref[BEHIND:end, :], wout[:, cols], preferred_element_type=F32)
        x = h_ref[BEHIND:end, cols] - cond_ref[:, cols].astype(F32) - half_time[:, cols]
        out_ref[:, cols] = (x + 0.5 * moved).astype(BF16)


def clear_spare(refs):
    for ref in refs:
        ref[ref.shape[0] - SPARE :, :] = jnp.zeros((SPARE, ref.shape[1]), ref.dtype)


def one_step(
    final, h_ref, small_ref, behind_ref, ahead_ref, wqkv, wout,
    out_ref,
    normed_ref, q_ref, k_ref, v_ref, att_ref, seg_ref, bias_ref, range_ref, *group_refs,
):
    total = h_ref.shape[0]
    own = total - BEHIND - AHEAD
    kv_first = UNIT if final else 0
    first, last = (BEHIND, BEHIND + own) if final else (UNIT, total)
    own_segments(small_ref, seg_ref, own)
    edge_segments(behind_ref, ahead_ref, seg_ref)
    build_masks((1, total // UNIT), seg_ref, bias_ref)
    clear_spare((k_ref, v_ref))
    gain = small_ref[2:3, :].astype(F32)
    normalize(lambda at: h_ref[at, :], normed_ref, gain, kv_first, total)
    project(normed_ref, wqkv.at[1], kv_first, total, k_ref, [(total - kv_first, kv_first)])
    project(normed_ref, wqkv.at[2], kv_first, total, v_ref, [(total - kv_first, kv_first)])
    project(normed_ref, wqkv.at[0], first, last, q_ref, [(last - first, first)])

    def every(shift):
        attend(
            (last - first) // UNIT, in_line(first // UNIT),
            q_ref, k_ref, v_ref, att_ref, bias_ref, range_ref, group_refs, shift,
        )

    unshifted_first(range_ref, (every,))
    for at in range(0, wout.shape[1], TILE):
        cols = slice(at, at + TILE)
        out_ref[:, cols] = jnp.dot(
            att_ref[first:last, :], wout[:, cols], preferred_element_type=F32
        ).astype(BF16)


def shards(state, condition, time_vector, norm_gain, w_qkv, w_out, utterance_ids):
    own, depth = state.shape
    width = w_qkv.shape[2]
    total = BEHIND + own + AHEAD
    parts = lax.axis_size("mp")
    count = lax.axis_size("seq")
    ids = utterance_ids.reshape(1, own)
    vmem = pl.BlockSpec(memory_space=pltpu.VMEM)
    hbm = pl.BlockSpec(memory_space=pltpu.HBM)

    def limit(mib):
        return pltpu.CompilerParams(vmem_limit_bytes=int(mib * 2**20))

    cross, core, small = pl.pallas_call(
        edge_kernel,
        out_shape=[jax.ShapeDtypeStruct((rows, depth), BF16) for rows in (PAYLOAD, PAYLOAD, 2 * own)],
        in_specs=[hbm] * 5,
        out_specs=[hbm] * 3,
        scratch_shapes=[pltpu.VMEM((PAYLOAD, depth), BF16)] * 2
        + [pltpu.VMEM((SMALL, depth), BF16)]
        + [pltpu.VMEM((BEHIND, depth), BF16)] * 2
        + [pltpu.VMEM((AHEAD, depth), BF16)] * 2
        + [pltpu.VMEM((1, own), jnp.int32)]
        + [pltpu.VMEM((depth,), BF16)] * 2
        + [pltpu.SemaphoreType.DMA((10,))],
        compiler_params=limit(EDGE_LIMIT),
    )(state, condition, ids, time_vector, norm_gain)
    ends = [(i, i + 1) for i in range(1, count - 1, 2)]
    cross = lax.ppermute(cross, "seq", ends + [(j, i) for i, j in ends])
    ends = [(i, i + 1) for i in range(0, count - 1, 2)]
    core = lax.ppermute(core, "seq", ends + [(j, i) for i, j in ends])

    work = [((total, depth), BF16), ((total, width), BF16)]
    work += [((total + SPARE, width), BF16)] * 2
    work += [
        ((total, width), BF16),
        ((total + SPARE, 128), F32),
        ((total // UNIT, UNIT, WINDOW), F32),
        ((2, UNIT, PAIR), F32),
    ]
    groups = [((FOUR * UNIT, WINDOW), kind) for kind in (F32, BF16) for _ in range(width // (FOUR * HEAD_DIM))]
    groups = [pltpu.VMEM(*one) for one in groups]
    if parts == 1:
        kept = [((SMALL, depth), BF16)] + [(state.shape, BF16)] * 2 + [((own, width), BF16)] * 3
        kept += [((total + SPARE, 128), F32), ((total // UNIT, UNIT, WINDOW), F32)]
        kept = pl.pallas_call(
            own_kernel,
            out_shape=[jax.ShapeDtypeStruct(*one) for one in kept],
            in_specs=[hbm] * 4,
            out_specs=[vmem] * 8,
            scratch_shapes=[pltpu.VMEM((depth, width), BF16)] * 3
            + [pltpu.VMEM((own, depth), BF16), pltpu.SemaphoreType.DMA((6,))],
            compiler_params=limit(OWN_LIMIT),
            cost_estimate=pl.CostEstimate(
                flops=6 * own * depth * width, bytes_accessed=2 * 4 * depth * width, transcendentals=0
            ),
        )(small, state, condition, w_qkv)
        first = [((depth, width), BF16)] * 3 + [(w_out.shape, BF16)] + [((PAYLOAD, depth), BF16)] * 2
        first += [((BEHIND + AHEAD, depth), BF16), ((total, depth), F32)]
        first += [((4 * UNIT, width), BF16)] + [((2 * EDGE, width), BF16)] * 2
        return pl.pallas_call(
            rest_kernel,
            out_shape=jax.ShapeDtypeStruct((own, depth), BF16),
            in_specs=[vmem] * 10 + [hbm] * 2,
            out_specs=vmem,
            scratch_shapes=[pltpu.VMEM(*one) for one in first + work]
            + [pltpu.SemaphoreType.DMA((4,))]
            + groups,
            compiler_params=limit(LIMIT),
        )(cross, core, *kept, w_qkv, w_out)

    even = lax.axis_index("seq") % 2 == 0
    small = small[:SMALL]
    behind = jnp.where(even, cross, core)
    ahead = jnp.where(even, core, cross)

    def terms(h, final):
        rows = own if final else total - UNIT
        mine = pl.pallas_call(
            functools.partial(one_step, final),
            out_shape=jax.ShapeDtypeStruct((rows, depth), BF16),
            in_specs=[vmem] * 6,
            out_specs=vmem,
            scratch_shapes=[pltpu.VMEM(*one) for one in work] + groups,
            compiler_params=limit(LIMIT),
        )(h, small, behind, ahead, w_qkv, w_out)
        return lax.psum(mine, "mp").astype(F32)

    start = state.astype(F32)
    h = jnp.concatenate(
        [behind[:BEHIND].astype(F32), start + condition.astype(F32), ahead[:AHEAD].astype(F32)]
    )
    velocity = terms(h, False)
    later = jnp.pad(velocity, ((UNIT, 0), (0, 0))) * 0.5 + 0.5 * time_vector.astype(F32)
    x = start + 0.5 * velocity[UNIT : UNIT + own] + 0.5 * terms(h + later, True)
    share = depth // parts
    mine = lax.dynamic_slice_in_dim(x, lax.axis_index("mp") * share, share, 1)
    return mine.astype(BF16)


def solution(mesh):
    in_specs = (
        P("seq", None),
        P("seq", None),
        P(),
        P(),
        P(None, None, "mp"),
        P("mp", None),
        P("seq"),
    )
    out_specs = P("seq", "mp")
    return jax.shard_map(shards, mesh=mesh, in_specs=in_specs, out_specs=out_specs, check_vma=False)
```

```python
import functools
import math

import jax
import jax.numpy as jnp
from jax import lax
from jax.experimental import pallas as pl
from jax.experimental.pallas import tpu as pltpu
from jax.sharding import PartitionSpec as P

HEAD_DIM = 64
BLOCK = 24
UNIT = 2 * BLOCK
BEHIND = 4 * BLOCK
AHEAD = 2 * BLOCK
WINDOW = 128
SPARE = WINDOW - 2 * UNIT
EDGE = UNIT + WINDOW
PAIR = 2 * HEAD_DIM
MANY = 8
FOUR = 4
SUM_LOW, SUM_HIGH = 2.0**-60, 2.0**100
SMALL = 16
PAYLOAD = BEHIND + 16
TILE = 512
ROWS = 16
MANY_ROWS = 640
EDGE_LIMIT, OWN_LIMIT, LIMIT = 56, 48, 48
F32 = jnp.float32
BF16 = jnp.bfloat16
NEG = -1e30


def column_of(row):
    n = row.shape[1]
    same = lax.broadcasted_iota(jnp.int32, (n, n), 0) == lax.broadcasted_iota(jnp.int32, (n, n), 1)
    column = jnp.sum(jnp.where(same, row, 0.0), axis=1, keepdims=True)
    return jnp.broadcast_to(column, (n, 128))


def own_segments(small_ref, seg_ref, own):
    for at in range(0, own, 128):
        n = min(128, own - at)
        row = small_ref[0:1, at : at + n].astype(F32)
        seg_ref[BEHIND + at : BEHIND + at + n, :] = column_of(row)


def edge_segments(behind_ref, ahead_ref, seg_ref):
    end = seg_ref.shape[0] - SPARE
    seg_ref[0:BEHIND, :] = column_of(behind_ref[BEHIND : BEHIND + 1, 0:BEHIND].astype(F32))
    seg_ref[end - AHEAD : end, :] = column_of(ahead_ref[BEHIND : BEHIND + 1, 0:AHEAD].astype(F32))
    seg_ref[end : end + SPARE, :] = jnp.full((SPARE, 128), -1.0, F32)


def build_mask(unit, seg_ref, bias_ref):
    start = unit * UNIT
    if not isinstance(unit, int):
        start = pl.multiple_of(start, 16)
    window = seg_ref[pl.ds(start - UNIT, WINDOW), :]
    r = lax.broadcasted_iota(jnp.int32, (WINDOW, WINDOW), 0)
    c = lax.broadcasted_iota(jnp.int32, (WINDOW, WINDOW), 1)
    keys = jnp.sum(jnp.where(r == c, window, 0.0), axis=0, keepdims=True)
    queries = seg_ref[pl.ds(start, UNIT), :]
    row = lax.broadcasted_iota(jnp.int32, (UNIT, WINDOW), 0)
    col = lax.broadcasted_iota(jnp.int32, (UNIT, WINDOW), 1)
    first = jnp.where(row < BLOCK, 0, BLOCK)
    band = (col >= first) & (col < first + 4 * BLOCK)
    bias_ref[unit] = jnp.where(band & (queries == keys), 0.0, NEG)


def build_masks(units, seg_ref, bias_ref):
    for unit in range(*units):
        build_mask(unit, seg_ref, bias_ref)


def normalize(load, normed_ref, gain, first, last):
    groups = (last - first) // ROWS
    many = max(n for n in range(1, MANY_ROWS // ROWS + 1) if groups % n == 0)

    def one(i, carry):
        for j in range(many):
            start = first + (i * many + j) * ROWS
            at = pl.ds(start if isinstance(start, int) else pl.multiple_of(start, ROWS), ROWS)
            h = load(at)
            scale = lax.rsqrt(jnp.mean(h * h, axis=-1, keepdims=True) + 1e-06)
            normed_ref[at, :] = (h * scale * gain).astype(BF16)
        return carry

    if groups == many:
        one(0, 0)
    else:
        lax.fori_loop(0, groups // many, one, 0)


def project(normed_ref, w_ref, first, last, out_ref, places):
    width = w_ref.shape[1]
    tile = min(TILE, width)
    for at in range(0, width, tile):
        cols = slice(at, at + tile)
        out = jnp.dot(
            normed_ref[first:last, :], w_ref[:, cols], preferred_element_type=F32
        ).astype(BF16)
        done = 0
        for rows, place in places:
            out_ref[place : place + rows, cols] = out[done : done + rows]
            done += rows


def attend(count, place, q_ref, k_ref, v_ref, att_ref, bias_ref, range_ref, group_refs, shift=False):
    wide = FOUR * HEAD_DIM
    groups = q_ref.shape[1] // wide
    factor = HEAD_DIM**-0.5 * math.log2(math.e)

    def row(start):
        return start if isinstance(start, int) else pl.multiple_of(start, 16)

    score_refs, prob_refs = group_refs[:groups], group_refs[groups:]

    def score(i, g):
        _, q_row, kv_row, _ = place(i)
        rows, window = pl.ds(row(q_row), UNIT), pl.ds(row(kv_row), WINDOW)
        head = lax.broadcasted_iota(jnp.int32, (UNIT, wide), 1) // HEAD_DIM
        lanes = slice(g * wide, (g + 1) * wide)
        q = q_ref[rows, lanes]
        zero = jnp.zeros_like(q)
        stacked = jnp.concatenate([jnp.where(head == j, q, zero) for j in range(FOUR)], axis=0)
        score_refs[g][...] = lax.dot_general(
            stacked, k_ref[window, lanes], (((1,), (1,)), ((), ())), preferred_element_type=F32
        )

    def soften(i, g):
        bias = bias_ref[place(i)[0]]
        low, high = range_ref[0], range_ref[1]
        for j in range(FOUR):
            rows = slice(j * UNIT, (j + 1) * UNIT)
            s = score_refs[g][rows, :] * factor + bias
            if shift:
                s = s - jnp.max(s, axis=-1, keepdims=True)
            expo = jnp.exp2(s)
            total = jnp.sum(expo, axis=-1, keepdims=True)
            low, high = jnp.minimum(low, total), jnp.maximum(high, total)
            prob_refs[g][rows, :] = (expo * pl.reciprocal(total, approx=True)).astype(BF16)
        range_ref[0] = low
        range_ref[1] = high

    def mix(i, g):
        _, _, kv_row, att_row = place(i)
        rows, window = pl.ds(row(att_row), UNIT), pl.ds(row(kv_row), WINDOW)
        one = lax.broadcasted_iota(jnp.int32, (UNIT, PAIR), 1) < HEAD_DIM
        lanes = slice(g * wide, (g + 1) * wide)
        out = jnp.dot(prob_refs[g][...], v_ref[window, lanes], preferred_element_type=F32)
        for p in range(FOUR // 2):
            low, high = 2 * p * UNIT, (2 * p + 1) * UNIT
            cols = slice(p * PAIR, (p + 1) * PAIR)
            mixed = jnp.where(one, out[low : low + UNIT, cols], out[high : high + UNIT, cols])
            att_ref[rows, g * wide + p * PAIR : g * wide + (p + 1) * PAIR] = mixed.astype(BF16)

    def stages(mixed=None, softened=None, scored=None):
        for g in range(groups):
            if mixed is not None:
                mix(mixed, g)
            if softened is not None:
                soften(softened, g)
            if scored is not None:
                score(scored, g)

    if shift:

        def all_stages(i, carry):
            for g in range(groups):
                score(i, g)
                soften(i, g)
                mix(i, g)
            return carry

        lax.fori_loop(0, count, all_stages, 0)
        return

    stages(scored=0)
    stages(softened=0, scored=1)
    steady = count - 2
    many = max(n for n in range(1, MANY + 1) if steady % n == 0)

    def one(i, carry):
        for j in range(many):
            stages(i * many + j, i * many + j + 1, i * many + j + 2)
        return carry

    if steady == many:
        one(0, 0)
    else:
        lax.fori_loop(0, steady // many, one, 0)
    stages(mixed=count - 2, softened=count - 1)
    stages(mixed=count - 1)


def unshifted_first(range_ref, parts, between=None):
    range_ref[...] = jnp.ones_like(range_ref)
    for i, part in enumerate(parts):
        if i > 0:
            between()
        part(False)
    fine = (jnp.min(range_ref[0]) >= SUM_LOW) & (jnp.max(range_ref[1]) <= SUM_HIGH)

    @pl.when(jnp.logical_not(fine))
    def _():
        for part in parts:
            part(True)


def in_line(first):
    return lambda i: (first + i, (first + i) * UNIT, (first + i - 1) * UNIT, (first + i) * UNIT)


def edge_kernel(
    state_hbm, cond_hbm, ids_hbm, time_hbm, gain_hbm,
    cross_hbm, core_hbm, small_hbm,
    cross_ref, core_ref, small_ref, state_last, cond_last, state_first, cond_first, ids_ref, time_ref, gain_ref, sems,
):
    own = state_hbm.shape[0]
    copies = [
        pltpu.make_async_copy(source, target, sems.at[i])
        for i, (source, target) in enumerate(
            (
                (state_hbm.at[pl.ds(own - BEHIND, BEHIND)], state_last),
                (cond_hbm.at[pl.ds(own - BEHIND, BEHIND)], cond_last),
                (state_hbm.at[pl.ds(0, AHEAD)], state_first),
                (cond_hbm.at[pl.ds(0, AHEAD)], cond_first),
                (ids_hbm, ids_ref),
                (time_hbm, time_ref),
                (gain_hbm, gain_ref),
            )
        )
    ]
    for copy in copies:
        copy.start()
    even = lax.rem(lax.axis_index("seq"), 2) == 0
    for copy in copies[4:]:
        copy.wait()

    depth = core_ref.shape[1]

    def number_row(ids):
        blank = jnp.zeros((1, depth - ids.shape[1]), F32)
        return jnp.concatenate([(ids + 1).astype(F32), blank], axis=1)

    vectors = [ref[...].astype(F32).reshape(1, -1) for ref in (time_ref, gain_ref)]
    blank = jnp.zeros((SMALL - 3, depth), F32)
    small_ref[...] = jnp.concatenate([number_row(ids_ref[...]), *vectors, blank], axis=0).astype(BF16)
    leaving = [
        pltpu.make_async_copy(small_ref, small_hbm.at[pl.ds(0, SMALL)], sems.at[7]),
        pltpu.make_async_copy(cross_ref, cross_hbm, sems.at[8]),
        pltpu.make_async_copy(core_ref, core_hbm, sems.at[9]),
    ]
    leaving[0].start()
    for copy in copies[:4]:
        copy.wait()

    def fill(ref, state, cond, ids):
        rows = state.shape[0]
        ref[0:rows, :] = (state[...].astype(F32) + cond[...].astype(F32)).astype(BF16)
        if rows < BEHIND:
            ref[rows:BEHIND, :] = jnp.zeros((BEHIND - rows, depth), BF16)
        ref[BEHIND:, :] = jnp.broadcast_to(number_row(ids), (PAYLOAD - BEHIND, depth)).astype(BF16)

    def fill_both(to_next, to_previous):
        fill(to_next, state_last, cond_last, ids_ref[:, own - BEHIND :])
        fill(to_previous, state_first, cond_first, ids_ref[:, :BEHIND])

    @pl.when(even)
    def _():
        fill_both(core_ref, cross_ref)

    @pl.when(jnp.logical_not(even))
    def _():
        fill_both(cross_ref, core_ref)

    leaving[1].start()
    leaving[2].start()
    for copy in leaving:
        copy.wait()


def own_kernel(
    small_hbm, state_hbm, cond_hbm, wqkv_hbm,
    small_ref, state_ref, cond_ref, q_ref, k_ref, v_ref, seg_ref, bias_ref,
    wk_ref, wv_ref, wq_ref, normed_ref, sems,
):
    own = state_ref.shape[0]
    copies = [
        pltpu.make_async_copy(state_hbm, state_ref, sems.at[0]),
        pltpu.make_async_copy(cond_hbm, cond_ref, sems.at[1]),
        pltpu.make_async_copy(small_hbm.at[pl.ds(0, SMALL)], small_ref, sems.at[5]),
    ]
    weights = [
        pltpu.make_async_copy(wqkv_hbm.at[which], w_ref, sems.at[2 + which])
        for which, w_ref in ((1, wk_ref), (2, wv_ref), (0, wq_ref))
    ]
    for copy in copies + weights[:1]:
        copy.start()
    copies[2].wait()
    gain = small_ref[2:3, :].astype(F32)
    own_segments(small_ref, seg_ref, own)
    build_masks((3, own // UNIT + 1), seg_ref, bias_ref)
    copies[0].wait()
    copies[1].wait()
    for copy in weights[1:]:
        copy.start()

    def hidden(at):
        return state_ref[at, :].astype(F32) + cond_ref[at, :].astype(F32)

    normalize(hidden, normed_ref, gain, 0, own)
    for w_ref, copy, out_ref in zip((wk_ref, wv_ref, wq_ref), weights, (k_ref, v_ref, q_ref)):
        copy.wait()
        project(normed_ref, w_ref, 0, own, out_ref, [(own, 0)])


def rest_kernel(
    cross_ref, core_ref, small_ref, state_ref, cond_ref, q_own, k_own, v_own, seg_own, bias_own,
    wqkv_hbm, wout_hbm,
    out_ref,
    wk_ref, wv_ref, wq_ref, wout, behind_ref, ahead_ref, halo_ref, h_ref, q_edge, k_edge, v_edge,
    normed_ref, q_ref, k_ref, v_ref, att_ref, seg_ref, bias_ref, range_ref, sems, *group_refs,
):
    own = state_ref.shape[0]
    units = own // UNIT
    end = BEHIND + own
    total = end + AHEAD
    weights = [
        pltpu.make_async_copy(wqkv_hbm.at[which], w_ref, sems.at[which])
        for which, w_ref in ((1, wk_ref), (2, wv_ref), (0, wq_ref))
    ]
    wout_copy = pltpu.make_async_copy(wout_hbm, wout, sems.at[3])
    for copy in weights:
        copy.start()
    half_time = 0.5 * small_ref[1:2, :].astype(F32)
    gain = small_ref[2:3, :].astype(F32)
    even = lax.rem(lax.axis_index("seq"), 2) == 0

    bias_ref[3 : units + 1] = bias_own[3 : units + 1]

    def interior(shift):
        attend(
            units - 2,
            lambda i: (i + 3, (i + 1) * UNIT, i * UNIT, (i + 3) * UNIT),
            q_own, k_own, v_own, att_ref, bias_ref, range_ref, group_refs, shift,
        )

    def prepare_edges():
        def take(before, after):
            behind_ref[...] = before[...]
            ahead_ref[...] = after[...]

        @pl.when(even)
        def _():
            take(cross_ref, core_ref)

        @pl.when(jnp.logical_not(even))
        def _():
            take(core_ref, cross_ref)

        seg_ref[BEHIND:end, :] = seg_own[BEHIND:end, :]
        edge_segments(behind_ref, ahead_ref, seg_ref)
        for unit in (1, 2, units + 1, units + 2):
            build_mask(unit, seg_ref, bias_ref)
        for ref, rows, first in ((behind_ref, BEHIND, 0), (ahead_ref, AHEAD, BEHIND)):
            for at in range(0, rows, ROWS):
                h = ref[at : at + ROWS, :].astype(F32)
                scale = lax.rsqrt(jnp.mean(h * h, axis=-1, keepdims=True) + 1e-06)
                halo_ref[first + at : first + at + ROWS, :] = (h * scale * gain).astype(BF16)
        for ref, whole in ((k_edge, k_own), (v_edge, v_own)):
            ref[BEHIND:EDGE, :] = whole[0 : EDGE - BEHIND, :]
            ref[EDGE : EDGE + BEHIND, :] = whole[own - BEHIND : own, :]
        q_edge[UNIT : 2 * UNIT, :] = q_own[0:UNIT, :]
        q_edge[2 * UNIT : 3 * UNIT, :] = q_own[own - UNIT : own, :]
        clear_spare((k_edge, v_edge))
        both = [(BEHIND, 0), (AHEAD, EDGE + BEHIND)]
        weights[0].wait()
        wout_copy.start()
        project(halo_ref, wk_ref, 0, BEHIND + AHEAD, k_edge, both)
        weights[1].wait()
        project(halo_ref, wv_ref, 0, BEHIND + AHEAD, v_edge, both)
        weights[2].wait()
        project(halo_ref, wq_ref, UNIT, BEHIND + AHEAD, q_edge, [(UNIT, 0), (UNIT, 3 * UNIT)])

    def edge_unit(i):
        side = i // 2
        unit = i + 1 + side * (units - 2)
        return unit, i * UNIT, side * EDGE + (i - 2 * side) * UNIT, unit * UNIT

    def edges(shift):
        attend(4, edge_unit, q_edge, k_edge, v_edge, att_ref, bias_ref, range_ref, group_refs, shift)

    unshifted_first(range_ref, (interior, edges), prepare_edges)
    wout_copy.wait()
    depth = wout.shape[1]
    for at in range(0, depth, TILE):
        cols = slice(at, at + TILE)
        moved = 0.5 * jnp.dot(att_ref[UNIT:total, :], wout[:, cols], preferred_element_type=F32)
        moved = moved + half_time[:, cols]
        h_ref[UNIT:BEHIND, cols] = behind_ref[UNIT:BEHIND, cols].astype(F32) + moved[:UNIT]
        h_ref[BEHIND:end, cols] = (
            state_ref[:, cols].astype(F32) + cond_ref[:, cols].astype(F32)
        ) + moved[UNIT : UNIT + own]
        h_ref[end:total, cols] = ahead_ref[0:AHEAD, cols].astype(F32) + moved[UNIT + own :]

    normalize(lambda at: h_ref[at, :], normed_ref, gain, UNIT, total)
    project(normed_ref, wk_ref, UNIT, total, k_ref, [(total - UNIT, UNIT)])
    project(normed_ref, wv_ref, UNIT, total, v_ref, [(total - UNIT, UNIT)])
    project(normed_ref, wq_ref, BEHIND, end, q_ref, [(own, BEHIND)])

    def second(shift):
        attend(units, in_line(2), q_ref, k_ref, v_ref, att_ref, bias_ref, range_ref, group_refs, shift)

    unshifted_first(range_ref, (second,))
    for at in range(0, depth, TILE):
        cols = slice(at, at + TILE)
        moved = jnp.dot(att_ref[BEHIND:end, :], wout[:, cols], preferred_element_type=F32)
        x = h_ref[BEHIND:end, cols] - cond_ref[:, cols].astype(F32) - half_time[:, cols]
        out_ref[:, cols] = (x + 0.5 * moved).astype(BF16)


def clear_spare(refs):
    for ref in refs:
        ref[ref.shape[0] - SPARE :, :] = jnp.zeros((SPARE, ref.shape[1]), ref.dtype)


def one_step(
    final, h_ref, small_ref, behind_ref, ahead_ref, wqkv, wout,
    out_ref,
    normed_ref, q_ref, k_ref, v_ref, att_ref, seg_ref, bias_ref, range_ref, *group_refs,
):
    total = h_ref.shape[0]
    own = total - BEHIND - AHEAD
    kv_first = UNIT if final else 0
    first, last = (BEHIND, BEHIND + own) if final else (UNIT, total)
    own_segments(small_ref, seg_ref, own)
    edge_segments(behind_ref, ahead_ref, seg_ref)
    build_masks((1, total // UNIT), seg_ref, bias_ref)
    clear_spare((k_ref, v_ref))
    gain = small_ref[2:3, :].astype(F32)
    normalize(lambda at: h_ref[at, :], normed_ref, gain, kv_first, total)
    project(normed_ref, wqkv.at[1], kv_first, total, k_ref, [(total - kv_first, kv_first)])
    project(normed_ref, wqkv.at[2], kv_first, total, v_ref, [(total - kv_first, kv_first)])
    project(normed_ref, wqkv.at[0], first, last, q_ref, [(last - first, first)])

    def every(shift):
        attend(
            (last - first) // UNIT, in_line(first // UNIT),
            q_ref, k_ref, v_ref, att_ref, bias_ref, range_ref, group_refs, shift,
        )

    unshifted_first(range_ref, (every,))
    for at in range(0, wout.shape[1], TILE):
        cols = slice(at, at + TILE)
        out_ref[:, cols] = jnp.dot(
            att_ref[first:last, :], wout[:, cols], preferred_element_type=F32
        ).astype(BF16)


def shards(state, condition, time_vector, norm_gain, w_qkv, w_out, utterance_ids):
    own, depth = state.shape
    width = w_qkv.shape[2]
    total = BEHIND + own + AHEAD
    parts = lax.axis_size("mp")
    count = lax.axis_size("seq")
    ids = utterance_ids.reshape(1, own)
    vmem = pl.BlockSpec(memory_space=pltpu.VMEM)
    hbm = pl.BlockSpec(memory_space=pltpu.HBM)

    def limit(mib):
        return pltpu.CompilerParams(vmem_limit_bytes=int(mib * 2**20))

    cross, core, small = pl.pallas_call(
        edge_kernel,
        out_shape=[jax.ShapeDtypeStruct((rows, depth), BF16) for rows in (PAYLOAD, PAYLOAD, 2 * own)],
        in_specs=[hbm] * 5,
        out_specs=[hbm] * 3,
        scratch_shapes=[pltpu.VMEM((PAYLOAD, depth), BF16)] * 2
        + [pltpu.VMEM((SMALL, depth), BF16)]
        + [pltpu.VMEM((BEHIND, depth), BF16)] * 2
        + [pltpu.VMEM((AHEAD, depth), BF16)] * 2
        + [pltpu.VMEM((1, own), jnp.int32)]
        + [pltpu.VMEM((depth,), BF16)] * 2
        + [pltpu.SemaphoreType.DMA((10,))],
        compiler_params=limit(EDGE_LIMIT),
    )(state, condition, ids, time_vector, norm_gain)
    ends = [(i, i + 1) for i in range(1, count - 1, 2)]
    cross = lax.ppermute(cross, "seq", ends + [(j, i) for i, j in ends])
    ends = [(i, i + 1) for i in range(0, count - 1, 2)]
    core = lax.ppermute(core, "seq", ends + [(j, i) for i, j in ends])

    work = [((total, depth), BF16), ((total, width), BF16)]
    work += [((total + SPARE, width), BF16)] * 2
    work += [
        ((total, width), BF16),
        ((total + SPARE, 128), F32),
        ((total // UNIT, UNIT, WINDOW), F32),
        ((2, UNIT, PAIR), F32),
    ]
    groups = [((FOUR * UNIT, WINDOW), kind) for kind in (F32, BF16) for _ in range(width // (FOUR * HEAD_DIM))]
    groups = [pltpu.VMEM(*one) for one in groups]
    if parts == 1:
        kept = [((SMALL, depth), BF16)] + [(state.shape, BF16)] * 2 + [((own, width), BF16)] * 3
        kept += [((total + SPARE, 128), F32), ((total // UNIT, UNIT, WINDOW), F32)]
        kept = pl.pallas_call(
            own_kernel,
            out_shape=[jax.ShapeDtypeStruct(*one) for one in kept],
            in_specs=[hbm] * 4,
            out_specs=[vmem] * 8,
            scratch_shapes=[pltpu.VMEM((depth, width), BF16)] * 3
            + [pltpu.VMEM((own, depth), BF16), pltpu.SemaphoreType.DMA((6,))],
            compiler_params=limit(OWN_LIMIT),
            cost_estimate=pl.CostEstimate(
                flops=6 * own * depth * width, bytes_accessed=2 * 4 * depth * width, transcendentals=0
            ),
        )(small, state, condition, w_qkv)
        first = [((depth, width), BF16)] * 3 + [(w_out.shape, BF16)] + [((PAYLOAD, depth), BF16)] * 2
        first += [((BEHIND + AHEAD, depth), BF16), ((total, depth), F32)]
        first += [((4 * UNIT, width), BF16)] + [((2 * EDGE, width), BF16)] * 2
        return pl.pallas_call(
            rest_kernel,
            out_shape=jax.ShapeDtypeStruct((own, depth), BF16),
            in_specs=[vmem] * 10 + [hbm] * 2,
            out_specs=vmem,
            scratch_shapes=[pltpu.VMEM(*one) for one in first + work]
            + [pltpu.SemaphoreType.DMA((4,))]
            + groups,
            compiler_params=limit(LIMIT),
        )(cross, core, *kept, w_qkv, w_out)

    even = lax.axis_index("seq") % 2 == 0
    small = small[:SMALL]
    behind = jnp.where(even, cross, core)
    ahead = jnp.where(even, core, cross)

    def terms(h, final):
        rows = own if final else total - UNIT
        mine = pl.pallas_call(
            functools.partial(one_step, final),
            out_shape=jax.ShapeDtypeStruct((rows, depth), BF16),
            in_specs=[vmem] * 6,
            out_specs=vmem,
            scratch_shapes=[pltpu.VMEM(*one) for one in work] + groups,
            compiler_params=limit(LIMIT),
        )(h, small, behind, ahead, w_qkv, w_out)
        return lax.psum(mine, "mp").astype(F32)

    start = state.astype(F32)
    h = jnp.concatenate(
        [behind[:BEHIND].astype(F32), start + condition.astype(F32), ahead[:AHEAD].astype(F32)]
    )
    velocity = terms(h, False)
    later = jnp.pad(velocity, ((UNIT, 0), (0, 0))) * 0.5 + 0.5 * time_vector.astype(F32)
    x = start + 0.5 * velocity[UNIT : UNIT + own] + 0.5 * terms(h + later, True)
    share = depth // parts
    mine = lax.dynamic_slice_in_dim(x, lax.axis_index("mp") * share, share, 1)
    return mine.astype(BF16)


def solution(mesh):
    in_specs = (
        P("seq", None),
        P("seq", None),
        P(),
        P(),
        P(None, None, "mp"),
        P("mp", None),
        P("seq"),
    )
    out_specs = P("seq", "mp")
    return jax.shard_map(shards, mesh=mesh, in_specs=in_specs, out_specs=out_specs, check_vma=False)
```
